128 devices in a mesh: slab: 4 (over x_hi, core), sub: 32 (over y, x_lo, z).
Axes of the slice: x: 4 (x_hi: 2, x_lo: 2; x = x_hi * 2 + x_lo), y: 4, z: 4, core: 2. Of those that a mesh axis runs over, the one named last changes fastest.
Arguments:
- positions: float32 [3, 131072], P(None, ('slab', 'sub')), may hold values from 0 to 10
- fraction: float32 [3, 131072], P(None, ('slab', 'sub')), may hold values from 0 to 1
- grid_base: int32 [3, 131072], P(None, ('slab', 'sub')), may hold values from 0 to 255, as said below
- polarizability: float32 [131072], P(('slab', 'sub')), may hold values from 0.1 to 0.5
- perm_field: float32 [3, 131072], P(None, ('slab', 'sub')), may hold values from -6 to 6
- influence: float32 [256, 256, 256], P('slab', 'sub'), may hold values from 0.5 to 1094
- neighbour_cells: int32 [2048, 16], P(('slab', 'sub')), may hold values from 0 to 47, as said below
- neighbour_count: int32 [2048], P(('slab', 'sub')), may hold values from 1 to 16, as said below
- send_cells: int32 [128, 4, 8], P(('slab', 'sub')), may hold values from 0 to 15, as said below
Outputs:
- dipoles: float32 [3, 131072], P(None, ('slab', 'sub'))
The draws below stay inside these ranges and needn't reach their ends.
Inputs may be any that keep to these rules, and one draw needn't show every extreme that they name: `grid_base`: rows 0, 1, 2 are the first grid point along x, y, z: along x counted within the device's 256/4 points, along y within its 256/32 points, along z over all 256 points. `neighbour_cells`: entry 0 of a cell's row is the cell's own index among its device's 16 cells; the entries of a row are distinct and index the device's extended table of 48 cells. Only the first neighbour_count entries of a cell's row are live; some cell has all 16 live. send_cells[d, q] lists 8 distinct cells of device d: q = 0 go to the next device along sub, q = 1 to the previous along sub, q = 2 to the next along slab, q = 3 to the previous along slab, cyclically.
All inputs are finite; a program needn't handle non-finite values.
Results may differ from the reference program's by a relative error of at most 0.0003.
Values sent between devices are 32-bit elements; how exact they have to be, the bound alone decides.
A program may use at most 128 MiB of HBM per device.

```python
import math
import jax
import jax.numpy as jnp
from jax import lax

G = 256
CELL_ATOMS = 64
CELLS_DEV = 16
NB = 16
ITERS = 2
GHOST = 8
CELLS = 2048
ATOMS = 131072
N_SLAB = 4
N_SUB = 32


def draw_grid_base(key, part):
    limits = jnp.array([G // N_SLAB, G // N_SUB, G], jnp.int32)
    return jax.random.randint(key, (3, ATOMS), 0, limits[:, None]).astype(jnp.int32)


def draw_influence(key, part):
    frequency = jnp.arange(G, dtype=jnp.int32).astype(jnp.float32)
    cosine_term = jnp.cos(2.0 * jnp.pi * frequency / G)
    denominator = 4.0 + 2.0 * cosine_term
    modulus = 36.0 / (denominator * denominator)
    product = modulus[:, None, None] * modulus[None, :, None] * modulus[None, None, :]
    picked = jax.random.uniform(jax.random.fold_in(key, 41), (G, G, G), jnp.float32, 0.0, 1.0)
    factor = jnp.exp(jnp.log(0.5) + picked * jnp.log(3.0))
    return (factor * product).astype(jnp.float32)


def draw_neighbour_cells(key, part):
    extended = 3 * CELLS_DEV
    slots = jnp.arange(extended, dtype=jnp.int32)
    scores = jax.random.randint(jax.random.fold_in(key, 11), (CELLS, extended), 0, 1 << 20) * extended + slots[None, :]
    own_cells = (jnp.arange(CELLS, dtype=jnp.int32) % CELLS_DEV).astype(jnp.int32)
    scores = jnp.where(slots[None, :] == own_cells[:, None], 1 << 30, scores)
    ranked = jnp.argsort(scores, axis=1).astype(jnp.int32)
    return jnp.concatenate([own_cells[:, None], ranked[:, :NB - 1]], axis=1).astype(jnp.int32)


def draw_neighbour_count(key, part):
    devices = N_SLAB * N_SUB
    load_level = jax.random.randint(jax.random.fold_in(key, 21), (devices, 1), 2, NB + 1)
    counts = jax.random.randint(jax.random.fold_in(key, 22), (devices, CELLS_DEV), 1, load_level + 1)
    return counts.reshape(-1).at[0].set(NB).astype(jnp.int32)


def draw_send_cells(key, part):
    devices = N_SLAB * N_SUB
    slots = jnp.arange(CELLS_DEV, dtype=jnp.int32)
    scores = jax.random.randint(jax.random.fold_in(key, 31), (devices, 4, CELLS_DEV), 0, 1 << 20) * CELLS_DEV + slots
    ranked = jnp.argsort(scores, axis=2).astype(jnp.int32)
    return ranked[:, :, :GHOST]


def steps_of(key, extent, cuts, least, largest):
    gain, own = 1.0, jax.random.fold_in(key, 6)
    for dim, shards_of in cuts:
        draws = jnp.exp(jax.random.uniform(jax.random.fold_in(own, dim), (shards_of,), jnp.float32, least / len(cuts), largest / len(cuts)))
        gain = gain * jnp.repeat(draws, extent[dim] // shards_of).reshape([-1 if axis == dim else 1 for axis in range(len(extent))])
    return gain


def scatter_about(key, shape, width, reach, split=(), kind=jnp.bfloat16):
    values = jax.random.normal(key, shape, jnp.float32) * width
    if len(split) > 0:
        values = steps_of(key, shape, split, -0.22, 0.18) * values
    return jnp.clip(values, min=-reach, max=reach).astype(kind)


def setup_inputs(seed: int = 0) -> dict:
    key_list = jax.random.split(jax.random.key(seed), 10)
    positions = jnp.clip(10.0 * jax.random.uniform(key_list[0], (3, ATOMS), jnp.float32) ** steps_of(key_list[0], (3, ATOMS), ((1, 128),), -0.2, 0.2), 0.0, 10.0)
    fraction = jnp.clip(1.0 * jax.random.uniform(key_list[1], (3, ATOMS), jnp.float32) ** steps_of(key_list[1], (3, ATOMS), ((1, 128),), -0.2, 0.2), 0.0, 1.0)
    grid_base = draw_grid_base(jax.random.fold_in(key_list[9], 71), 0)
    polarizability = jnp.clip(jnp.exp(math.log(0.5) - 1.609438 * jax.random.uniform(key_list[3], (ATOMS,), jnp.float32) ** steps_of(key_list[3], (ATOMS,), ((0, 128),), -0.2, 0.2)), 0.1, 0.5)
    perm_field = scatter_about(key_list[4], (3, ATOMS), 1.0, 6.0, ((1, 128),), jnp.float32)
    influence = draw_influence(jax.random.fold_in(key_list[9], 71), 0)
    neighbour_cells = draw_neighbour_cells(jax.random.fold_in(key_list[9], 71), 0)
    neighbour_count = draw_neighbour_count(jax.random.fold_in(key_list[9], 71), 0)
    send_cells = draw_send_cells(jax.random.fold_in(key_list[9], 71), 0)
    return {"positions": positions, "fraction": fraction, "grid_base": grid_base, "polarizability": polarizability, "perm_field": perm_field, "influence": influence, "neighbour_cells": neighbour_cells, "neighbour_count": neighbour_count, "send_cells": send_cells}


damping = 1.0
recip_scale = 16.0

def spline_weights(fraction):
    square = fraction * fraction
    cube = square * fraction
    rest = 1.0 - fraction
    return jnp.stack([rest * rest * rest / 6.0, (3.0 * cube - 6.0 * square + 4.0) / 6.0, (-3.0 * cube + 3.0 * square + 3.0 * fraction + 1.0) / 6.0, cube / 6.0])

def signed_index(position):
    return jnp.where(position < G // 2, position, position - G).astype(jnp.float32)

def pair_field(pos_near, pos_far, mom_far, live_pairs):
    delta_x = pos_near[0][..., :, None] - pos_far[0][..., None, :]
    delta_y = pos_near[1][..., :, None] - pos_far[1][..., None, :]
    delta_z = pos_near[2][..., :, None] - pos_far[2][..., None, :]
    softened = delta_x * delta_x + delta_y * delta_y + delta_z * delta_z + damping
    inverse = 1.0 / jnp.sqrt(softened)
    inverse_cube = inverse * inverse * inverse
    inverse_fifth = inverse_cube * inverse * inverse
    projection = delta_x * mom_far[0][..., None, :] + delta_y * mom_far[1][..., None, :] + delta_z * mom_far[2][..., None, :]
    radial = jnp.where(live_pairs, 3.0 * projection * inverse_fifth, 0.0)
    plain = jnp.where(live_pairs, inverse_cube, 0.0)
    return jnp.stack([lax.optimization_barrier(jnp.sum(radial * delta_x - plain * mom_far[0][..., None, :], axis=-1)), lax.optimization_barrier(jnp.sum(radial * delta_y - plain * mom_far[1][..., None, :], axis=-1)), lax.optimization_barrier(jnp.sum(radial * delta_z - plain * mom_far[2][..., None, :], axis=-1))])

def reference(positions, fraction, grid_base, polarizability, perm_field, influence, neighbour_cells, neighbour_count, send_cells):
    devices = N_SLAB * N_SUB
    pos_blocks = positions.reshape(3, devices, CELLS_DEV, CELL_ATOMS)
    neighbour_blocks = neighbour_cells.reshape(devices, CELLS_DEV, NB)
    count_blocks = neighbour_count.reshape(devices, CELLS_DEV)
    own_cells = jnp.arange(CELLS_DEV, dtype=jnp.int32)
    atom_slot = jnp.arange(CELL_ATOMS, dtype=jnp.int32)
    same_atom = atom_slot[:, None] == atom_slot[None, :]

    def extend(blocks):
        pieces = [blocks]
        for direction, (axis_pos, amount) in enumerate(((2, 1), (2, -1), (1, 1), (1, -1))):
            picked = jnp.take_along_axis(blocks, send_cells[:, direction][None, :, :, None], axis=2)
            layout = picked.reshape(blocks.shape[0], N_SLAB, N_SUB, GHOST, CELL_ATOMS)
            pieces.append(jnp.roll(layout, amount, axis=axis_pos).reshape(blocks.shape[0], devices, GHOST, CELL_ATOMS))
        return jnp.concatenate(pieces, axis=2)
    pos_ext = extend(pos_blocks)

    def real_field(moments):
        mom_ext = extend(moments.reshape(3, devices, CELLS_DEV, CELL_ATOMS))

        def accumulate(running, column):
            chosen = lax.dynamic_index_in_dim(neighbour_blocks, column, 2, keepdims=False)
            lookup = chosen[None, :, :, None]
            pos_far = jnp.take_along_axis(pos_ext, lookup, axis=2)
            mom_far = jnp.take_along_axis(mom_ext, lookup, axis=2)
            live_cell = column < count_blocks
            itself = chosen == own_cells[None, :]
            live_pairs = live_cell[:, :, None, None] & jnp.logical_not(itself[:, :, None, None] & same_atom)
            return (running + pair_field(pos_blocks, pos_far, mom_far, live_pairs), None)
        running, unused = lax.scan(accumulate, jnp.zeros((3, devices, CELLS_DEV, CELL_ATOMS), jnp.float32), jnp.arange(NB, dtype=jnp.int32))
        return running.reshape(3, ATOMS)
    atom_device = jnp.arange(ATOMS, dtype=jnp.int32) // (CELLS_DEV * CELL_ATOMS)
    start_x = atom_device // N_SUB * (G // N_SLAB) + grid_base[0]
    start_y = atom_device % N_SUB * (G // N_SUB) + grid_base[1]
    start_z = grid_base[2]
    weights = spline_weights(fraction)
    offsets = jnp.arange(4, dtype=jnp.int32)
    shape_full = (4, 4, 4, ATOMS)
    index_x = jnp.broadcast_to((start_x[None, None, None, :] + offsets[:, None, None, None]) % G, shape_full)
    index_y = jnp.broadcast_to((start_y[None, None, None, :] + offsets[None, :, None, None]) % G, shape_full)
    index_z = jnp.broadcast_to((start_z[None, None, None, :] + offsets[None, None, :, None]) % G, shape_full)
    stencil = weights[:, 0][:, None, None, :] * weights[:, 1][None, :, None, :] * weights[:, 2][None, None, :, :]
    position = jnp.arange(G, dtype=jnp.int32)
    freq_x = signed_index(position)[:, None, None]
    freq_y = signed_index(position)[None, :, None]
    freq_z = signed_index(position)[None, None, :]
    freq_sq = freq_x * freq_x + freq_y * freq_y + freq_z * freq_z
    anchor = (position[:, None, None] == 0) & (position[None, :, None] == 0) & (position[None, None, :] == 0)
    width_sq = G / 4.0 * (G / 4.0)
    moduli = jnp.transpose(influence, (2, 0, 1))
    kernel = jnp.where(anchor, 0.0, -recip_scale * moduli * jnp.exp(-freq_sq / (2.0 * width_sq)) / jnp.where(anchor, 1.0, freq_sq))

    def recip_field(moments):
        density = jnp.zeros((3, G, G, G), jnp.float32)
        density = density.at[:, index_x, index_y, index_z].add(moments[:, None, None, None, :] * stencil[None])
        spectra = jnp.fft.fftn(density, axes=(1, 2, 3))
        dotted = freq_x * spectra[0] + freq_y * spectra[1] + freq_z * spectra[2]
        field_spec = jnp.stack([freq_x * kernel * dotted, freq_y * kernel * dotted, freq_z * kernel * dotted])
        field_grid = jnp.real(jnp.fft.ifftn(field_spec, axes=(1, 2, 3)))
        sampled = field_grid[:, index_x, index_y, index_z] * stencil[None]
        return lax.optimization_barrier(jnp.sum(sampled, axis=(1, 2, 3)))
    moments = polarizability[None, :] * perm_field
    for advance in range(ITERS):
        moments = polarizability[None, :] * (perm_field + real_field(moments) + recip_field(moments))
    return moments
```

```python
import functools
import math

import jax
import jax.numpy as jnp
import numpy as np
from jax import lax
from jax.experimental import pallas as pl
from jax.experimental.pallas import tpu as pltpu
from jax.sharding import PartitionSpec as P

G = 256
ITERS = 2

damping = 1.0
recip_scale = 16.0
high = lax.Precision.HIGH
highest = lax.Precision.HIGHEST
LANES = 128
MESH = pl.DeviceIdType.MESH


def shifted(value, axis, steps):
    count = lax.axis_size(axis)
    pairs = [(source, (source + steps) % count) for source in range(count)]
    return lax.ppermute(value, axis, pairs)


def spline_weights(fraction):
    square = fraction * fraction
    cube = square * fraction
    rest = 1.0 - fraction
    return [
        rest * rest * rest / 6.0,
        (3.0 * cube - 6.0 * square + 4.0) / 6.0,
        (-3.0 * cube + 3.0 * square + 3.0 * fraction + 1.0) / 6.0,
        cube / 6.0,
    ]


def axis_table(start, fraction, length, wrapped):
    offset = jnp.arange(length, dtype=jnp.int32)[:, None] - start[..., None, :]
    if wrapped:
        offset = offset % length
    table = 0.0
    for stencil, weight in enumerate(spline_weights(fraction)):
        table = table + jnp.where(offset == stencil, weight[..., None, :], 0.0)
    return table


def pair_kernel(cell_count, width, list_ref, count_ref, table_ref, near_ref, out_ref):
    lane = lax.broadcasted_iota(jnp.int32, (8, 2 * width), 1)
    row = lax.broadcasted_iota(jnp.int32, (8, 2 * width), 0)
    first_half = lane < width
    is_moment = row >= 3
    itself = lax.broadcasted_iota(jnp.int32, (width, 2 * width), 0) == lax.broadcasted_iota(
        jnp.int32, (width, 2 * width), 1
    )

    def one_cell(cell, _):
        base = pl.multiple_of(cell * width, width)
        near = near_ref[pl.ds(base, width), :]
        near_x = jnp.broadcast_to(near[:, 0:1], (width, 2 * width))
        near_y = jnp.broadcast_to(near[:, 1:2], (width, 2 * width))
        near_z = jnp.broadcast_to(near[:, 2:3], (width, 2 * width))
        count = count_ref[cell]

        def terms(pair, masked):
            one = table_ref[list_ref[cell, 2 * pair]]
            two = table_ref[list_ref[cell, 2 * pair + 1]]
            live = 2 * pair + 1 < count
            two = jnp.where(jnp.logical_and(is_moment, jnp.logical_not(live)), 0.0, two)
            far = jnp.where(first_half, one, two)
            dx = near_x - far[0:1]
            dy = near_y - far[1:2]
            dz = near_z - far[2:3]
            mx, my, mz = far[3:4], far[4:5], far[5:6]
            softened = dx * dx + dy * dy + dz * dz + damping
            inverse = lax.rsqrt(softened)
            square = inverse * inverse
            cube = square * inverse
            if masked:
                cube = jnp.where(itself, 0.0, cube)
            radial = (3.0 * (dx * mx + dy * my + dz * mz)) * (cube * square)
            return radial * dx - cube * mx, radial * dy - cube * my, radial * dz - cube * mz

        def step(pair, totals):
            return tuple(t + a for t, a in zip(totals, terms(pair, False)))

        totals = lax.fori_loop(1, (count + 1) // 2, step, terms(0, True))
        sums = [jnp.sum(t, axis=1, keepdims=True) for t in totals]
        column = lax.broadcasted_iota(jnp.int32, (width, 8), 1)
        out = jnp.where(column == 0, sums[0], jnp.where(column == 1, sums[1], sums[2]))
        out_ref[pl.ds(base, width), :] = out
        return 0

    lax.fori_loop(0, cell_count, one_cell, 0)


def pair_field(lists, counts, table, near):
    cell_count = counts.shape[0]
    width = near.shape[0] // cell_count
    vmem = pl.BlockSpec(memory_space=pltpu.VMEM)
    smem = pl.BlockSpec(memory_space=pltpu.SMEM)
    pairs = cell_count * lists.shape[1] * width * width // 2
    return pl.pallas_call(
        functools.partial(pair_kernel, cell_count, width),
        out_shape=jax.ShapeDtypeStruct((near.shape[0], 8), jnp.float32),
        in_specs=[smem, smem, vmem, vmem],
        out_specs=vmem,
        cost_estimate=pl.CostEstimate(flops=40 * pairs, bytes_accessed=1 << 20, transcendentals=pairs),
        name="pair_field",
    )(lists, counts, table, near)


def influence_kernel(slabs, subs, moved_ref, planes_ref, send_sem, recv_sem):
    slab, sub = lax.axis_index("slab"), lax.axis_index("sub")
    depth, rows = moved_ref.shape[0], moved_ref.shape[1]
    half = slabs * subs

    def parts(i):
        kz = depth * sub + i
        upper = kz >= half
        folded = jnp.where(upper, lax.rem(2 * half - kz, half), kz)
        slot = upper.astype(jnp.int32)
        return lax.rem(folded, slabs), folded // slabs, slot

    def both(i):
        to_slab, to_sub, slot = parts(i)
        target = planes_ref.at[slot, pl.ds(slab * rows, rows)]
        far = pltpu.make_async_remote_copy(
            src_ref=moved_ref.at[i],
            dst_ref=target,
            send_sem=send_sem.at[i],
            recv_sem=recv_sem.at[slot, slab],
            device_id=(to_slab, to_sub),
            device_id_type=MESH,
        )
        here = pltpu.make_async_copy(moved_ref.at[i], target, recv_sem.at[slot, slab])
        return far, here, jnp.logical_and(to_slab == slab, to_sub == sub)

    for i in range(depth):
        far, here, mine = both(i)

        @pl.when(mine)
        def _():
            here.start()

        @pl.when(jnp.logical_not(mine))
        def _():
            far.start()

    for slot in range(2):
        for source in range(slabs):
            pltpu.make_async_copy(
                planes_ref.at[slot, pl.ds(source * rows, rows)],
                planes_ref.at[slot, pl.ds(source * rows, rows)],
                recv_sem.at[slot, source],
            ).wait()
    for i in range(depth):
        far, here, mine = both(i)

        @pl.when(jnp.logical_not(mine))
        def _():
            far.wait_send()


def influence_planes(influence, slabs, subs):
    moved = jnp.transpose(influence, (1, 0, 2))
    depth, rows, columns = moved.shape
    anywhere = pl.BlockSpec(memory_space=pl.ANY)
    return pl.pallas_call(
        functools.partial(influence_kernel, slabs, subs),
        out_shape=jax.ShapeDtypeStruct((2, slabs * rows, columns), jnp.float32),
        in_specs=[anywhere],
        out_specs=anywhere,
        scratch_shapes=[pltpu.SemaphoreType.DMA((depth,)), pltpu.SemaphoreType.DMA((2, slabs))],
        compiler_params=pltpu.CompilerParams(has_side_effects=True),
        name="influence_planes",
    )(moved)


def shards(
    positions,
    fraction,
    grid_base,
    polarizability,
    perm_field,
    influence,
    neighbour_cells,
    neighbour_count,
    send_cells,
):
    atoms = positions.shape[1]
    cells = neighbour_cells.shape[0]
    width = atoms // cells
    ghosts = send_cells.shape[2]
    slabs = lax.axis_size("slab")
    subs = lax.axis_size("sub")
    slab = lax.axis_index("slab")
    sub = lax.axis_index("sub")
    grid_x = G // slabs
    grid_y = G // subs
    pad_x = grid_x + 8
    half = G // 2
    nyquist = float(-half)

    index = np.arange(G)
    angle = (index[:, None] * index[None, :] % G) * (2.0 * np.pi / G)
    cosine = jnp.asarray(np.cos(angle), jnp.float32)
    sine = jnp.asarray(np.sin(angle), jnp.float32)
    signed = np.where(index < half, index, index - G).astype(np.float32)
    odd = np.where(index == half, 0.0, signed).astype(np.float32)
    even = np.where(index == half, nyquist, 0.0).astype(np.float32)

    kz_all = slabs * jnp.arange(subs, dtype=jnp.int32) + slab
    kz_here = slabs * sub + slab

    planes = influence_planes(influence, slabs, subs)
    flip = jnp.asarray((index[:, None] == (-index[None, :]) % G).astype(np.float32))
    mirrored = jnp.dot(jnp.dot(flip, planes[1], precision=highest), flip, precision=highest)
    first = planes[0]
    sq = jnp.asarray(signed[:, None] ** 2 + signed[None, :] ** 2)
    kzf = kz_here.astype(jnp.float32)
    freq_sq = sq + kzf * kzf
    width_sq = G / 4.0 * (G / 4.0)
    gauss = jnp.where(
        freq_sq == 0.0,
        0.0,
        jnp.exp(-freq_sq / (2.0 * width_sq)) / jnp.where(freq_sq == 0.0, 1.0, freq_sq),
    ) * (-recip_scale / (float(G) ** 3))
    flat = kz_here == 0
    kernel_even = gauss * jnp.where(flat, first, first + mirrored)
    kernel_odd = gauss * jnp.where(flat, first, first - mirrored)
    rows_mid = jnp.transpose(influence[:, 0, :])
    rows_mid = lax.all_to_all(rows_mid, "slab", split_axis=0, concat_axis=1, tiled=True)
    rows_mid = lax.all_to_all(
        rows_mid.reshape(subs, 2, G), "sub", split_axis=0, concat_axis=0, tiled=True
    )
    mid = rows_mid[subs // 2]
    kx_mid = (2 * (subs * slab + sub) + jnp.arange(2, dtype=jnp.int32)).astype(jnp.float32)
    kx_mid = jnp.where(kx_mid < half, kx_mid, kx_mid - G)
    mid_sq = (kx_mid * kx_mid)[None, :] + jnp.asarray(signed[:, None] ** 2) + float(half * half)
    kernel_mid = (
        jnp.transpose(mid) * jnp.exp(-mid_sq / (2.0 * width_sq)) / mid_sq * (-recip_scale / (float(G) ** 3))
    )

    moments = polarizability[None, :] * perm_field
    sent_lists = jnp.pad(
        send_cells.reshape(1, 4 * ghosts).astype(jnp.float32), ((0, 0), (0, atoms - 4 * ghosts))
    )
    packet = jnp.concatenate(
        [moments, positions, fraction, grid_base.astype(jnp.float32), sent_lists], axis=0
    )

    def blocks(packet):
        own = lax.all_gather(packet, "slab", axis=0)
        before = shifted(own, "sub", 1)
        after = shifted(packet, "sub", -1)
        near = jnp.stack(
            [
                packet,
                lax.dynamic_index_in_dim(before, slab, 0, keepdims=False),
                after,
                lax.dynamic_index_in_dim(own, lax.rem(slab + slabs - 1, slabs), 0, keepdims=False),
                lax.dynamic_index_in_dim(own, lax.rem(slab + 1, slabs), 0, keepdims=False),
            ]
        )
        return jnp.stack([own, before]), near

    both, near = blocks(packet)
    frac = both[:, :, 6:9]
    base = both[:, :, 9:12].astype(jnp.int32)
    table_x = axis_table(base[:, :, 0], frac[:, :, 0], pad_x, False)
    table_y = axis_table(base[:, :, 1], frac[:, :, 1], grid_y + 3, False)
    depth = axis_table(base[:, :, 2], frac[:, :, 2], G, True)
    plane_own = (table_y[0, :, :grid_y, None, :] * table_x[0, :, None, :, :]).reshape(
        slabs, grid_y * pad_x, atoms
    )
    plane_before = (table_y[1, :, grid_y:, None, :] * table_x[1, :, None, :, :]).reshape(
        slabs, 3 * pad_x, atoms
    )
    pick = (kz_all[:, None] == jnp.arange(G)[None, :]).astype(jnp.float32)
    cos_z = jnp.dot(pick, cosine, precision=highest)
    sin_z = jnp.dot(pick, sine, precision=highest)
    alternate = jnp.asarray(np.where(index % 2 == 0, 1.0, -1.0).astype(np.float32))[None]
    phase = jnp.concatenate([cos_z, -sin_z, alternate], axis=0)
    zhat = jnp.einsum("rz,pbza->pbra", phase, depth, precision=high)
    ranks = 2 * subs + 1

    lists = jnp.where(neighbour_cells < cells, neighbour_cells, 0)
    for q in range(4):
        for slot in range(ghosts):
            entry = cells + q * ghosts + slot
            cell = near[1 + q, 12, q * ghosts + slot].astype(jnp.int32) + cells * (1 + q)
            lists = lists + jnp.where(neighbour_cells == entry, cell, 0)
    near_atoms = jnp.pad(jnp.transpose(positions), ((0, 0), (0, 5)))

    def far_table(near_moments):
        rows = jnp.concatenate([near[:, 3:6], near_moments], axis=1)
        rows = jnp.transpose(rows.reshape(5, 6, cells, width), (0, 2, 1, 3)).reshape(5 * cells, 6, width)
        rows = jnp.pad(rows, ((0, 0), (0, 2), (0, 0)))
        return jnp.concatenate([rows, rows], axis=2)

    forward = jnp.concatenate([cosine, sine], axis=1)
    upright = jnp.concatenate([cosine, sine], axis=0)
    odd_j, even_j, signed_j = jnp.asarray(odd), jnp.asarray(even), jnp.asarray(signed)
    at_half = jnp.asarray((index == half).astype(np.float32))
    kz_f = kz_all.astype(jnp.float32)[:, None, None]
    group = 2 * subs
    cos_group = lax.dynamic_slice_in_dim(cosine, slab * group, group, 0)
    sin_group = lax.dynamic_slice_in_dim(sine, slab * group, group, 0)
    signed_group = lax.dynamic_slice_in_dim(signed_j, slab * group, group, 0)

    def reciprocal(block_moments):
        values = (block_moments[:, :, :, None, :] * zhat[:, :, None, :, :]).reshape(
            2, slabs, 3 * ranks, atoms
        )
        spread = jnp.einsum("bga,bra->bgr", plane_own, values[0], precision=high)
        extra = jnp.einsum("bga,bra->bgr", plane_before, values[1], precision=high)
        spread = spread.reshape(slabs, grid_y, pad_x, 3 * ranks)
        extra = extra.reshape(slabs, 3, pad_x, 3 * ranks)
        spread = jnp.concatenate([spread[:, :3] + extra, spread[:, 3:]], axis=1)
        spill = jnp.roll(spread[:, :, grid_x:], 1, axis=0)
        spread = jnp.concatenate(
            [spread[:, :, :8] + spill, spread[:, :, 8:grid_x]], axis=2
        )
        turned = jnp.einsum(
            "byxr,bxk->ryk", spread, forward.reshape(slabs, grid_x, 2 * G), precision=high
        ).reshape(3, ranks, grid_y, 2, G)
        real_c, real_s = turned[:, :subs, :, 0], turned[:, :subs, :, 1]
        imag_c, imag_s = turned[:, subs : 2 * subs, :, 0], turned[:, subs : 2 * subs, :, 1]
        spec_re = real_c + imag_s
        spec_im = imag_c - real_s
        a_re = odd_j * spec_re[0] + kz_f * spec_re[2]
        a_im = odd_j * spec_im[0] + kz_f * spec_im[2]
        ae = nyquist * jnp.stack([spec_re[0, :, :, half], spec_im[0, :, :, half]], axis=-1)
        mid_re = lax.dynamic_slice_in_dim(turned[:, -1, :, 0], slab * group, group, 2)
        mid_im = -lax.dynamic_slice_in_dim(turned[:, -1, :, 1], slab * group, group, 2)
        mid_ab = jnp.stack(
            [
                signed_group * mid_re[0] + nyquist * mid_re[2],
                signed_group * mid_im[0] + nyquist * mid_im[2],
                mid_re[1],
                mid_im[1],
            ]
        )
        mid_ab = jnp.transpose(mid_ab.reshape(4, grid_y, subs, 2), (2, 1, 0, 3)).reshape(
            subs, grid_y, 8
        )
        payload = jnp.concatenate(
            [
                a_re,
                a_im,
                spec_re[1],
                spec_im[1],
                ae,
                mid_ab,
                jnp.zeros((subs, grid_y, LANES - 10), jnp.float32),
            ],
            axis=2,
        )
        got = lax.all_to_all(payload, "sub", split_axis=0, concat_axis=0, tiled=True)
        got = got.reshape(G, 4 * G + LANES)

        y = jnp.dot(upright, got, precision=high)
        yc, ys = y[:G], y[G:]

        def pick2(part, start, count):
            return part[:, start : start + count]

        def forward_y(re_start, im_start, count):
            return (
                pick2(yc, re_start, count) + pick2(ys, im_start, count),
                pick2(yc, im_start, count) - pick2(ys, re_start, count),
            )

        ar, ai = forward_y(0, G, G)
        br, bi = forward_y(2 * G, 3 * G, G)
        er, ei = forward_y(4 * G, 4 * G + 1, 1)
        mar, mai = forward_y(4 * G + 2, 4 * G + 4, 2)
        mbr, mbi = forward_y(4 * G + 6, 4 * G + 8, 2)
        odd_y, even_y, full_y = odd_j[:, None], even_j[:, None], signed_j[:, None]

        def applied(a, b, e):
            level = a + odd_y * b
            edge = even_y * b + at_half[None, :] * e
            phi = kernel_even * level + kernel_odd * edge
            phi_edge = kernel_odd * level + kernel_even * edge
            return phi, odd_y * phi + even_y * phi_edge, phi_edge[:, half : half + 1]

        phr, oyr, per = applied(ar, br, er)
        phi_, oyi, pei = applied(ai, bi, ei)
        mpr = kernel_mid * (mar + full_y * mbr)
        mpi = kernel_mid * (mai + full_y * mbi)
        spec = jnp.concatenate(
            [
                phr,
                phi_,
                oyr,
                oyi,
                per,
                pei,
                mpr,
                mpi,
                full_y * mpr,
                full_y * mpi,
                jnp.zeros((G, LANES - 10), jnp.float32),
            ],
            axis=1,
        )
        y = jnp.dot(upright, spec, precision=high)
        yc, ys = y[:G], y[G:]

        def backward_y(re_start, im_start, count):
            return [
                pick2(yc, re_start, count) - pick2(ys, im_start, count),
                pick2(yc, im_start, count) + pick2(ys, re_start, count),
            ]

        payload = jnp.concatenate(
            backward_y(0, G, G)
            + backward_y(2 * G, 3 * G, G)
            + backward_y(4 * G, 4 * G + 1, 1)
            + backward_y(4 * G + 2, 4 * G + 4, 2)
            + backward_y(4 * G + 6, 4 * G + 8, 2)
            + [jnp.zeros((G, LANES - 10), jnp.float32)],
            axis=1,
        ).reshape(subs, grid_y, 4 * G + LANES)
        got = lax.all_to_all(payload, "sub", split_axis=0, concat_axis=0, tiled=True)

        ph_r, ph_i = got[:, :, :G], got[:, :, G : 2 * G]
        pe_r, pe_i = got[:, :, 4 * G : 4 * G + 1], got[:, :, 4 * G + 1 : 4 * G + 2]
        ex_r = odd_j * ph_r + even_j * pe_r
        ex_i = odd_j * ph_i + even_j * pe_i
        stacked_r = jnp.stack([ex_r, got[:, :, 2 * G : 3 * G], kz_f * ph_r])
        stacked_i = jnp.stack([ex_i, got[:, :, 3 * G : 4 * G], kz_f * ph_i])
        parts = jnp.einsum(
            "icjyk,kn->cyijn", jnp.stack([stacked_r, stacked_i]), forward, precision=high
        )
        field_r = parts[:, :, 0, :, :G] - parts[:, :, 1, :, G:]
        field_i = parts[:, :, 0, :, G:] + parts[:, :, 1, :, :G]
        mids = jnp.transpose(
            got[:, :, 4 * G + 2 : 4 * G + 10].reshape(subs, grid_y, 4, 2), (2, 1, 0, 3)
        ).reshape(4, grid_y, group)
        mid_r = jnp.stack([signed_group * mids[0], mids[2], nyquist * mids[0]])
        mid_i = jnp.stack([signed_group * mids[1], mids[3], nyquist * mids[1]])
        field_m = jnp.dot(mid_r, cos_group, precision=high) - jnp.dot(mid_i, sin_group, precision=high)
        field = jnp.concatenate([field_r, field_i, field_m[:, :, None, :]], axis=2)
        field = jnp.transpose(field, (1, 3, 0, 2)).reshape(grid_y, slabs, grid_x, 3 * ranks)
        wide = jnp.concatenate([field, jnp.roll(field[:, :, :8], -1, axis=1)], axis=2)
        wide = jnp.transpose(wide, (1, 0, 2, 3))
        mixed_own = jnp.einsum(
            "bga,bgr->bra",
            plane_own,
            wide.reshape(slabs, grid_y * pad_x, 3 * ranks),
            precision=high,
        )
        mixed_before = jnp.einsum(
            "bga,bgr->bra",
            plane_before,
            wide[:, :3].reshape(slabs, 3 * pad_x, 3 * ranks),
            precision=high,
        )
        mixed = jnp.stack([mixed_own, mixed_before]).reshape(2, slabs, 3, ranks, atoms)
        return jnp.sum(mixed * zhat[:, :, None], axis=3)

    block_moments = both[:, :, :3]
    near_moments = near[:, :3]
    for advance in range(ITERS):
        pair = pair_field(lists, neighbour_count, far_table(near_moments), near_atoms)
        share = reciprocal(block_moments)
        share = jnp.transpose(share, (1, 0, 2, 3)).reshape(slabs, 6, atoms)
        share = lax.psum_scatter(share, "slab", scatter_dimension=0)
        field = share[:3] + shifted(share[3:], "sub", -1)
        moments = polarizability[None, :] * (perm_field + jnp.transpose(pair[:, :3]) + field)
        if advance + 1 < ITERS:
            block_moments, near_moments = blocks(moments)
    return moments


def solution(mesh):
    in_specs = (
        P(None, ("slab", "sub")),
        P(None, ("slab", "sub")),
        P(None, ("slab", "sub")),
        P(("slab", "sub")),
        P(None, ("slab", "sub")),
        P("slab", "sub", None),
        P(("slab", "sub"), None),
        P(("slab", "sub")),
        P(("slab", "sub"), None, None),
    )
    out_specs = P(None, ("slab", "sub"))
    return jax.shard_map(shards, mesh=mesh, in_specs=in_specs, out_specs=out_specs, check_vma=False)
```

```python
import functools
import math

import jax
import jax.numpy as jnp
import numpy as np
from jax import lax
from jax.experimental import pallas as pl
from jax.experimental.pallas import tpu as pltpu
from jax.sharding import PartitionSpec as P

G = 256
ITERS = 2

damping = 1.0
recip_scale = 16.0
highest = lax.Precision.HIGHEST
LANES = 128
TILES = 4 * G // LANES + 1
MESH = pl.DeviceIdType.MESH


def spline_weights(fraction):
    square = fraction * fraction
    cube = square * fraction
    rest = 1.0 - fraction
    return [
        rest * rest * rest / 6.0,
        (3.0 * cube - 6.0 * square + 4.0) / 6.0,
        (-3.0 * cube + 3.0 * square + 3.0 * fraction + 1.0) / 6.0,
        cube / 6.0,
    ]


def pair_kernel(cell_count, width, list_ref, count_ref, ghost_ref, table_ref, near_ref, out_ref):
    lane = lax.broadcasted_iota(jnp.int32, (8, 2 * width), 1)
    row = lax.broadcasted_iota(jnp.int32, (8, 2 * width), 0)
    first_half = lane < width
    is_moment = row >= 3
    itself = lax.broadcasted_iota(jnp.int32, (width, 2 * width), 0) == lax.broadcasted_iota(
        jnp.int32, (width, 2 * width), 1
    )

    ghosts = ghost_ref.shape[1]

    def place(entry):
        ghost = jnp.maximum(entry - cell_count, 0)
        source = lax.div(ghost, ghosts)
        there = cell_count * (1 + source) + ghost_ref[source, lax.rem(ghost, ghosts)]
        return jnp.where(entry < cell_count, entry, there)

    def one_cell(cell, _):
        base = pl.multiple_of(cell * width, width)
        near = near_ref[pl.ds(base, width), :]
        near_x = jnp.broadcast_to(near[:, 0:1], (width, 2 * width))
        near_y = jnp.broadcast_to(near[:, 1:2], (width, 2 * width))
        near_z = jnp.broadcast_to(near[:, 2:3], (width, 2 * width))
        count = count_ref[cell]

        def terms(pair, masked):
            one = table_ref[place(list_ref[cell, 2 * pair])]
            two = table_ref[place(list_ref[cell, 2 * pair + 1])]
            live = 2 * pair + 1 < count
            two = jnp.where(jnp.logical_and(is_moment, jnp.logical_not(live)), 0.0, two)
            far = jnp.where(first_half, one, two)
            dx = near_x - far[0:1]
            dy = near_y - far[1:2]
            dz = near_z - far[2:3]
            mx, my, mz = far[3:4], far[4:5], far[5:6]
            softened = dx * dx + dy * dy + dz * dz + damping
            inverse = lax.rsqrt(softened)
            square = inverse * inverse
            cube = square * inverse
            if masked:
                cube = jnp.where(itself, 0.0, cube)
            radial = (3.0 * (dx * mx + dy * my + dz * mz)) * (cube * square)
            return radial * dx - cube * mx, radial * dy - cube * my, radial * dz - cube * mz

        def step(pair, totals):
            return tuple(t + a for t, a in zip(totals, terms(pair, False)))

        totals = lax.fori_loop(1, (count + 1) // 2, step, terms(0, True))
        sums = [jnp.sum(t, axis=1, keepdims=True) for t in totals]
        column = lax.broadcasted_iota(jnp.int32, (width, 8), 1)
        out = jnp.where(column == 0, sums[0], jnp.where(column == 1, sums[1], sums[2]))
        out_ref[pl.ds(base, width), :] = out
        return 0

    lax.fori_loop(0, cell_count, one_cell, 0)


def pair_field(lists, counts, ghosts, table, near):
    cell_count = counts.shape[0]
    width = near.shape[0] // cell_count
    vmem = pl.BlockSpec(memory_space=pltpu.VMEM)
    smem = pl.BlockSpec(memory_space=pltpu.SMEM)
    pairs = cell_count * lists.shape[1] * width * width // 2
    return pl.pallas_call(
        functools.partial(pair_kernel, cell_count, width),
        out_shape=jax.ShapeDtypeStruct((near.shape[0], 8), jnp.float32),
        in_specs=[smem, smem, smem, vmem, vmem],
        out_specs=vmem,
        cost_estimate=pl.CostEstimate(flops=40 * pairs, bytes_accessed=1 << 20, transcendentals=pairs),
        name="pair_field",
    )(lists, counts, ghosts, table, near)


def split(x):
    top = x.astype(jnp.bfloat16)
    return top, (x - top.astype(jnp.float32)).astype(jnp.bfloat16)


def dot3(a, b, turned=False):
    dims = (((1,), (1 if turned else 0,)), ((), ()))

    def one(x, y):
        return lax.dot_general(x, y, dims, preferred_element_type=jnp.float32)

    return one(a[0], b[0]) + (one(a[1], b[0]) + one(a[0], b[1]))


def parts_of(table):
    table = np.asarray(table, np.float32)
    top = table.astype(jnp.bfloat16)
    low = (table - top.astype(np.float32)).astype(jnp.bfloat16)
    return jnp.asarray(top), jnp.asarray(low)


def lanes_of(shape):
    return lax.broadcasted_iota(jnp.int32, shape, len(shape) - 1)


def rows_of(shape):
    return lax.broadcasted_iota(jnp.int32, shape, len(shape) - 2)


def tables_of(packet_ref, block, phase, tx_ref, ty_ref, zh_ref):
    packet = packet_ref[block]

    def table(axis, length, wrapped):
        start = packet[9 + axis : 10 + axis].astype(jnp.int32)
        offset = rows_of((length, packet.shape[1])) - start
        if wrapped:
            offset = jnp.where(offset < 0, offset + length, offset)
        total = jnp.zeros(offset.shape, jnp.float32)
        for stencil, weight in enumerate(spline_weights(packet[6 + axis : 7 + axis])):
            total = jnp.where(offset == stencil, weight, total)
        return total

    tx_ref[block] = table(0, tx_ref.shape[1], False)
    ty_ref[block] = table(1, ty_ref.shape[1], False)
    zh_ref[block] = dot3(phase, split(table(2, G, True)))


def frequency_rows(kind):
    k = lanes_of((1, G))
    signed = jnp.where(k < G // 2, k, k - G).astype(jnp.float32)
    if kind == "odd":
        return jnp.where(k == G // 2, 0.0, signed)
    if kind == "even":
        return jnp.where(k == G // 2, signed, 0.0)
    return signed


def frequency_columns(kind):
    k = lax.broadcasted_iota(jnp.int32, (G, 1), 0)
    signed = jnp.where(k < G // 2, k, k - G).astype(jnp.float32)
    if kind == "odd":
        return jnp.where(k == G // 2, 0.0, signed)
    if kind == "even":
        return jnp.where(k == G // 2, signed, 0.0)
    return signed


def spread_kernel(
    slabs, subs, slab_ref, mom_ref, tx_ref, ty_ref, zh_ref, wt_ref, wl_ref, sel_ref, out_ref, grid_ref, mid_ref
):
    slab = slab_ref[0]
    grid_y = G // subs
    grid_x = G // slabs
    pad_x = grid_x + 8
    half = G // 2
    grid_ref[...] = jnp.zeros_like(grid_ref)

    def one(block, _):
        for part in range(2):
            mu = mom_ref[part * slabs + block]
            zh = zh_ref[part * slabs + block]
            tx = tx_ref[part * slabs + block][:pad_x]
            ty = ty_ref[part * slabs + block]
            values = jnp.concatenate(
                [zh[: 2 * subs] * mu[c : c + 1] for c in range(3)] + [mu[:8] * zh[2 * subs : 2 * subs + 1]],
                axis=0,
            )
            first, count = (0, grid_y) if part == 0 else (grid_y, 3)
            plane = jnp.concatenate([tx * ty[first + y : first + y + 1] for y in range(count)], axis=0)
            got = dot3(split(plane), split(values), True)
            columns = values.shape[0]
            for y in range(count):
                where = pl.ds(pl.multiple_of(block * grid_x, grid_x), pad_x)
                grid_ref[y, where, :columns] += got[y * pad_x : (y + 1) * pad_x]
        return 0

    lax.fori_loop(0, slabs, one, 0)
    rows = []
    for y in range(grid_y):
        grid_ref[y, :8] += grid_ref[y, G : G + 8]
        turned = grid_ref[y, :G].T
        for c in range(3):
            base = 2 * subs * c
            rows.append(
                jnp.concatenate([turned[base : base + subs], turned[base + subs : base + 2 * subs]], axis=1)
            )
        mids = turned[6 * subs : 6 * subs + 8]
        rows.append(jnp.concatenate([mids, jnp.zeros_like(mids)], axis=1))
    spec = dot3(split(jnp.concatenate(rows, axis=0)), (wt_ref[...], wl_ref[...]))
    odd, signed = frequency_rows("odd"), frequency_rows("signed")
    kz = (slabs * lax.broadcasted_iota(jnp.int32, (subs, 1), 0) + slab).astype(jnp.float32)
    lane = lanes_of((subs, LANES))
    per_y = 3 * subs + 8
    for y in range(grid_y):
        at = spec[y * per_y : (y + 1) * per_y]
        re = [at[c * subs : (c + 1) * subs, :G] for c in range(3)]
        im = [at[c * subs : (c + 1) * subs, G:] for c in range(3)]
        edge = jnp.where(
            lane == 0,
            -float(half) * re[0][:, half : half + 1],
            jnp.where(lane == 1, -float(half) * im[0][:, half : half + 1], 0.0),
        )
        full = [odd * re[0] + kz * re[2], odd * im[0] + kz * im[2], re[1], im[1]]
        tiles = [v[:, t * LANES : (t + 1) * LANES] for v in full for t in range(G // LANES)]
        for t, value in enumerate([*tiles, edge]):
            out_ref[pl.ds(t * grid_y + y, subs, stride=TILES * grid_y), :] = value
        mid = at[3 * subs :]
        for part, shift in ((0, 0), (1, G)):
            mx, my, mz = (mid[c : c + 1, shift : shift + G] for c in range(3))
            mid_ref[part, y : y + 1] = signed * mx - float(half) * mz
            mid_ref[2 + part, y : y + 1] = my
    window = pl.ds(pl.multiple_of(slab // 2 * LANES, LANES), LANES)
    pair = (lanes_of((grid_y, LANES)) - lax.rem(slab, 2) * (2 * subs)) >> 1
    columns = []
    for q in range(4):
        value = mid_ref[q, :, window]
        columns.append(jnp.concatenate([jnp.where(pair == j, value, 0.0) for j in range(subs)], axis=0))
    top, low = split(jnp.concatenate(columns, axis=1))
    sel = sel_ref[...]
    more = jnp.dot(top, sel, preferred_element_type=jnp.float32) + jnp.dot(
        low, sel, preferred_element_type=jnp.float32
    )
    for j in range(subs):
        where = pl.ds((j * TILES + TILES - 1) * grid_y, grid_y)
        out_ref[where, :] += more[j * grid_y : (j + 1) * grid_y]


def from_tiles(ref):
    blocks, rows, lanes = ref.shape
    high = rows // TILES
    return jnp.concatenate(
        [ref[:, t * high : (t + 1) * high, :].reshape(blocks * high, lanes) for t in range(TILES)], axis=1
    )


def swapped(x):
    last = x[:, 4 * G :]
    lane = lanes_of(last.shape)
    back = pltpu.roll(last, LANES - 1, 1)
    on = pltpu.roll(last, 1, 1)
    back2 = pltpu.roll(last, LANES - 2, 1)
    on2 = pltpu.roll(last, 2, 1)
    upper = ((lane - 2) & 2) == 0
    last = jnp.where(lane == 0, back, jnp.where(lane == 1, -on, jnp.where(upper, back2, -on2)))
    return jnp.concatenate(
        [x[:, G : 2 * G], -x[:, :G], x[:, 3 * G : 4 * G], -x[:, 2 * G : 3 * G], last], axis=1
    )


def middle_kernel(got_ref, even_ref, odd_ref, mid_ref, ft_ref, fl_ref, bt_ref, bl_ref, out_ref):
    half = G // 2

    def both(x):
        return split(jnp.concatenate([x, swapped(x)], axis=0))

    y = dot3((ft_ref[...], fl_ref[...]), both(from_tiles(got_ref)))
    last = y[:, 4 * G :]
    lane = lanes_of(last.shape)
    at_half = (lanes_of((1, G)) == half).astype(jnp.float32)
    odd_y, even_y, full_y = (frequency_columns(k) for k in ("odd", "even", "signed"))
    kernel_even, kernel_odd = even_ref[...], odd_ref[...]
    blocks, columns = [None] * 4, []
    for part in range(2):
        a = y[:, part * G : (part + 1) * G]
        b = y[:, (2 + part) * G : (3 + part) * G]
        level = a + odd_y * b
        edge = even_y * b + at_half * last[:, part : part + 1]
        phi = kernel_even * level + kernel_odd * edge
        phi_edge = kernel_odd * level + kernel_even * edge
        blocks[part] = phi
        blocks[2 + part] = odd_y * phi + even_y * phi_edge
        columns.append(phi_edge[:, half : half + 1])
    mid = mid_ref[...] * (last + full_y * pltpu.roll(last, LANES - 4, 1))
    mid = mid + full_y * pltpu.roll(mid, 4, 1)
    last = jnp.where(lane == 0, columns[0], jnp.where(lane == 1, columns[1], mid))
    back = dot3((bt_ref[...], bl_ref[...]), both(jnp.concatenate(blocks + [last], axis=1)))
    count, rows, lanes = out_ref.shape
    high = rows // TILES
    for t in range(TILES):
        out_ref[:, t * high : (t + 1) * high, :] = back[:, t * lanes : (t + 1) * lanes].reshape(
            count, high, lanes
        )


def sample_kernel(
    slabs,
    subs,
    slab_ref,
    got_ref,
    tx_ref,
    ty_ref,
    zh_ref,
    wt_ref,
    wl_ref,
    mt_ref,
    ml_ref,
    sel_ref,
    out_ref,
    field_ref,
    top_ref,
    low_ref,
):
    slab = slab_ref[0]
    grid_y = G // subs
    half = G // 2
    got = from_tiles(got_ref)
    last = got[:, 4 * G :]
    odd, even = frequency_rows("odd"), frequency_rows("even")
    kz = (slabs * (lax.broadcasted_iota(jnp.int32, (G, 1), 0) // grid_y) + slab).astype(jnp.float32)
    phi = [got[:, :G], got[:, G : 2 * G]]
    along_x = [odd * phi[part] + even * last[:, part : part + 1] for part in range(2)]
    lhs = jnp.concatenate(
        [
            jnp.concatenate(along_x, axis=1),
            got[:, 2 * G : 4 * G],
            jnp.concatenate([kz * phi[0], kz * phi[1]], axis=1),
        ],
        axis=0,
    )
    field = dot3(split(lhs), (wt_ref[...], wl_ref[...]))
    for t in range(2 * G // LANES):
        field_ref[pl.ds(t * 3 * G, 3 * G), :] = field[:, t * LANES : (t + 1) * LANES]
    sel = sel_ref[...]
    top, low = split(last)
    expanded = jnp.dot(top, sel, preferred_element_type=jnp.float32) + jnp.dot(
        low, sel, preferred_element_type=jnp.float32
    )
    pair = ((lanes_of((grid_y, 4 * LANES)) & (LANES - 1)) - lax.rem(slab, 2) * (2 * subs)) >> 1
    mids = jnp.zeros((grid_y, 4 * LANES), jnp.float32)
    for j in range(subs):
        mids = mids + jnp.where(pair == j, expanded[j * grid_y : (j + 1) * grid_y], 0.0)
    k = slab // 2 * LANES + (lanes_of((1, 2 * LANES)) & (LANES - 1))
    signed = jnp.where(k < half, k, k - G).astype(jnp.float32)
    mid_phi = mids[:, : 2 * LANES]
    mid_lhs = jnp.concatenate([signed * mid_phi, mids[:, 2 * LANES :], -float(half) * mid_phi], axis=0)
    mid_field = dot3(split(mid_lhs), (mt_ref[...], ml_ref[...]))
    row = rows_of((8, G))
    for y in range(grid_y):
        rows = []
        for c in range(3):
            for part in range(2):
                tiles = [
                    field_ref[pl.ds((part * G // LANES + t) * 3 * G + c * G + y, subs, stride=grid_y), :]
                    for t in range(G // LANES)
                ]
                rows.append(jnp.concatenate(tiles, axis=1))
        mid = jnp.zeros((8, G), jnp.float32)
        for c in range(3):
            mid = jnp.where(row == c, mid_field[c * grid_y + y : c * grid_y + y + 1], mid)
        here = jnp.concatenate(rows + [mid, jnp.zeros((8, G), jnp.float32)], axis=0)
        for turn in range(2):
            value = here if turn == 0 else pltpu.roll(here, G - G // slabs, 1)
            top_ref[turn, y], low_ref[turn, y] = split(value)

    def one(block, _):
        turn = lax.rem(block, 2)
        window = pl.ds(pl.multiple_of(block // 2 * LANES, LANES), LANES)
        for part in range(2):
            zh = zh_ref[part * slabs + block]
            tx = tx_ref[part * slabs + block]
            ty = ty_ref[part * slabs + block]
            first, count = (0, grid_y) if part == 0 else (grid_y, 3)
            a = tuple(
                jnp.concatenate([ref[turn, y, :, window] for y in range(count)], axis=1)
                for ref in (top_ref, low_ref)
            )
            tops, lows = [], []
            blank = jnp.zeros((LANES - tx.shape[0], tx.shape[1]), jnp.bfloat16)
            for y in range(count):
                top, low = split(tx * ty[first + y : first + y + 1])
                tops += [top, blank]
                lows += [low, blank]
            b = (jnp.concatenate(tops, axis=0), jnp.concatenate(lows, axis=0))
            mixed = dot3(a, b)
            fields = []
            for c in range(3):
                base = 2 * subs * c
                field = jnp.sum(mixed[base : base + 2 * subs] * zh[: 2 * subs], axis=0, keepdims=True)
                at = 6 * subs + c
                fields.append(field + mixed[at : at + 1] * zh[2 * subs : 2 * subs + 1])
            r = rows_of((8, tx.shape[1]))
            out_ref[part * slabs + block] = jnp.where(
                r == 0, fields[0], jnp.where(r == 1, fields[1], jnp.where(r == 2, fields[2], 0.0))
            )
        return 0

    lax.fori_loop(0, slabs, one, 0)


def around(slabs, subs):
    slab, sub = lax.axis_index("slab"), lax.axis_index("sub")
    up, down = lax.rem(sub + 1, subs), lax.rem(sub + subs - 1, subs)
    turns = [lax.rem(slab + k, slabs) for k in range(slabs)]
    return slab, sub, up, down, turns


def send_packet(slabs, subs, source_ref, all_ref, send_sem, recv_sem, first):
    slab, sub, up, down, turns = around(slabs, subs)
    goals = [(t, sub, slab) for t in turns[1:]]
    goals += [(t, up, slabs + slab) for t in turns]
    goals += [(slab, down, 2 * slabs)]
    copies = []
    for number, (to_slab, to_sub, slot) in enumerate(goals):
        copies.append(
            pltpu.make_async_remote_copy(
                src_ref=source_ref,
                dst_ref=all_ref.at[slot],
                send_sem=send_sem.at[first + number],
                recv_sem=recv_sem.at[slot],
                device_id=(to_slab, to_sub),
                device_id_type=MESH,
            )
        )
    return copies


def wait_packets(slabs, subs, all_ref, recv_sem):
    slab, sub, up, down, turns = around(slabs, subs)
    for slot in [*turns[1:], *(slabs + k for k in range(slabs)), 2 * slabs]:
        pltpu.make_async_copy(all_ref.at[slot], all_ref.at[slot], recv_sem.at[slot]).wait()


def greet(peers):
    barrier = pltpu.get_barrier_semaphore()
    for peer in peers:
        pl.semaphore_signal(barrier, inc=1, device_id=peer, device_id_type=MESH)
    pl.semaphore_wait(barrier, len(peers))


def all_peers(slabs, subs):
    slab, sub, up, down, turns = around(slabs, subs)
    return [(t, sub) for t in turns[1:]] + [(t, up) for t in turns] + [(t, down) for t in turns]


def start_kernel(
    slabs,
    subs,
    pol_ref,
    perm_ref,
    pos_ref,
    frac_ref,
    base_ref,
    lists_ref,
    top_ref,
    low_ref,
    influence_ref,
    all_ref,
    tx_ref,
    ty_ref,
    zh_ref,
    planes_ref,
    mids_ref,
    packet_ref,
    moved_ref,
    turned_ref,
    hop_ref,
    send_sem,
    recv_sem,
    move_sem,
    plane_send,
    plane_recv,
    hop_send,
    hop_recv,
    mid_send,
    mid_recv,
):
    slab, sub, up, down, turns = around(slabs, subs)
    depth, rows = moved_ref.shape[0], moved_ref.shape[1]
    half = slabs * subs
    middle = subs // 2
    group = 2 * subs

    moves = [pltpu.make_async_copy(influence_ref.at[:, i, :], moved_ref.at[i], move_sem.at[i]) for i in range(depth)]
    for move in moves:
        move.start()
    packet_ref[0:3] = pol_ref[...] * perm_ref[...]
    packet_ref[3:6] = pos_ref[...]
    packet_ref[6:9] = frac_ref[...]
    packet_ref[9:12] = base_ref[...].astype(jnp.float32)
    packet_ref[12:16] = jnp.zeros((4, packet_ref.shape[1]), jnp.float32)
    packet_ref[12:13, : lists_ref.shape[1]] = lists_ref[...].astype(jnp.float32)
    copies = send_packet(slabs, subs, packet_ref, all_ref, send_sem, recv_sem, 0)
    for copy in copies:
        copy.start()
    all_ref[slab] = packet_ref[...]

    def plane(i):
        kz = depth * sub + i
        upper = kz >= half
        folded = jnp.where(upper, lax.rem(2 * half - kz, half), kz)
        slot = jnp.where(upper, 1, 0)
        to_slab, to_sub = lax.rem(folded, slabs), lax.div(folded, slabs)
        target = planes_ref.at[slot, pl.ds(slab * rows, rows)]
        far = pltpu.make_async_remote_copy(
            src_ref=moved_ref.at[i],
            dst_ref=target,
            send_sem=plane_send.at[i],
            recv_sem=plane_recv.at[slot, slab],
            device_id=(to_slab, to_sub),
            device_id_type=MESH,
        )
        return far, slot, jnp.logical_and(to_slab == slab, to_sub == sub)

    def here(i, slot):
        return pltpu.make_async_copy(
            moved_ref.at[i], planes_ref.at[slot, pl.ds(slab * rows, rows)], plane_recv.at[slot, slab]
        )

    for i in range(depth):
        moves[i].wait()
        far, slot, mine = plane(i)

        @pl.when(mine)
        def _():
            here(i, slot).start()

        @pl.when(jnp.logical_not(mine))
        def _():
            far.start()

    first = moved_ref[0]
    turned_ref[...] = jnp.concatenate([first] + [first] * (LANES // rows - 1), axis=0).T

    def hop(number):
        return pltpu.make_async_remote_copy(
            src_ref=turned_ref.at[pl.ds(turns[number] * group, group)],
            dst_ref=hop_ref.at[slab],
            send_sem=hop_send.at[number - 1],
            recv_sem=hop_recv.at[slab],
            device_id=(turns[number], sub),
            device_id_type=MESH,
        )

    def mid(number):
        to_sub = lax.rem(middle + number, subs)
        return pltpu.make_async_remote_copy(
            src_ref=hop_ref.at[:, pl.ds(lax.div(to_sub, 4) * 8, 8)],
            dst_ref=mids_ref,
            send_sem=mid_send.at[number - 1],
            recv_sem=mid_recv,
            device_id=(slab, to_sub),
            device_id_type=MESH,
        )

    @pl.when(sub == middle)
    def _():
        for number in range(1, slabs):
            hop(number).start()
        hop_ref[slab] = turned_ref[pl.ds(pl.multiple_of(slab * group, group), group)]

    wait_packets(slabs, subs, all_ref, recv_sem)
    phase = (top_ref[...], low_ref[...])

    def one(block, _):
        tables_of(all_ref, block, phase, tx_ref, ty_ref, zh_ref)
        return 0

    lax.fori_loop(0, slabs, one, 0)

    @pl.when(sub == middle)
    def _():
        for t in turns[1:]:
            pltpu.make_async_copy(hop_ref.at[t], hop_ref.at[t], hop_recv.at[t]).wait()
        for number in range(1, subs):
            mid(number).start()
        mids_ref[...] = hop_ref[:, (middle // 4) * 8 : (middle // 4) * 8 + 8]

    lax.fori_loop(slabs, 2 * slabs, one, 0)

    @pl.when(sub == middle)
    def _():
        for number in range(1, slabs):
            hop(number).wait_send()
        for number in range(1, subs):
            mid(number).wait_send()

    @pl.when(sub != middle)
    def _():
        pltpu.make_async_copy(mids_ref, mids_ref, mid_recv).wait()

    for slot in range(2):
        for source in range(slabs):
            target = planes_ref.at[slot, pl.ds(source * rows, rows)]
            pltpu.make_async_copy(target, target, plane_recv.at[slot, source]).wait()
    for i in range(depth):
        far, slot, mine = plane(i)

        @pl.when(jnp.logical_not(mine))
        def _():
            far.wait_send()

    for copy in copies:
        copy.wait_send()


def update_kernel(slabs, subs, last, share_ref, rest_ref, pol_ref, *refs):
    if last:
        out_ref, land_ref, send_sem, land_sem = refs
    else:
        out_ref, all_ref, land_ref, send_sem, land_sem, recv_sem = refs
    slab, sub, up, down, turns = around(slabs, subs)
    greet(all_peers(slabs, subs))
    goals = [(t, sub, t, slab) for t in turns[1:]] + [(t, down, slabs + t, slabs + slab) for t in turns]
    copies = []
    for number, (to_slab, to_sub, source, slot) in enumerate(goals):
        copies.append(
            pltpu.make_async_remote_copy(
                src_ref=share_ref.at[source],
                dst_ref=land_ref.at[slot],
                send_sem=send_sem.at[number],
                recv_sem=land_sem.at[slot],
                device_id=(to_slab, to_sub),
                device_id_type=MESH,
            )
        )
    for copy in copies:
        copy.start()
    total = rest_ref[...] + share_ref[slab]
    for slot in [*turns[1:], *(slabs + k for k in range(slabs))]:
        pltpu.make_async_copy(land_ref.at[slot], land_ref.at[slot], land_sem.at[slot]).wait()
        total = total + land_ref[slot]
    moments = pol_ref[...] * total
    out_ref[...] = moments[: out_ref.shape[0]]
    if not last:
        more = send_packet(slabs, subs, out_ref, all_ref, send_sem, recv_sem, len(goals))
        for copy in more:
            copy.start()
        all_ref[slab] = moments
        wait_packets(slabs, subs, all_ref, recv_sem)
        copies += more
    for copy in copies:
        copy.wait_send()


def in_vmem(
    body, name, shapes, operands, scratch=(), smem_first=False, collective=None, anywhere=None, flops=0
):
    vmem = pl.BlockSpec(memory_space=pltpu.VMEM)
    smem = pl.BlockSpec(memory_space=pltpu.SMEM)
    params = dict(vmem_limit_bytes=56 << 20)
    if collective is not None:
        params.update(collective_id=collective, has_side_effects=True)
    if anywhere is not None:
        params.update(has_side_effects=True)
    specs = [smem if smem_first and n == 0 else vmem for n in range(len(operands))]
    if anywhere is not None:
        specs[anywhere] = pl.BlockSpec(memory_space=pl.ANY)
    out_shape = [jax.ShapeDtypeStruct(shape, jnp.float32) for shape in shapes]
    single = len(shapes) == 1
    return pl.pallas_call(
        body,
        out_shape=out_shape[0] if single else out_shape,
        in_specs=specs,
        out_specs=vmem if single else [vmem] * len(shapes),
        scratch_shapes=list(scratch),
        compiler_params=pltpu.CompilerParams(**params),
        cost_estimate=pl.CostEstimate(flops=flops, bytes_accessed=1 << 22, transcendentals=0),
        name=name,
    )(*operands)


def shards(
    positions,
    fraction,
    grid_base,
    polarizability,
    perm_field,
    influence,
    neighbour_cells,
    neighbour_count,
    send_cells,
):
    atoms = positions.shape[1]
    cells = neighbour_cells.shape[0]
    width = atoms // cells
    ghosts = send_cells.shape[2]
    slabs = lax.axis_size("slab")
    subs = lax.axis_size("sub")
    slab = lax.axis_index("slab")
    sub = lax.axis_index("sub")
    grid_x = G // slabs
    grid_y = G // subs
    half = G // 2

    index = np.arange(G)
    angle = (index[:, None] * index[None, :] % G) * (2.0 * np.pi / G)
    signed = np.where(index < half, index, index - G).astype(np.float32)

    kz_here = slabs * sub + slab

    slab_word = slab.astype(jnp.int32).reshape(1)
    kz_rows = np.arange(slabs)[:, None] + slabs * np.arange(subs)[None, :]
    turn = kz_rows[:, :, None] * index[None, None, :] % G * (2.0 * np.pi / G)
    phase = np.zeros((slabs, 2 * subs + 8, G), np.float32)
    phase[:, :subs] = np.cos(turn)
    phase[:, subs : 2 * subs] = -np.sin(turn)
    phase[:, 2 * subs] = np.where(index % 2 == 0, 1.0, -1.0)
    cos_np, sin_np = np.cos(angle), np.sin(angle)
    turn_x = parts_of(np.block([[cos_np, -sin_np], [sin_np, cos_np]]))
    back_x = parts_of(np.block([[cos_np, sin_np], [-sin_np, cos_np]]))
    turn_y = parts_of(np.concatenate([cos_np, sin_np], axis=1))
    back_y = parts_of(np.concatenate([cos_np, -sin_np], axis=1))
    wide = np.stack(
        [
            np.concatenate([cos_np[w : w + LANES], -sin_np[w : w + LANES]], axis=0)
            for w in (np.arange(slabs) // 2 * LANES)
        ]
    )

    def mine(pair):
        return tuple(lax.dynamic_index_in_dim(p, slab, 0, keepdims=False) for p in pair)

    phase, back_mid = mine(parts_of(phase)), mine(parts_of(wide))
    select = np.zeros((4, LANES, LANES), np.float32)
    for q in range(4):
        for lane in range(LANES):
            select[q, lane, 2 + 2 * q + lane % 2] = 1.0
    gather = jnp.asarray(select.reshape(4 * LANES, LANES), jnp.bfloat16)
    expand = jnp.asarray(np.concatenate(list(select.transpose(0, 2, 1)), axis=1), jnp.bfloat16)
    slots = 2 * slabs + 1
    ranks = 2 * subs + 8
    depth = G // subs
    dma = pltpu.SemaphoreType.DMA
    packets, tx, ty, zh, planes, mids = in_vmem(
        functools.partial(start_kernel, slabs, subs),
        "start",
        [
            (slots, 16, atoms),
            (2 * slabs, grid_x + 16, atoms),
            (2 * slabs, 16, atoms),
            (2 * slabs, ranks, atoms),
            (2, G, G),
            (slabs, 8, LANES),
        ],
        [
            polarizability[None, :],
            perm_field,
            positions,
            fraction,
            grid_base,
            send_cells.reshape(1, 4 * ghosts),
            *phase,
            influence,
        ],
        [
            pltpu.VMEM((16, atoms), jnp.float32),
            pltpu.VMEM((depth, grid_x, G), jnp.float32),
            pltpu.VMEM((G, LANES), jnp.float32),
            pltpu.VMEM((slabs, grid_x, LANES), jnp.float32),
            dma((2 * slabs,)),
            dma((slots,)),
            dma((depth,)),
            dma((depth,)),
            dma((2, slabs)),
            dma((slabs - 1,)),
            dma((slabs,)),
            dma((subs - 1,)),
            dma,
        ],
        anywhere=8,
        flops=1 << 31,
    )

    flip = jnp.asarray((index[:, None] == (-index[None, :]) % G).astype(np.float32))
    mirrored = jnp.dot(jnp.dot(flip, planes[1], precision=highest), flip, precision=highest)
    first = planes[0]
    sq = jnp.asarray(signed[:, None] ** 2 + signed[None, :] ** 2)
    kzf = kz_here.astype(jnp.float32)
    freq_sq = sq + kzf * kzf
    width_sq = G / 4.0 * (G / 4.0)
    gauss = jnp.where(
        freq_sq == 0.0,
        0.0,
        jnp.exp(-freq_sq / (2.0 * width_sq)) / jnp.where(freq_sq == 0.0, 1.0, freq_sq),
    ) * (-recip_scale / (float(G) ** 3))
    flat = kz_here == 0
    kernel_even = gauss * jnp.where(flat, first, first + mirrored)
    kernel_odd = gauss * jnp.where(flat, first, first - mirrored)
    mid = lax.dynamic_slice_in_dim(mids[:, :, :grid_x], lax.rem(2 * sub, 8), 2, 1)
    mid = jnp.transpose(mid, (1, 0, 2)).reshape(2, G)
    kx_mid = (2 * (subs * slab + sub) + jnp.arange(2, dtype=jnp.int32)).astype(jnp.float32)
    kx_mid = jnp.where(kx_mid < half, kx_mid, kx_mid - G)
    mid_sq = (kx_mid * kx_mid)[None, :] + jnp.asarray(signed[:, None] ** 2) + float(half * half)
    kernel_mid = (
        jnp.transpose(mid) * jnp.exp(-mid_sq / (2.0 * width_sq)) / mid_sq * (-recip_scale / (float(G) ** 3))
    )

    mid_tile = jnp.concatenate(
        [jnp.zeros((G, 2), jnp.float32), kernel_mid, kernel_mid, jnp.zeros((G, LANES - 6), jnp.float32)], axis=1
    )

    def near_of(blocks):
        own = [lax.dynamic_index_in_dim(blocks, k, 0, keepdims=False) for k in (
            slab,
            slabs + slab,
            2 * slabs,
            lax.rem(slab + slabs - 1, slabs),
            lax.rem(slab + 1, slabs),
        )]
        return jnp.stack(own)

    near = near_of(packets)

    ghost_lists = jnp.stack(
        [near[1 + q, 12, q * ghosts : (q + 1) * ghosts] for q in range(4)]
    ).astype(jnp.int32)
    near_atoms = jnp.pad(jnp.transpose(positions), ((0, 0), (0, 5)))

    def far_table(near_moments):
        rows = jnp.concatenate([near[:, 3:6], near_moments], axis=1)
        rows = jnp.transpose(rows.reshape(5, 6, cells, width), (0, 2, 1, 3)).reshape(5 * cells, 6, width)
        rows = jnp.pad(rows, ((0, 0), (0, 2), (0, 0)))
        return jnp.concatenate([rows, rows], axis=2)

    def reciprocal(block_moments):
        payload = in_vmem(
            functools.partial(spread_kernel, slabs, subs),
            "spread",
            [(subs * TILES * grid_y, LANES)],
            [slab_word, block_moments, tx, ty, zh, *turn_x, gather],
            [pltpu.VMEM((grid_y, G + 8, 256), jnp.float32), pltpu.VMEM((4, grid_y, G), jnp.float32)],
            smem_first=True,
            flops=1 << 33,
        ).reshape(subs, TILES * grid_y, LANES)
        got = lax.all_to_all(payload, "sub", split_axis=0, concat_axis=0, tiled=True)
        payload = in_vmem(
            middle_kernel,
            "second_frequency",
            [(subs, TILES * grid_y, LANES)],
            [got, kernel_even, kernel_odd, mid_tile, *turn_y, *back_y],
            flops=1 << 32,
        ).reshape(subs, TILES * grid_y, LANES)
        got = lax.all_to_all(payload, "sub", split_axis=0, concat_axis=0, tiled=True)
        columns = 6 * subs + 16
        return in_vmem(
            functools.partial(sample_kernel, slabs, subs),
            "sample",
            [(2 * slabs, 8, atoms)],
            [slab_word, got, tx, ty, zh, *back_x, *back_mid, expand],
            [
                pltpu.VMEM((6 * G * G // LANES, LANES), jnp.float32),
                pltpu.VMEM((2, grid_y, columns, G), jnp.bfloat16),
                pltpu.VMEM((2, grid_y, columns, G), jnp.bfloat16),
            ],
            smem_first=True,
            flops=1 << 33,
        )

    block_moments = packets
    near_moments = near[:, :3]
    pol = polarizability[None, :]
    for advance in range(ITERS):
        last = advance + 1 == ITERS
        pair = pair_field(neighbour_cells, neighbour_count, ghost_lists, far_table(near_moments), near_atoms)
        share = reciprocal(block_moments)
        rest = jnp.pad(perm_field + jnp.transpose(pair[:, :3]), ((0, 5), (0, 0)))
        scratch = [
            pltpu.VMEM((2 * slabs, 8, atoms), jnp.float32),
            pltpu.SemaphoreType.DMA((4 * slabs,)),
            pltpu.SemaphoreType.DMA((2 * slabs,)),
        ]
        if last:
            moments = in_vmem(
                functools.partial(update_kernel, slabs, subs, True),
                "last_update",
                [(3, atoms)],
                [share, rest, pol],
                scratch,
                collective=2,
            )
        else:
            moments, blocks = in_vmem(
                functools.partial(update_kernel, slabs, subs, False),
                "update",
                [(8, atoms), (slots, 8, atoms)],
                [share, rest, pol],
                scratch + [pltpu.SemaphoreType.DMA((slots,))],
                collective=3,
            )
            block_moments, near_moments = blocks, near_of(blocks)[:, :3]
    return moments


def solution(mesh):
    in_specs = (
        P(None, ("slab", "sub")),
        P(None, ("slab", "sub")),
        P(None, ("slab", "sub")),
        P(("slab", "sub")),
        P(None, ("slab", "sub")),
        P("slab", "sub", None),
        P(("slab", "sub"), None),
        P(("slab", "sub")),
        P(("slab", "sub"), None, None),
    )
    out_specs = P(None, ("slab", "sub"))
    return jax.shard_map(shards, mesh=mesh, in_specs=in_specs, out_specs=out_specs, check_vma=False)
```

```python
import functools
import math

import jax
import jax.numpy as jnp
import numpy as np
from jax import lax
from jax.experimental import pallas as pl
from jax.experimental.pallas import tpu as pltpu
from jax.sharding import PartitionSpec as P

G = 256
ITERS = 2

damping = 1.0
recip_scale = 16.0
highest = lax.Precision.HIGHEST
LANES = 128
TILES = 4 * G // LANES + 1
EXTRA = 2 * G // LANES
MESH = pl.DeviceIdType.MESH


def spline_weights(fraction):
    square = fraction * fraction
    cube = square * fraction
    rest = 1.0 - fraction
    return [
        rest * rest * rest / 6.0,
        (3.0 * cube - 6.0 * square + 4.0) / 6.0,
        (-3.0 * cube + 3.0 * square + 3.0 * fraction + 1.0) / 6.0,
        cube / 6.0,
    ]


def split(x):
    top = x.astype(jnp.bfloat16)
    return top, (x - top.astype(jnp.float32)).astype(jnp.bfloat16)


def dot3(a, b, turned=False):
    dims = (((1,), (1 if turned else 0,)), ((), ()))

    def one(x, y):
        return lax.dot_general(x, y, dims, preferred_element_type=jnp.float32)

    return one(a[0], b[0]) + (one(a[1], b[0]) + one(a[0], b[1]))


def parts_of(table):
    table = np.asarray(table, np.float32)
    top = table.astype(jnp.bfloat16)
    low = (table - top.astype(np.float32)).astype(jnp.bfloat16)
    return jnp.asarray(top), jnp.asarray(low)


def lanes_of(shape):
    return lax.broadcasted_iota(jnp.int32, shape, len(shape) - 1)


def rows_of(shape):
    return lax.broadcasted_iota(jnp.int32, shape, len(shape) - 2)


def window_of(slabs):
    return G // slabs + 8


def plane_rows(slabs, subs):
    window = window_of(slabs)
    return tuple(-(-count * window // LANES) * LANES for count in (G // subs, 3))


def tables_of(slabs, subs, still_ref, block, before, phase, top_ref, low_ref, zh_ref):
    at = block + slabs if before else block
    still = still_ref[at]
    atoms = still.shape[1]

    def table(axis, length, wrapped):
        start = still[3 + axis : 4 + axis].astype(jnp.int32)
        offset = rows_of((length, atoms)) - start
        if wrapped:
            offset = jnp.where(offset < 0, offset + length, offset)
        total = jnp.zeros(offset.shape, jnp.float32)
        for stencil, weight in enumerate(spline_weights(still[axis : 1 + axis])):
            total = jnp.where(offset == stencil, weight, total)
        return total

    along_x, along_y = table(0, window_of(slabs), False), table(1, 16, False)
    grid_y = G // subs
    first, count = (grid_y, 3) if before else (0, grid_y)
    own, spilt = plane_rows(slabs, subs)
    start, rows = (own, spilt) if before else (0, own)
    blank = jnp.zeros((rows - count * along_x.shape[0], atoms), jnp.float32)
    plane = [along_x * along_y[first + y : first + y + 1] for y in range(count)]
    top, low = split(jnp.concatenate([*plane, blank], axis=0))
    top_ref[block, start : start + rows] = top
    low_ref[block, start : start + rows] = low
    zh_ref[at] = dot3(phase, split(table(2, G, True)))


def frequency_rows(kind):
    k = lanes_of((1, G))
    signed = jnp.where(k < G // 2, k, k - G).astype(jnp.float32)
    if kind == "odd":
        return jnp.where(k == G // 2, 0.0, signed)
    if kind == "even":
        return jnp.where(k == G // 2, signed, 0.0)
    return signed


def frequency_columns(kind):
    k = lax.broadcasted_iota(jnp.int32, (G, 1), 0)
    signed = jnp.where(k < G // 2, k, k - G).astype(jnp.float32)
    if kind == "odd":
        return jnp.where(k == G // 2, 0.0, signed)
    if kind == "even":
        return jnp.where(k == G // 2, signed, 0.0)
    return signed


def density(slabs, subs, mom_ref, top_ref, low_ref, zh_ref, grid_ref):
    grid_y = G // subs
    grid_x = G // slabs
    window = window_of(slabs)
    own, _ = plane_rows(slabs, subs)
    grid_ref[...] = jnp.zeros_like(grid_ref)

    def one(block, _):
        for part in range(2):
            mu = mom_ref[part * slabs + block]
            zh = zh_ref[part * slabs + block]
            values = jnp.concatenate(
                [zh[: 2 * subs] * mu[c : c + 1] for c in range(3)] + [mu * zh[2 * subs : 2 * subs + 1]],
                axis=0,
            )
            start, count = (0, grid_y) if part == 0 else (own, 3)
            rows = -(-count * window // 16) * 16
            plane = tuple(ref[block, start : start + rows] for ref in (top_ref, low_ref))
            got = dot3(plane, split(values), True)
            columns = values.shape[0]
            for y in range(count):
                where = pl.ds(pl.multiple_of(block * grid_x, grid_x), window)
                grid_ref[y, where, :columns] += got[y * window : (y + 1) * window]
        return 0

    lax.fori_loop(0, slabs, one, 0)
    for y in range(grid_y):
        grid_ref[y, :8] += grid_ref[y, G : G + 8]


def first_frequency(slabs, subs, slab, grid_ref, wt_ref, wl_ref, sel_ref, out_ref, mid_ref, send_part):
    grid_y = G // subs
    half = G // 2
    flat_ref = out_ref.reshape(subs * TILES * grid_y, LANES)
    turned = [grid_ref[y, :G].T for y in range(grid_y)]
    weights = (wt_ref[...], wl_ref[...])

    def pair_rows(value, c):
        base = 2 * subs * c
        return jnp.concatenate([value[base : base + subs], value[base + subs : base + 2 * subs]], axis=1)

    def put(first, y, values):
        tiles = [v[:, t * LANES : (t + 1) * LANES] for v in values for t in range(v.shape[1] // LANES)]
        for t, value in enumerate(tiles):
            flat_ref[pl.ds((first + t) * grid_y + y, subs, stride=TILES * grid_y), :] = value

    spec = dot3(split(jnp.concatenate([pair_rows(v, 1) for v in turned], axis=0)), weights)
    for y in range(grid_y):
        put(EXTRA + 1, y, [spec[y * subs : (y + 1) * subs]])
    send_part(1)
    rows = []
    for v in turned:
        mids = v[6 * subs : 6 * subs + 8]
        rows += [pair_rows(v, 0), pair_rows(v, 2), jnp.concatenate([mids, jnp.zeros_like(mids)], axis=1)]
    spec = dot3(split(jnp.concatenate(rows, axis=0)), weights)
    odd, signed = frequency_rows("odd"), frequency_rows("signed")
    kz = (slabs * lax.broadcasted_iota(jnp.int32, (subs, 1), 0) + slab).astype(jnp.float32)
    lane = lanes_of((subs, LANES))
    per_y = 2 * subs + 8
    for y in range(grid_y):
        at = spec[y * per_y : (y + 1) * per_y]
        sx, sz, mid = at[:subs], at[subs : 2 * subs], at[2 * subs :]
        edge = jnp.where(
            lane == 0,
            -float(half) * sx[:, half : half + 1],
            jnp.where(lane == 1, -float(half) * sx[:, G + half : G + half + 1], 0.0),
        )
        put(0, y, [odd * sx[:, :G] + kz * sz[:, :G], odd * sx[:, G:] + kz * sz[:, G:], edge])
        for part, shift in ((0, 0), (1, G)):
            mx, my, mz = (mid[c : c + 1, shift : shift + G] for c in range(3))
            mid_ref[part, y : y + 1] = signed * mx - float(half) * mz
            mid_ref[2 + part, y : y + 1] = my
    window = pl.ds(pl.multiple_of(slab // 2 * LANES, LANES), LANES)
    pair = (lanes_of((grid_y, LANES)) - lax.rem(slab, 2) * (2 * subs)) >> 1
    columns = []
    for q in range(4):
        value = mid_ref[q, :, window]
        columns.append(jnp.concatenate([jnp.where(pair == j, value, 0.0) for j in range(subs)], axis=0))
    top, low = split(jnp.concatenate(columns, axis=1))
    sel = sel_ref[...]
    more = jnp.dot(top, sel, preferred_element_type=jnp.float32) + jnp.dot(
        low, sel, preferred_element_type=jnp.float32
    )
    out_ref[:, EXTRA * grid_y : (EXTRA + 1) * grid_y, :] += more.reshape(subs, grid_y, LANES)
    send_part(0)


def part_rows(part, high):
    return (0, (EXTRA + 1) * high) if part == 0 else ((EXTRA + 1) * high, EXTRA * high)


def from_tiles(ref, part):
    blocks, rows, lanes = ref.shape
    high = rows // TILES
    first, count = part_rows(part, high)
    return jnp.concatenate(
        [ref[:, r : r + high, :].reshape(blocks * high, lanes) for r in range(first, first + count, high)], axis=1
    )


def to_tiles(value, ref, part):
    blocks, rows, lanes = ref.shape
    high = rows // TILES
    first, count = part_rows(part, high)
    for t in range(count // high):
        ref[:, first + t * high : first + (t + 1) * high, :] = value[:, t * lanes : (t + 1) * lanes].reshape(
            blocks, high, lanes
        )


def with_swapped(x):
    top, low = split(x[:, : 2 * G])
    both = [
        jnp.concatenate([v, jnp.concatenate([v[:, G:], -v[:, :G]], axis=1)], axis=0) for v in (top, low)
    ]
    if x.shape[1] > 2 * G:
        last = x[:, 2 * G :]
        lane = lanes_of(last.shape)
        back, on = pltpu.roll(last, LANES - 1, 1), pltpu.roll(last, 1, 1)
        back2, on2 = pltpu.roll(last, LANES - 2, 1), pltpu.roll(last, 2, 1)
        upper = ((lane - 2) & 2) == 0
        turned = jnp.where(lane == 0, back, jnp.where(lane == 1, -on, jnp.where(upper, back2, -on2)))
        more = split(jnp.concatenate([last, turned], axis=0))
        both = [jnp.concatenate([a, b], axis=1) for a, b in zip(both, more)]
    return tuple(both)


def second(got_ref, even_ref, odd_ref, mid_ref, ft_ref, fl_ref, bt_ref, bl_ref, out_ref, wait_part, send_part):
    half = G // 2
    forward, backward = (ft_ref[...], fl_ref[...]), (bt_ref[...], bl_ref[...])
    wait_part(1)
    b_all = dot3(forward, with_swapped(from_tiles(got_ref, 1)))
    wait_part(0)
    a_all = dot3(forward, with_swapped(from_tiles(got_ref, 0)))
    last = a_all[:, 2 * G :]
    lane = lanes_of(last.shape)
    at_half = (lanes_of((1, G)) == half).astype(jnp.float32)
    odd_y, even_y, full_y = (frequency_columns(k) for k in ("odd", "even", "signed"))
    kernel_even, kernel_odd = even_ref[...], odd_ref[...]
    phis, along_y, columns = [], [], []
    for part in range(2):
        a = a_all[:, part * G : (part + 1) * G]
        b = b_all[:, part * G : (part + 1) * G]
        level = a + odd_y * b
        edge = even_y * b + at_half * last[:, part : part + 1]
        phi = kernel_even * level + kernel_odd * edge
        phi_edge = kernel_odd * level + kernel_even * edge
        phis.append(phi)
        along_y.append(odd_y * phi + even_y * phi_edge)
        columns.append(phi_edge[:, half : half + 1])
    mid = mid_ref[...] * (last + full_y * pltpu.roll(last, LANES - 4, 1))
    mid = mid + full_y * pltpu.roll(mid, 4, 1)
    last = jnp.where(lane == 0, columns[0], jnp.where(lane == 1, columns[1], mid))
    to_tiles(dot3(backward, with_swapped(jnp.concatenate([*phis, last], axis=1))), out_ref, 0)
    send_part(0)
    to_tiles(dot3(backward, with_swapped(jnp.concatenate(along_y, axis=1))), out_ref, 1)
    send_part(1)


def sample(
    slabs,
    subs,
    slab,
    got_ref,
    top_ref,
    low_ref,
    zh_ref,
    wt_ref,
    wl_ref,
    mt_ref,
    ml_ref,
    sel_ref,
    out_ref,
    field_ref,
    here_ref,
    lhs_t_ref,
    lhs_l_ref,
    wait_part,
):
    grid_y = G // subs
    grid_x = G // slabs
    half = G // 2
    window = window_of(slabs)
    own, spilt = plane_rows(slabs, subs)
    weights = (wt_ref[...], wl_ref[...])

    def put(component, value):
        for t in range(2 * G // LANES):
            field_ref[pl.ds((3 * t + component) * G, G), :] = value[:, t * LANES : (t + 1) * LANES]

    wait_part(0)
    got = from_tiles(got_ref, 0)
    last = got[:, 2 * G :]
    odd, even = frequency_rows("odd"), frequency_rows("even")
    kz = (slabs * (lax.broadcasted_iota(jnp.int32, (G, 1), 0) // grid_y) + slab).astype(jnp.float32)
    phi = [got[:, :G], got[:, G : 2 * G]]
    along_x = [odd * phi[part] + even * last[:, part : part + 1] for part in range(2)]
    lhs = jnp.concatenate(
        [jnp.concatenate(along_x, axis=1), jnp.concatenate([kz * phi[0], kz * phi[1]], axis=1)], axis=0
    )
    field = dot3(split(lhs), weights)
    put(0, field[:G])
    put(2, field[G:])
    sel = sel_ref[...]
    top, low = split(last)
    expanded = jnp.dot(top, sel, preferred_element_type=jnp.float32) + jnp.dot(
        low, sel, preferred_element_type=jnp.float32
    )
    pair = ((lanes_of((grid_y, 4 * LANES)) & (LANES - 1)) - lax.rem(slab, 2) * (2 * subs)) >> 1
    mids = jnp.zeros((grid_y, 4 * LANES), jnp.float32)
    for j in range(subs):
        mids = mids + jnp.where(pair == j, expanded[j * grid_y : (j + 1) * grid_y], 0.0)
    k = slab // 2 * LANES + (lanes_of((1, 2 * LANES)) & (LANES - 1))
    signed = jnp.where(k < half, k, k - G).astype(jnp.float32)
    mid_phi = mids[:, : 2 * LANES]
    mid_lhs = jnp.concatenate([signed * mid_phi, mids[:, 2 * LANES :], -float(half) * mid_phi], axis=0)
    mid_field = dot3(split(mid_lhs), (mt_ref[...], ml_ref[...]))
    wait_part(1)
    put(1, dot3(split(from_tiles(got_ref, 1)), weights))
    row = rows_of((8, G))
    for y in range(grid_y):
        rows = []
        for c in range(3):
            for part in range(2):
                tiles = [
                    field_ref[pl.ds((3 * (part * G // LANES + t) + c) * G + y, subs, stride=grid_y), :]
                    for t in range(G // LANES)
                ]
                rows.append(jnp.concatenate(tiles, axis=1))
        mid = jnp.zeros((8, G), jnp.float32)
        for c in range(3):
            mid = jnp.where(row == c, mid_field[c * grid_y + y : c * grid_y + y + 1], mid)
        here_ref[y] = jnp.concatenate(rows + [mid, jnp.zeros((8, G), jnp.float32)], axis=0)
    lane = lanes_of((here_ref.shape[1], LANES))
    for block in range(slabs):
        turned = [pltpu.roll(here_ref[y], (window * y - grid_x * block) % G, 1) for y in range(grid_y)]
        tiles = []
        for t in range(own // LANES):
            value = jnp.zeros(lane.shape, jnp.float32)
            for y in range(grid_y):
                low_lane = window * y - LANES * t
                if low_lane + window <= 0 or low_lane >= LANES:
                    continue
                side = t * LANES % G
                inside = jnp.logical_and(lane >= low_lane, lane < low_lane + window)
                value = jnp.where(inside, turned[y][:, side : side + LANES], value)
            tiles.append(value)
        lhs_t_ref[block], lhs_l_ref[block] = split(jnp.concatenate(tiles, axis=1))

    def one(block, _):
        for part in range(2):
            zh = zh_ref[part * slabs + block]
            start, rows = (0, own) if part == 0 else (own, spilt)
            a = tuple(ref[block, :, :rows] for ref in (lhs_t_ref, lhs_l_ref))
            b = tuple(ref[block, start : start + rows] for ref in (top_ref, low_ref))
            mixed = dot3(a, b)
            fields = []
            for c in range(3):
                base = 2 * subs * c
                value = jnp.sum(mixed[base : base + 2 * subs] * zh[: 2 * subs], axis=0, keepdims=True)
                at = 6 * subs + c
                fields.append(value + mixed[at : at + 1] * zh[2 * subs : 2 * subs + 1])
            r = rows_of((8, zh.shape[1]))
            out_ref[part * slabs + block] = jnp.where(
                r == 0, fields[0], jnp.where(r == 1, fields[1], jnp.where(r == 2, fields[2], 0.0))
            )
        return 0

    lax.fori_loop(0, slabs, one, 0)


def kernel_planes(slabs, subs, slab, sub, planes_ref, mids_ref, even_ref, odd_ref, mid_ref):
    half = G // 2
    width_sq = G / 4.0 * (G / 4.0)
    scale = -recip_scale / (float(G) ** 3)
    flip = ((rows_of((G, G)) + lanes_of((G, G))) & (G - 1)) == 0
    flip = flip.astype(jnp.float32).astype(jnp.bfloat16)

    def product(a, b):
        return jnp.dot(a, b, preferred_element_type=jnp.float32)

    top, low = split(planes_ref[1])
    top, low = split(product(flip, top) + product(flip, low))
    mirrored = product(top, flip) + product(low, flip)
    first = planes_ref[0]
    kx, ky = frequency_rows("signed"), frequency_columns("signed")
    kz_here = slabs * sub + slab
    kz = kz_here.astype(jnp.float32)
    freq_sq = kx * kx + ky * ky + kz * kz
    anchor = freq_sq == 0.0
    gauss = jnp.where(
        anchor, 0.0, scale * jnp.exp(freq_sq * (-0.5 / width_sq)) / jnp.where(anchor, 1.0, freq_sq)
    )
    flat = kz_here == 0
    even_ref[...] = gauss * jnp.where(flat, first, first + mirrored)
    odd_ref[...] = gauss * jnp.where(flat, first, first - mirrored)
    rows = G // slabs
    tall = [
        jnp.concatenate([mids_ref[s]] * (LANES // 8), axis=0).T[:rows] for s in range(slabs)
    ]
    tall = jnp.concatenate(tall, axis=0)
    lane = lanes_of(tall.shape)
    chosen = lax.rem(2 * sub, 8)
    columns = [jnp.sum(jnp.where(lane == chosen + t, tall, 0.0), axis=1, keepdims=True) for t in range(2)]
    kx = 2 * (subs * slab + sub) + (lane & 1)
    kx = jnp.where(kx < half, kx, kx - G).astype(jnp.float32)
    mid_sq = kx * kx + ky * ky + float(half * half)
    value = jnp.where((lane & 1) == 0, columns[0], columns[1])
    value = jnp.where(jnp.logical_and(lane >= 2, lane < 6), value, 0.0)
    mid_ref[...] = value * (scale * jnp.exp(mid_sq * (-0.5 / width_sq)) / mid_sq)


def near_columns(positions, near_ref):
    for t in range(positions.shape[1] // LANES):
        tile = positions[:, t * LANES : (t + 1) * LANES]
        near_ref[t * LANES : (t + 1) * LANES, :] = jnp.concatenate([tile] * (LANES // 8), axis=0).T


def own_cells(own_ref, table_ref):
    for t in range(own_ref.shape[1] // LANES):
        tile = own_ref[:, t * LANES : (t + 1) * LANES]
        other = pltpu.roll(tile, LANES // 2, 1)
        first = lanes_of(tile.shape) < LANES // 2
        table_ref[2 * t] = jnp.where(first, tile, other)
        table_ref[2 * t + 1] = jnp.where(first, other, tile)


def pair_field(list_ref, count_ref, table_ref, near_ref, pair_ref):
    cells, entries = list_ref.shape
    width = LANES // 2
    first_half = lanes_of((8, LANES)) < width
    is_moment = rows_of((8, LANES)) < 3
    itself = rows_of((width, LANES)) == lanes_of((width, LANES))

    def one_cell(cell, _):
        base = pl.multiple_of(cell * width, width)
        near = near_ref[pl.ds(base, width), :]
        near_x, near_y, near_z = (
            jnp.broadcast_to(near[:, 3 + a : 4 + a], (width, LANES)) for a in range(3)
        )
        count = count_ref[cell]

        def terms(pair, masked):
            one = table_ref[list_ref[cell, 2 * pair]]
            two = table_ref[list_ref[cell, 2 * pair + 1]]
            live_one = jnp.where(2 * pair < count, 1.0, 0.0)
            live_two = jnp.where(2 * pair + 1 < count, 1.0, 0.0)
            far = jnp.where(first_half, one, two)
            far = jnp.where(is_moment, far * jnp.where(first_half, live_one, live_two), far)
            mx, my, mz = far[0:1], far[1:2], far[2:3]
            dx = near_x - far[3:4]
            dy = near_y - far[4:5]
            dz = near_z - far[5:6]
            softened = dx * dx + dy * dy + dz * dz + damping
            inverse = lax.rsqrt(softened)
            square = inverse * inverse
            cube = square * inverse
            if masked:
                cube = jnp.where(itself, 0.0, cube)
            radial = (3.0 * (dx * mx + dy * my + dz * mz)) * (cube * square)
            return radial * dx - cube * mx, radial * dy - cube * my, radial * dz - cube * mz

        def step(pair, totals):
            return tuple(t + a for t, a in zip(totals, terms(pair, False)))

        totals = lax.fori_loop(1, entries // 2, step, terms(0, True))
        sums = [jnp.sum(t, axis=1, keepdims=True) for t in totals]
        lane = lanes_of((width, LANES))
        pair_ref[pl.ds(base, width), :] = jnp.where(
            lane == 0, sums[0], jnp.where(lane == 1, sums[1], jnp.where(lane == 2, sums[2], 0.0))
        )
        return 0

    lax.fori_loop(0, cells, one_cell, 0)


def around(slabs, subs):
    slab, sub = lax.axis_index("slab"), lax.axis_index("sub")
    up, down = lax.rem(sub + 1, subs), lax.rem(sub + subs - 1, subs)
    turns = [lax.rem(slab + k, slabs) for k in range(slabs)]
    return slab, sub, up, down, turns


def remote(source, target, send_sem, recv_sem, device):
    return pltpu.make_async_remote_copy(
        src_ref=source,
        dst_ref=target,
        send_sem=send_sem,
        recv_sem=recv_sem,
        device_id=device,
        device_id_type=MESH,
    )


def landed(ref, sem):
    pltpu.make_async_copy(ref, ref, sem).wait()


INPUTS = (
    ["cells", "counts", "sends", "pol", "perm", "pos", "frac", "base"]
    + ["phase_t", "phase_l", "tx_t", "tx_l", "bx_t", "bx_l", "ty_t", "ty_l", "by_t", "by_l"]
    + ["bm_t", "bm_l", "gather", "expand", "influence"]
)
SMEM_INPUTS = 3


class Refs:
    def __init__(self, names, refs):
        for name, ref in zip(names, refs, strict=True):
            setattr(self, name, ref)


def whole_kernel(slabs, subs, names, *refs):
    r = Refs(names, refs)
    slab, sub, up, down, turns = around(slabs, subs)
    depth, rows = r.moved.shape[0], r.moved.shape[1]
    half = slabs * subs
    middle = subs // 2
    group = 2 * subs

    def to_group(source, target, send_sem, recv_sem):
        goals = [(t, sub, slab) for t in turns[1:]] + [(t, up, slabs + slab) for t in turns]
        return [
            remote(source, target.at[slot], send_sem.at[n], recv_sem.at[slot], (to_slab, to_sub))
            for n, (to_slab, to_sub, slot) in enumerate(goals)
        ]

    def group_landed(target, recv_sem):
        for slot in [*turns[1:], *(slabs + k for k in range(slabs))]:
            landed(target.at[slot], recv_sem.at[slot])

    def ghost_copies(it):
        goals = [(slab, up), (slab, down), (turns[1], sub), (turns[-1], sub)]
        cells, ghosts = r.cells.shape[0], r.ghosts.shape[2]
        return [
            remote(
                r.ghosts.at[it, q],
                r.tables.at[it, pl.ds(cells + q * ghosts, ghosts)],
                r.ghost_send.at[q],
                r.ghost_recv.at[it, q],
                goal,
            )
            for q, goal in enumerate(goals)
        ]

    def send_cells(it):
        own_cells(r.own, r.own_tiles)
        r.tables[it, : r.cells.shape[0]] = r.own_tiles[...]
        ghosts = r.ghosts.shape[2]
        for q in range(4):
            for slot in range(ghosts):
                r.ghosts[it, q, slot] = r.own_tiles[r.sends[q * ghosts + slot]]
        for copy in ghost_copies(it):
            copy.start()

    def send_moments(it):
        for copy in to_group(r.own, r.mom.at[it], r.mom_send, r.mom_recv.at[it]):
            copy.start()
        r.mom[it, slab] = r.own[...]
        send_cells(it)

    moves = [pltpu.make_async_copy(r.influence.at[:, i, :], r.moved.at[i], r.move.at[i]) for i in range(depth)]
    for move in moves:
        move.start()
    atoms = r.own.shape[1]
    r.own[0:3] = r.pol[...] * r.perm[...]
    r.own[3:6] = r.pos[...]
    r.own[6:8] = jnp.zeros((2, atoms), jnp.float32)
    r.still[slab, 0:3] = r.frac[...]
    r.still[slab, 3:6] = r.base[...].astype(jnp.float32)
    r.still[slab, 6:8] = jnp.zeros((2, atoms), jnp.float32)
    still_copies = to_group(r.still.at[slab], r.still, r.still_send, r.still_recv)
    for copy in still_copies:
        copy.start()
    send_moments(0)

    def plane(i):
        kz = depth * sub + i
        upper = kz >= half
        folded = jnp.where(upper, lax.rem(2 * half - kz, half), kz)
        slot = jnp.where(upper, 1, 0)
        to_slab, to_sub = lax.rem(folded, slabs), lax.div(folded, slabs)
        target = r.planes.at[slot, pl.ds(slab * rows, rows)]
        far = remote(
            r.moved.at[i], target, r.plane_send.at[i], r.plane_recv.at[slot, slab], (to_slab, to_sub)
        )
        return far, slot, jnp.logical_and(to_slab == slab, to_sub == sub)

    def here(i, slot):
        return pltpu.make_async_copy(
            r.moved.at[i], r.planes.at[slot, pl.ds(slab * rows, rows)], r.plane_recv.at[slot, slab]
        )

    for i in range(depth):
        moves[i].wait()
        far, slot, mine = plane(i)

        @pl.when(mine)
        def _():
            here(i, slot).start()

        @pl.when(jnp.logical_not(mine))
        def _():
            far.start()

    first = r.moved[0]
    r.turned[...] = jnp.concatenate([first] * (LANES // rows), axis=0).T

    def hop(n):
        return remote(
            r.turned.at[pl.ds(turns[n] * group, group)],
            r.hop.at[slab],
            r.hop_send.at[n - 1],
            r.hop_recv.at[slab],
            (turns[n], sub),
        )

    def mid(n):
        to_sub = lax.rem(middle + n, subs)
        return remote(
            r.hop.at[:, pl.ds(lax.div(to_sub, 4) * 8, 8)],
            r.mids,
            r.mid_send.at[n - 1],
            r.mid_recv,
            (slab, to_sub),
        )

    @pl.when(sub == middle)
    def _():
        for n in range(1, slabs):
            hop(n).start()
        r.hop[slab] = r.turned[pl.ds(pl.multiple_of(slab * group, group), group)]

    near_columns(r.own[...], r.near)
    group_landed(r.still, r.still_recv)
    phase = (r.phase_t[...], r.phase_l[...])

    def tables(before):
        def one(block, _):
            tables_of(slabs, subs, r.still, block, before, phase, r.plane_t, r.plane_l, r.zhat)
            return 0

        lax.fori_loop(0, slabs, one, 0)

    tables(False)

    @pl.when(sub == middle)
    def _():
        for t in turns[1:]:
            landed(r.hop.at[t], r.hop_recv.at[t])
        for n in range(1, subs):
            mid(n).start()
        r.mids[...] = r.hop[:, (middle // 4) * 8 : (middle // 4) * 8 + 8]

    tables(True)

    def exchange(send, got, part, send_sem, recv_sem):
        first, count = part_rows(part, send.shape[1] // TILES)
        rows = pl.ds(first, count)
        pltpu.make_async_copy(send.at[sub, rows], got.at[sub, rows], recv_sem.at[part]).start()

        def one(n, _):
            to_sub = lax.rem(sub + n, subs)
            remote(
                send.at[to_sub, rows], got.at[sub, rows], send_sem.at[part], recv_sem.at[part], (slab, to_sub)
            ).start()
            return 0

        lax.fori_loop(1, subs, one, 0)

    def exchanged(got, part, recv_sem):
        first, count = part_rows(part, got.shape[1] // TILES)
        landed(got.at[:, pl.ds(first, count)], recv_sem.at[part])

    def iteration(it, _):
        group_landed(r.mom.at[it], r.mom_recv.at[it])
        density(slabs, subs, r.mom.at[it], r.plane_t, r.plane_l, r.zhat, r.grid)
        got_a, got_b = r.got_a.at[it], r.got_b.at[it]
        first_frequency(
            slabs,
            subs,
            slab,
            r.grid,
            r.tx_t,
            r.tx_l,
            r.gather,
            r.send_a,
            r.mid_rows,
            lambda part: exchange(r.send_a, got_a, part, r.a_send, r.a_recv.at[it]),
        )

        @pl.when(it == 0)
        def _():
            @pl.when(sub != middle)
            def _():
                landed(r.mids, r.mid_recv)

            for slot in range(2):
                for source in range(slabs):
                    landed(r.planes.at[slot, pl.ds(source * rows, rows)], r.plane_recv.at[slot, source])
            kernel_planes(slabs, subs, slab, sub, r.planes, r.mids, r.even, r.odd, r.mid_tile)

        cells, ghosts = r.cells.shape[0], r.ghosts.shape[2]
        for q in range(4):
            landed(r.tables.at[it, pl.ds(cells + q * ghosts, ghosts)], r.ghost_recv.at[it, q])
        pair_field(r.cells, r.counts, r.tables.at[it], r.near, r.pair)
        for t in range(atoms // LANES):
            tile = r.pair[t * LANES : (t + 1) * LANES, :].T[:8]
            r.rest[:, t * LANES : (t + 1) * LANES] = tile
        r.rest[0:3] += r.perm[...]

        second(
            got_a,
            r.even,
            r.odd,
            r.mid_tile,
            r.ty_t,
            r.ty_l,
            r.by_t,
            r.by_l,
            r.send_b,
            lambda part: exchanged(got_a, part, r.a_recv.at[it]),
            lambda part: exchange(r.send_b, got_b, part, r.b_send, r.b_recv.at[it]),
        )
        sample(
            slabs,
            subs,
            slab,
            got_b,
            r.plane_t,
            r.plane_l,
            r.zhat,
            r.bx_t,
            r.bx_l,
            r.bm_t,
            r.bm_l,
            r.expand,
            r.share,
            r.field,
            r.here,
            r.lhs_t,
            r.lhs_l,
            lambda part: exchanged(got_b, part, r.b_recv.at[it]),
        )
        goals = [(t, sub, t, slab) for t in turns[1:]] + [(t, down, slabs + t, slabs + slab) for t in turns]
        shares = [
            remote(
                r.share.at[source],
                r.land.at[it, slot],
                r.share_send.at[n],
                r.share_recv.at[it, slot],
                (to_slab, to_sub),
            )
            for n, (to_slab, to_sub, source, slot) in enumerate(goals)
        ]
        for copy in shares:
            copy.start()
        total = r.rest[...] + r.share[slab]
        for slot in [*turns[1:], *(slabs + k for k in range(slabs))]:
            landed(r.land.at[it, slot], r.share_recv.at[it, slot])
            total = total + r.land[it, slot]
        for copy in to_group(r.own, r.mom.at[it], r.mom_send, r.mom_recv.at[it]):
            copy.wait_send()
        for copy in ghost_copies(it):
            copy.wait_send()
        r.own[0:3] = r.pol[...] * total[0:3]

        @pl.when(it + 1 < ITERS)
        def _():
            send_moments(it + 1)

        for copy in shares:
            copy.wait_send()
        for part in range(2):
            rows_sent = pl.ds(*part_rows(part, r.send_a.shape[1] // TILES))
            landed(r.send_a.at[pl.ds(0, subs - 1), rows_sent], r.a_send.at[part])
            landed(r.send_b.at[pl.ds(0, subs - 1), rows_sent], r.b_send.at[part])
        return 0

    lax.fori_loop(0, ITERS, iteration, 0)
    r.out[...] = r.own[0:3]
    for copy in still_copies:
        copy.wait_send()

    @pl.when(sub == middle)
    def _():
        for n in range(1, slabs):
            hop(n).wait_send()
        for n in range(1, subs):
            mid(n).wait_send()

    for i in range(depth):
        far, slot, mine = plane(i)

        @pl.when(jnp.logical_not(mine))
        def _():
            far.wait_send()


def shards(
    positions,
    fraction,
    grid_base,
    polarizability,
    perm_field,
    influence,
    neighbour_cells,
    neighbour_count,
    send_cells,
):
    atoms = positions.shape[1]
    cells = neighbour_cells.shape[0]
    ghosts = send_cells.shape[2]
    slabs = lax.axis_size("slab")
    subs = lax.axis_size("sub")
    slab = lax.axis_index("slab")
    grid_x = G // slabs
    grid_y = G // subs
    depth = G // subs

    index = np.arange(G)
    angle = (index[:, None] * index[None, :] % G) * (2.0 * np.pi / G)
    kz_rows = np.arange(slabs)[:, None] + slabs * np.arange(subs)[None, :]
    turn = kz_rows[:, :, None] * index[None, None, :] % G * (2.0 * np.pi / G)
    ranks = 2 * subs + 8
    phase = np.zeros((slabs, ranks, G), np.float32)
    phase[:, :subs] = np.cos(turn)
    phase[:, subs : 2 * subs] = -np.sin(turn)
    phase[:, 2 * subs] = np.where(index % 2 == 0, 1.0, -1.0)
    cos_np, sin_np = np.cos(angle), np.sin(angle)
    turn_x = parts_of(np.block([[cos_np, -sin_np], [sin_np, cos_np]]))
    back_x = parts_of(np.block([[cos_np, sin_np], [-sin_np, cos_np]]))
    turn_y = parts_of(np.concatenate([cos_np, sin_np], axis=1))
    back_y = parts_of(np.concatenate([cos_np, -sin_np], axis=1))
    wide = np.stack(
        [
            np.concatenate([cos_np[w : w + LANES], -sin_np[w : w + LANES]], axis=0)
            for w in (np.arange(slabs) // 2 * LANES)
        ]
    )

    def mine(pair):
        return tuple(lax.dynamic_index_in_dim(p, slab, 0, keepdims=False) for p in pair)

    phase, back_mid = mine(parts_of(phase)), mine(parts_of(wide))
    select = np.zeros((4, LANES, LANES), np.float32)
    for q in range(4):
        for lane in range(LANES):
            select[q, lane, 2 + 2 * q + lane % 2] = 1.0
    gather = jnp.asarray(select.reshape(4 * LANES, LANES), jnp.bfloat16)
    expand = jnp.asarray(np.concatenate(list(select.transpose(0, 2, 1)), axis=1), jnp.bfloat16)

    operands = [
        neighbour_cells,
        neighbour_count,
        send_cells.reshape(4 * ghosts),
        polarizability[None, :],
        perm_field,
        positions,
        fraction,
        grid_base,
        *phase,
        *turn_x,
        *back_x,
        *turn_y,
        *back_y,
        *back_mid,
        gather,
        expand,
        influence,
    ]
    vmem = pl.BlockSpec(memory_space=pltpu.VMEM)
    smem = pl.BlockSpec(memory_space=pltpu.SMEM)
    specs = [smem] * SMEM_INPUTS + [vmem] * (len(operands) - SMEM_INPUTS - 1) + [pl.BlockSpec(memory_space=pl.ANY)]

    def held(*shape, dtype=jnp.float32):
        return pltpu.VMEM(shape, dtype)

    held16 = functools.partial(held, dtype=jnp.bfloat16)
    dma = pltpu.SemaphoreType.DMA
    chunk = (subs, TILES * grid_y, LANES)
    columns = 6 * subs + 16
    sends = 2 * slabs - 1
    planes = sum(plane_rows(slabs, subs))
    scratch = dict(
        mom=held(ITERS, 2 * slabs, 8, atoms),
        still=held(2 * slabs, 8, atoms),
        own=held(8, atoms),
        own_tiles=held(cells, 8, LANES),
        tables=held(ITERS, cells + 4 * ghosts, 8, LANES),
        ghosts=held(ITERS, 4, ghosts, 8, LANES),
        near=held(atoms, LANES),
        pair=held(atoms, LANES),
        rest=held(8, atoms),
        plane_t=held16(slabs, planes, atoms),
        plane_l=held16(slabs, planes, atoms),
        zhat=held(2 * slabs, ranks, atoms),
        moved=held(depth, grid_x, G),
        turned=held(G, LANES),
        hop=held(slabs, grid_x, LANES),
        planes=held(2, G, G),
        mids=held(slabs, 8, LANES),
        even=held(G, G),
        odd=held(G, G),
        mid_tile=held(G, LANES),
        grid=held(grid_y, G + 8, 256),
        mid_rows=held(4, grid_y, G),
        send_a=held(*chunk),
        got_a=held(ITERS, *chunk),
        send_b=held(*chunk),
        got_b=held(ITERS, *chunk),
        field=held(6 * G * G // LANES, LANES),
        here=held(grid_y, columns, G),
        lhs_t=held16(slabs, columns, plane_rows(slabs, subs)[0]),
        lhs_l=held16(slabs, columns, plane_rows(slabs, subs)[0]),
        share=held(2 * slabs, 8, atoms),
        land=held(ITERS, 2 * slabs, 8, atoms),
        mom_send=dma((sends,)),
        mom_recv=dma((ITERS, 2 * slabs)),
        still_send=dma((sends,)),
        still_recv=dma((2 * slabs,)),
        ghost_send=dma((4,)),
        ghost_recv=dma((ITERS, 4)),
        move=dma((depth,)),
        plane_send=dma((depth,)),
        plane_recv=dma((2, slabs)),
        hop_send=dma((slabs - 1,)),
        hop_recv=dma((slabs,)),
        mid_send=dma((subs - 1,)),
        mid_recv=dma,
        a_send=dma((2,)),
        a_recv=dma((ITERS, 2)),
        b_send=dma((2,)),
        b_recv=dma((ITERS, 2)),
        share_send=dma((sends,)),
        share_recv=dma((ITERS, 2 * slabs)),
    )
    names = [*INPUTS, "out", *scratch]
    return pl.pallas_call(
        functools.partial(whole_kernel, slabs, subs, names),
        out_shape=jax.ShapeDtypeStruct((3, atoms), jnp.float32),
        in_specs=specs,
        out_specs=vmem,
        scratch_shapes=list(scratch.values()),
        compiler_params=pltpu.CompilerParams(vmem_limit_bytes=60 << 20, has_side_effects=True),
        name="dipoles",
    )(*operands)


def solution(mesh):
    in_specs = (
        P(None, ("slab", "sub")),
        P(None, ("slab", "sub")),
        P(None, ("slab", "sub")),
        P(("slab", "sub")),
        P(None, ("slab", "sub")),
        P("slab", "sub", None),
        P(("slab", "sub"), None),
        P(("slab", "sub")),
        P(("slab", "sub"), None, None),
    )
    out_specs = P(None, ("slab", "sub"))
    return jax.shard_map(shards, mesh=mesh, in_specs=in_specs, out_specs=out_specs, check_vma=False)
```

```python
import functools
import math

import jax
import jax.numpy as jnp
import numpy as np
from jax import lax
from jax.experimental import pallas as pl
from jax.experimental.pallas import tpu as pltpu
from jax.sharding import PartitionSpec as P

G = 256
ITERS = 2

damping = 1.0
recip_scale = 16.0
highest = lax.Precision.HIGHEST
LANES = 128
TILES = 4 * G // LANES + 1
MESH = pl.DeviceIdType.MESH


def spline_weights(fraction):
    square = fraction * fraction
    cube = square * fraction
    rest = 1.0 - fraction
    return [
        rest * rest * rest / 6.0,
        (3.0 * cube - 6.0 * square + 4.0) / 6.0,
        (-3.0 * cube + 3.0 * square + 3.0 * fraction + 1.0) / 6.0,
        cube / 6.0,
    ]


def split(x):
    top = x.astype(jnp.bfloat16)
    return top, (x - top.astype(jnp.float32)).astype(jnp.bfloat16)


def dot3(a, b, turned=False):
    dims = (((1,), (1 if turned else 0,)), ((), ()))

    def one(x, y):
        return lax.dot_general(x, y, dims, preferred_element_type=jnp.float32)

    return one(a[0], b[0]) + (one(a[1], b[0]) + one(a[0], b[1]))


def parts_of(table):
    table = np.asarray(table, np.float32)
    top = table.astype(jnp.bfloat16)
    low = (table - top.astype(np.float32)).astype(jnp.bfloat16)
    return jnp.asarray(top), jnp.asarray(low)


def lanes_of(shape):
    return lax.broadcasted_iota(jnp.int32, shape, len(shape) - 1)


def rows_of(shape):
    return lax.broadcasted_iota(jnp.int32, shape, len(shape) - 2)


def window_of(slabs):
    return G // slabs + 8


def plane_rows(slabs, subs):
    window = window_of(slabs)
    return tuple(-(-count * window // LANES) * LANES for count in (G // subs, 3))


def tables_of(slabs, subs, still_ref, block, before, phase, top_ref, low_ref, zh_ref):
    at = block + slabs if before else block
    still = still_ref[at]
    atoms = still.shape[1]

    def table(axis, length):
        offset = rows_of((length, atoms)) - still[3 + axis : 4 + axis].astype(jnp.int32)
        total = jnp.zeros(offset.shape, jnp.float32)
        for stencil, weight in enumerate(spline_weights(still[axis : 1 + axis])):
            total = jnp.where(offset == stencil, weight, total)
        return total

    along_x, along_y = table(0, window_of(slabs)), table(1, 16)
    grid_y = G // subs
    first, count = (grid_y, 3) if before else (0, grid_y)
    own, spilt = plane_rows(slabs, subs)
    start, rows = (own, spilt) if before else (0, own)
    blank = jnp.zeros((rows - count * along_x.shape[0], atoms), jnp.float32)
    plane = [along_x * along_y[first + y : first + y + 1] for y in range(count)]
    top, low = split(jnp.concatenate([*plane, blank], axis=0))
    top_ref[block, start : start + rows] = top
    low_ref[block, start : start + rows] = low
    z0 = still[5:6].astype(jnp.int32)
    chosen = (rows_of((G, atoms)) == z0).astype(jnp.float32).astype(jnp.bfloat16)
    start = jnp.dot(phase[0], chosen, preferred_element_type=jnp.float32) + jnp.dot(
        phase[1], chosen, preferred_element_type=jnp.float32
    )
    steps = phase[0][:, :LANES].astype(jnp.float32) + phase[1][:, :LANES].astype(jnp.float32)
    wide = [jnp.zeros((subs, atoms), jnp.float32)] * 2
    mid = jnp.zeros((1, atoms), jnp.float32)
    for t, weight in enumerate(spline_weights(still[2:3])):
        wide = [v + weight * steps[n * subs : (n + 1) * subs, t : t + 1] for n, v in enumerate(wide)]
        mid = mid + (weight if t % 2 == 0 else -weight)
    re, im = start[:subs], start[subs : 2 * subs]
    zh_ref[at, :subs] = re * wide[0] - im * wide[1]
    zh_ref[at, subs : 2 * subs] = re * wide[1] + im * wide[0]
    zh_ref[at, 2 * subs :] = start[2 * subs :] * mid


def frequency_rows(kind):
    k = lanes_of((1, G))
    signed = jnp.where(k < G // 2, k, k - G).astype(jnp.float32)
    if kind == "odd":
        return jnp.where(k == G // 2, 0.0, signed)
    if kind == "even":
        return jnp.where(k == G // 2, signed, 0.0)
    return signed


def frequency_columns(kind):
    k = lax.broadcasted_iota(jnp.int32, (G, 1), 0)
    signed = jnp.where(k < G // 2, k, k - G).astype(jnp.float32)
    if kind == "odd":
        return jnp.where(k == G // 2, 0.0, signed)
    if kind == "even":
        return jnp.where(k == G // 2, signed, 0.0)
    return signed


def density(slabs, subs, slab, mom_ref, top_ref, low_ref, zh_ref, grid_ref, wait_block):
    grid_y = G // subs
    grid_x = G // slabs
    window = window_of(slabs)
    own, _ = plane_rows(slabs, subs)
    grid_ref[...] = jnp.zeros_like(grid_ref)

    for part in range(2):

        def one(n, _):
            block = lax.rem(slab + n, slabs)
            at = block + part * slabs
            if part == 0:

                @pl.when(n > 0)
                def _():
                    wait_block(at)

            else:
                wait_block(at)
            mu = mom_ref[at]
            zh = zh_ref[at]
            row = rows_of((8, mu.shape[1]))
            last = jnp.where(row == 0, mu[0:1], jnp.where(row == 1, mu[1:2], mu[2:3]))
            values = jnp.concatenate(
                [zh[: 2 * subs] * mu[c : c + 1] for c in range(3)] + [last * zh[2 * subs : 2 * subs + 1]], axis=0
            )
            start, count = (0, grid_y) if part == 0 else (own, 3)
            rows = -(-count * window // 16) * 16
            plane = tuple(ref[block, start : start + rows] for ref in (top_ref, low_ref))
            got = dot3(plane, split(values), True)
            columns = values.shape[0]
            for y in range(count):
                where = pl.ds(pl.multiple_of(block * grid_x, grid_x), window)
                grid_ref[y, where, :columns] += got[y * window : (y + 1) * window]
            return 0

        lax.fori_loop(0, slabs, one, 0)
    for y in range(grid_y):
        grid_ref[y, :8] += grid_ref[y, G : G + 8]


def half_of(row, part):
    return row[:, part * LANES : (part + 1) * LANES]


def first_frequency(slabs, subs, slab, grid_ref, wt_ref, wl_ref, sel_ref, out_ref, mid_ref, send_part):
    grid_y = G // subs
    half = G // 2
    flat_ref = out_ref.reshape(subs * TILES * grid_y, LANES)
    rows = []
    for y in range(grid_y):
        turned = grid_ref[y, :G].T
        for c in range(3):
            base = 2 * subs * c
            rows.append(
                jnp.concatenate([turned[base : base + subs], turned[base + subs : base + 2 * subs]], axis=1)
            )
        mids = turned[6 * subs : 6 * subs + 8]
        rows.append(jnp.concatenate([mids, jnp.zeros_like(mids)], axis=1))
    lhs = split(jnp.concatenate(rows, axis=0))
    odd, signed = frequency_rows("odd"), frequency_rows("signed")
    kz = (slabs * lax.broadcasted_iota(jnp.int32, (subs, 1), 0) + slab).astype(jnp.float32)
    lane = lanes_of((subs, LANES))
    per_y = 3 * subs + 8

    def transformed(part):
        columns = slice(part * 2 * LANES, (part + 1) * 2 * LANES)
        spec = dot3(lhs, (wt_ref[:, columns], wl_ref[:, columns]))
        for y in range(grid_y):
            at = spec[y * per_y : (y + 1) * per_y]
            sx, sy, sz = (at[c * subs : (c + 1) * subs] for c in range(3))
            tiles = [
                half_of(odd, part) * half_of(sx, n) + kz * half_of(sz, n) for n in range(2)
            ] + [half_of(sy, 0), half_of(sy, 1)]
            if part == 1:
                tiles.append(
                    -float(half) * jnp.where(lane == 0, sx[:, :1], jnp.where(lane == 1, sx[:, LANES : LANES + 1], 0.0))
                )
            for t, value in enumerate(tiles):
                flat_ref[pl.ds((part * 4 + t) * grid_y + y, subs, stride=TILES * grid_y), :] = value
            mid = at[3 * subs :]
            lanes = slice(part * LANES, (part + 1) * LANES)
            for n in range(2):
                mx, my, mz = (half_of(mid[c : c + 1], n) for c in range(3))
                mid_ref[n, y : y + 1, lanes] = half_of(signed, part) * mx - float(half) * mz
                mid_ref[2 + n, y : y + 1, lanes] = my

    transformed(0)
    send_part(0)
    transformed(1)
    window = pl.ds(pl.multiple_of(slab // 2 * LANES, LANES), LANES)
    pair = (lanes_of((grid_y, LANES)) - lax.rem(slab, 2) * (2 * subs)) >> 1
    columns = []
    for q in range(4):
        value = mid_ref[q, :, window]
        columns.append(jnp.concatenate([jnp.where(pair == j, value, 0.0) for j in range(subs)], axis=0))
    top, low = split(jnp.concatenate(columns, axis=1))
    sel = sel_ref[...]
    more = jnp.dot(top, sel, preferred_element_type=jnp.float32) + jnp.dot(
        low, sel, preferred_element_type=jnp.float32
    )
    out_ref[:, (TILES - 1) * grid_y :, :] += more.reshape(subs, grid_y, LANES)
    send_part(1)


def part_rows(part, high):
    return (0, 4 * high) if part == 0 else (4 * high, (TILES - 4) * high)


def from_tiles(ref, part):
    blocks, rows, lanes = ref.shape
    high = rows // TILES
    first, count = part_rows(part, high)
    return jnp.concatenate(
        [ref[:, r : r + high, :].reshape(blocks * high, lanes) for r in range(first, first + count, high)], axis=1
    )


def to_tiles(value, ref, part):
    blocks, rows, lanes = ref.shape
    high = rows // TILES
    first, count = part_rows(part, high)
    for t in range(count // high):
        ref[:, first + t * high : first + (t + 1) * high, :] = value[:, t * lanes : (t + 1) * lanes].reshape(
            blocks, high, lanes
        )


def with_swapped(x):
    def tile(v, t):
        return v[:, t * LANES : (t + 1) * LANES]

    both = [
        jnp.concatenate([v, jnp.concatenate([tile(v, 1), -tile(v, 0), tile(v, 3), -tile(v, 2)], axis=1)], axis=0)
        for v in split(x[:, : 4 * LANES])
    ]
    if x.shape[1] > 4 * LANES:
        last = x[:, 4 * LANES :]
        lane = lanes_of(last.shape)
        back, on = pltpu.roll(last, LANES - 1, 1), pltpu.roll(last, 1, 1)
        back2, on2 = pltpu.roll(last, LANES - 2, 1), pltpu.roll(last, 2, 1)
        upper = ((lane - 2) & 2) == 0
        turned = jnp.where(lane == 0, back, jnp.where(lane == 1, -on, jnp.where(upper, back2, -on2)))
        more = split(jnp.concatenate([last, turned], axis=0))
        both = [jnp.concatenate([a, b], axis=1) for a, b in zip(both, more)]
    return tuple(both)


def second(got_ref, even_ref, odd_ref, mid_ref, ft_ref, fl_ref, bt_ref, bl_ref, out_ref, wait_part, send_part):
    forward, backward = (ft_ref[...], fl_ref[...]), (bt_ref[...], bl_ref[...])
    odd_y, even_y, full_y = (frequency_columns(k) for k in ("odd", "even", "signed"))
    for part in range(2):
        wait_part(part)
        spec = dot3(forward, with_swapped(from_tiles(got_ref, part)))
        lanes = slice(part * LANES, (part + 1) * LANES)
        kernel_even, kernel_odd = even_ref[:, lanes], odd_ref[:, lanes]
        lane = lanes_of(kernel_even.shape)
        last = spec[:, 4 * LANES :]
        tiles, columns = [None] * 4, []
        for n in range(2):
            a = spec[:, n * LANES : (n + 1) * LANES]
            b = spec[:, (2 + n) * LANES : (3 + n) * LANES]
            level = a + odd_y * b
            edge = even_y * b
            if part == 1:
                edge = edge + jnp.where(lane == 0, last[:, n : n + 1], 0.0)
            phi = kernel_even * level + kernel_odd * edge
            phi_edge = kernel_odd * level + kernel_even * edge
            tiles[n] = phi
            tiles[2 + n] = odd_y * phi + even_y * phi_edge
            columns.append(phi_edge[:, :1])
        if part == 1:
            mid = mid_ref[...] * (last + full_y * pltpu.roll(last, LANES - 4, 1))
            mid = mid + full_y * pltpu.roll(mid, 4, 1)
            tiles.append(jnp.where(lane == 0, columns[0], jnp.where(lane == 1, columns[1], mid)))
        to_tiles(dot3(backward, with_swapped(jnp.concatenate(tiles, axis=1))), out_ref, part)
        send_part(part)


def sample(
    slabs,
    subs,
    slab,
    got_ref,
    top_ref,
    low_ref,
    zh_ref,
    wt_ref,
    wl_ref,
    mt_ref,
    ml_ref,
    sel_ref,
    out_ref,
    field_ref,
    here_ref,
    lhs_t_ref,
    lhs_l_ref,
    wait_part,
):
    grid_y = G // subs
    grid_x = G // slabs
    half = G // 2
    window = window_of(slabs)
    own, spilt = plane_rows(slabs, subs)
    odd, even = frequency_rows("odd"), frequency_rows("even")
    kz = (slabs * (lax.broadcasted_iota(jnp.int32, (G, 1), 0) // grid_y) + slab).astype(jnp.float32)
    for part in range(2):
        wait_part(part)
        got = from_tiles(got_ref, part)
        last = got[:, 4 * LANES :]
        phi = got[:, : 2 * LANES]
        along_x = [half_of(odd, part) * half_of(phi, n) for n in range(2)]
        if part == 1:
            along_x = [v + half_of(even, part) * last[:, n : n + 1] for n, v in enumerate(along_x)]
        lhs = jnp.concatenate([jnp.concatenate(along_x, axis=1), got[:, 2 * LANES : 4 * LANES], kz * phi], axis=0)
        rows = slice(part * 2 * LANES, (part + 1) * 2 * LANES)
        field = dot3(split(lhs), (wt_ref[rows], wl_ref[rows]))
        for t in range(2 * G // LANES):
            where = pl.ds(3 * t * G, 3 * G)
            value = field[:, t * LANES : (t + 1) * LANES]
            field_ref[where, :] = value if part == 0 else field_ref[where, :] + value
    sel = sel_ref[...]
    top, low = split(last)
    expanded = jnp.dot(top, sel, preferred_element_type=jnp.float32) + jnp.dot(
        low, sel, preferred_element_type=jnp.float32
    )
    pair = ((lanes_of((grid_y, 4 * LANES)) & (LANES - 1)) - lax.rem(slab, 2) * (2 * subs)) >> 1
    mids = jnp.zeros((grid_y, 4 * LANES), jnp.float32)
    for j in range(subs):
        mids = mids + jnp.where(pair == j, expanded[j * grid_y : (j + 1) * grid_y], 0.0)
    k = slab // 2 * LANES + (lanes_of((1, 2 * LANES)) & (LANES - 1))
    signed = jnp.where(k < half, k, k - G).astype(jnp.float32)
    mid_phi = mids[:, : 2 * LANES]
    mid_lhs = jnp.concatenate([signed * mid_phi, mids[:, 2 * LANES :], -float(half) * mid_phi], axis=0)
    mid_field = dot3(split(mid_lhs), (mt_ref[...], ml_ref[...]))
    row = rows_of((8, G))
    for y in range(grid_y):
        rows = []
        for c in range(3):
            for part in range(2):
                tiles = [
                    field_ref[pl.ds((3 * (part * G // LANES + t) + c) * G + y, subs, stride=grid_y), :]
                    for t in range(G // LANES)
                ]
                rows.append(jnp.concatenate(tiles, axis=1))
        mid = jnp.zeros((8, G), jnp.float32)
        for c in range(3):
            mid = jnp.where(row == c, mid_field[c * grid_y + y : c * grid_y + y + 1], mid)
        here_ref[y] = jnp.concatenate(rows + [mid, jnp.zeros((8, G), jnp.float32)], axis=0)
    lane = lanes_of((here_ref.shape[1], LANES))
    for block in range(slabs):
        turned = [pltpu.roll(here_ref[y], (window * y - grid_x * block) % G, 1) for y in range(grid_y)]
        tiles = []
        for t in range(own // LANES):
            value = jnp.zeros(lane.shape, jnp.float32)
            for y in range(grid_y):
                low_lane = window * y - LANES * t
                if low_lane + window <= 0 or low_lane >= LANES:
                    continue
                side = t * LANES % G
                inside = jnp.logical_and(lane >= low_lane, lane < low_lane + window)
                value = jnp.where(inside, turned[y][:, side : side + LANES], value)
            tiles.append(value)
        lhs_t_ref[block], lhs_l_ref[block] = split(jnp.concatenate(tiles, axis=1))

    def one(block, _):
        for part in range(2):
            zh = zh_ref[part * slabs + block]
            start, rows = (0, own) if part == 0 else (own, spilt)
            a = tuple(ref[block, :, :rows] for ref in (lhs_t_ref, lhs_l_ref))
            b = tuple(ref[block, start : start + rows] for ref in (top_ref, low_ref))
            mixed = dot3(a, b)
            fields = []
            for c in range(3):
                base = 2 * subs * c
                value = jnp.sum(mixed[base : base + 2 * subs] * zh[: 2 * subs], axis=0, keepdims=True)
                at = 6 * subs + c
                fields.append(value + mixed[at : at + 1] * zh[2 * subs : 2 * subs + 1])
            for c in range(3):
                out_ref[part * slabs + block, c : c + 1] = fields[c]
        return 0

    lax.fori_loop(0, slabs, one, 0)


def kernel_planes(slabs, subs, slab, sub, planes_ref, mids_ref, even_ref, odd_ref, mid_ref):
    half = G // 2
    width_sq = G / 4.0 * (G / 4.0)
    scale = -recip_scale / (float(G) ** 3)
    flip = ((rows_of((G, G)) + lanes_of((G, G))) & (G - 1)) == 0
    flip = flip.astype(jnp.float32).astype(jnp.bfloat16)

    def product(a, b):
        return jnp.dot(a, b, preferred_element_type=jnp.float32)

    top, low = split(planes_ref[1])
    top, low = split(product(flip, top) + product(flip, low))
    mirrored = product(top, flip) + product(low, flip)
    first = planes_ref[0]
    kx, ky = frequency_rows("signed"), frequency_columns("signed")
    kz_here = slabs * sub + slab
    kz = kz_here.astype(jnp.float32)
    freq_sq = kx * kx + ky * ky + kz * kz
    anchor = freq_sq == 0.0
    gauss = jnp.where(
        anchor, 0.0, scale * jnp.exp(freq_sq * (-0.5 / width_sq)) / jnp.where(anchor, 1.0, freq_sq)
    )
    flat = kz_here == 0
    even_ref[...] = gauss * jnp.where(flat, first, first + mirrored)
    odd_ref[...] = gauss * jnp.where(flat, first, first - mirrored)
    rows = G // slabs
    tall = [
        jnp.concatenate([mids_ref[s]] * (LANES // 8), axis=0).T[:rows] for s in range(slabs)
    ]
    tall = jnp.concatenate(tall, axis=0)
    lane = lanes_of(tall.shape)
    chosen = lax.rem(2 * sub, 8)
    columns = [jnp.sum(jnp.where(lane == chosen + t, tall, 0.0), axis=1, keepdims=True) for t in range(2)]
    kx = 2 * (subs * slab + sub) + (lane & 1)
    kx = jnp.where(kx < half, kx, kx - G).astype(jnp.float32)
    mid_sq = kx * kx + ky * ky + float(half * half)
    value = jnp.where((lane & 1) == 0, columns[0], columns[1])
    value = jnp.where(jnp.logical_and(lane >= 2, lane < 6), value, 0.0)
    mid_ref[...] = value * (scale * jnp.exp(mid_sq * (-0.5 / width_sq)) / mid_sq)


def near_columns(positions, near_ref):
    for t in range(positions.shape[1] // LANES):
        tile = positions[:, t * LANES : (t + 1) * LANES]
        near_ref[t * LANES : (t + 1) * LANES, :] = jnp.concatenate([tile] * (LANES // 8), axis=0).T


def own_cells(own_ref, table_ref):
    for t in range(own_ref.shape[1] // LANES):
        tile = own_ref[:, t * LANES : (t + 1) * LANES]
        other = pltpu.roll(tile, LANES // 2, 1)
        first = lanes_of(tile.shape) < LANES // 2
        table_ref[2 * t] = jnp.where(first, tile, other)
        table_ref[2 * t + 1] = jnp.where(first, other, tile)


def pair_field(list_ref, count_ref, table_ref, near_ref, pair_ref):
    cells, entries = list_ref.shape
    width = LANES // 2
    first_half = lanes_of((8, LANES)) < width
    is_moment = rows_of((8, LANES)) < 3
    itself = rows_of((width, LANES)) == lanes_of((width, LANES))

    def one_cell(cell, _):
        base = pl.multiple_of(cell * width, width)
        near = near_ref[pl.ds(base, width), :]
        near_x, near_y, near_z = (
            jnp.broadcast_to(near[:, 3 + a : 4 + a], (width, LANES)) for a in range(3)
        )
        count = count_ref[cell]

        def terms(pair, masked):
            one = table_ref[list_ref[cell, 2 * pair]]
            two = table_ref[list_ref[cell, 2 * pair + 1]]
            live_one = jnp.where(2 * pair < count, 1.0, 0.0)
            live_two = jnp.where(2 * pair + 1 < count, 1.0, 0.0)
            far = jnp.where(first_half, one, two)
            far = jnp.where(is_moment, far * jnp.where(first_half, live_one, live_two), far)
            mx, my, mz = far[0:1], far[1:2], far[2:3]
            dx = near_x - far[3:4]
            dy = near_y - far[4:5]
            dz = near_z - far[5:6]
            softened = dx * dx + dy * dy + dz * dz + damping
            inverse = lax.rsqrt(softened)
            square = inverse * inverse
            cube = square * inverse
            if masked:
                cube = jnp.where(itself, 0.0, cube)
            radial = (3.0 * (dx * mx + dy * my + dz * mz)) * (cube * square)
            return radial * dx - cube * mx, radial * dy - cube * my, radial * dz - cube * mz

        def step(pair, totals):
            return tuple(t + a for t, a in zip(totals, terms(pair, False)))

        totals = lax.fori_loop(1, entries // 2, step, terms(0, True))
        sums = [jnp.sum(t, axis=1, keepdims=True) for t in totals]
        lane = lanes_of((width, LANES))
        pair_ref[pl.ds(base, width), :] = jnp.where(
            lane == 0, sums[0], jnp.where(lane == 1, sums[1], jnp.where(lane == 2, sums[2], 0.0))
        )
        return 0

    lax.fori_loop(0, cells, one_cell, 0)


def around(slabs, subs):
    slab, sub = lax.axis_index("slab"), lax.axis_index("sub")
    up, down = lax.rem(sub + 1, subs), lax.rem(sub + subs - 1, subs)
    turns = [lax.rem(slab + k, slabs) for k in range(slabs)]
    return slab, sub, up, down, turns


def remote(source, target, send_sem, recv_sem, device):
    return pltpu.make_async_remote_copy(
        src_ref=source,
        dst_ref=target,
        send_sem=send_sem,
        recv_sem=recv_sem,
        device_id=device,
        device_id_type=MESH,
    )


def landed(ref, sem):
    pltpu.make_async_copy(ref, ref, sem).wait()


INPUTS = (
    ["cells", "counts", "sends", "pol", "perm", "pos", "frac", "base"]
    + ["phase_t", "phase_l", "bm_t", "bm_l", "gather", "expand", "influence"]
    + ["tx_t", "tx_l", "bx_t", "bx_l", "ty_t", "ty_l", "by_t", "by_l"]
)
TWIDDLES = INPUTS[-8:]
SMEM_INPUTS = 3


class Refs:
    def __init__(self, names, refs):
        for name, ref in zip(names, refs, strict=True):
            setattr(self, name, ref)


def whole_kernel(slabs, subs, names, *refs):
    r = Refs(names, refs)
    slab, sub, up, down, turns = around(slabs, subs)
    depth, rows = r.moved.shape[0], r.moved.shape[1]
    half = slabs * subs
    middle = subs // 2
    group = 2 * subs

    def to_group(source, target, send_sem, recv_sem):
        goals = [(t, sub, slab) for t in turns[1:]] + [(t, up, slabs + slab) for t in turns]
        return [
            remote(source, target.at[slot], send_sem.at[n], recv_sem.at[slot], (to_slab, to_sub))
            for n, (to_slab, to_sub, slot) in enumerate(goals)
        ]

    def ghost_copies(it):
        goals = [(slab, up), (slab, down), (turns[1], sub), (turns[-1], sub)]
        cells, ghosts = r.cells.shape[0], r.ghosts.shape[2]
        return [
            remote(
                r.ghosts.at[it, q],
                r.tables.at[it, pl.ds(cells + q * ghosts, ghosts)],
                r.ghost_send.at[q],
                r.ghost_recv.at[it, q],
                goal,
            )
            for q, goal in enumerate(goals)
        ]

    def send_cells(it):
        own_cells(r.body, r.own_tiles)
        r.tables[it, : r.cells.shape[0]] = r.own_tiles[...]
        ghosts = r.ghosts.shape[2]
        for q in range(4):
            for slot in range(ghosts):
                r.ghosts[it, q, slot] = r.own_tiles[r.sends[0, q, slot]]
        for copy in ghost_copies(it):
            copy.start()

    def send_moments(it):
        for copy in to_group(r.own, r.mom.at[it], r.mom_send, r.mom_recv.at[it]):
            copy.start()
        r.mom[it, slab] = r.own[...]
        r.body[0:3] = r.own[0:3]
        send_cells(it)

    moves = [pltpu.make_async_copy(r.influence.at[:, i, :], r.moved.at[i], r.move.at[i]) for i in range(depth)]
    loads = [
        pltpu.make_async_copy(getattr(r, name), getattr(r, "in_" + name), r.load.at[n])
        for n, name in enumerate(TWIDDLES)
    ]
    for move in [*moves, *loads]:
        move.start()
    atoms = r.own.shape[1]
    r.own[0:3] = r.pol[...] * r.perm[...]
    r.own[3:4] = jnp.zeros((1, atoms), jnp.float32)
    r.body[3:6] = r.pos[...]
    r.body[6:8] = jnp.zeros((2, atoms), jnp.float32)
    r.still[slab, 0:3] = r.frac[...]
    r.still[slab, 3:6] = r.base[...].astype(jnp.float32)
    r.still[slab, 6:8] = jnp.zeros((2, atoms), jnp.float32)
    still_copies = to_group(r.still.at[slab], r.still, r.still_send, r.still_recv)
    for copy in still_copies:
        copy.start()
    send_moments(0)

    def plane(i):
        kz = depth * sub + i
        upper = kz >= half
        folded = jnp.where(upper, lax.rem(2 * half - kz, half), kz)
        slot = jnp.where(upper, 1, 0)
        to_slab, to_sub = lax.rem(folded, slabs), lax.div(folded, slabs)
        target = r.planes.at[slot, pl.ds(slab * rows, rows)]
        far = remote(
            r.moved.at[i], target, r.plane_send.at[i], r.plane_recv.at[slot, slab], (to_slab, to_sub)
        )
        return far, slot, jnp.logical_and(to_slab == slab, to_sub == sub)

    def here(i, slot):
        return pltpu.make_async_copy(
            r.moved.at[i], r.planes.at[slot, pl.ds(slab * rows, rows)], r.plane_recv.at[slot, slab]
        )

    for i in range(depth):
        moves[i].wait()
        far, slot, mine = plane(i)

        @pl.when(mine)
        def _():
            here(i, slot).start()

        @pl.when(jnp.logical_not(mine))
        def _():
            far.start()

    first = r.moved[0]
    r.turned[...] = jnp.concatenate([first] * (LANES // rows), axis=0).T

    def hop(n):
        return remote(
            r.turned.at[pl.ds(turns[n] * group, group)],
            r.hop.at[slab],
            r.hop_send.at[n - 1],
            r.hop_recv.at[slab],
            (turns[n], sub),
        )

    def mid(n):
        to_sub = lax.rem(middle + n, subs)
        return remote(
            r.hop.at[:, pl.ds(lax.div(to_sub, 4) * 8, 8)],
            r.mids,
            r.mid_send.at[n - 1],
            r.mid_recv,
            (slab, to_sub),
        )

    @pl.when(sub == middle)
    def _():
        for n in range(1, slabs):
            hop(n).start()
        r.hop[slab] = r.turned[pl.ds(pl.multiple_of(slab * group, group), group)]

    near_columns(r.body[...], r.near)
    phase = (r.phase_t[slab], r.phase_l[slab])

    def tables(before):
        def one(n, _):
            block = lax.rem(slab + n, slabs)
            at = block + slabs if before else block

            @pl.when(jnp.logical_or(before, n > 0))
            def _():
                landed(r.still.at[at], r.still_recv.at[at])

            tables_of(slabs, subs, r.still, block, before, phase, r.plane_t, r.plane_l, r.zhat)
            return 0

        lax.fori_loop(0, slabs, one, 0)

    tables(False)

    @pl.when(sub == middle)
    def _():
        for t in turns[1:]:
            landed(r.hop.at[t], r.hop_recv.at[t])
        for n in range(1, subs):
            mid(n).start()
        r.mids[...] = r.hop[:, (middle // 4) * 8 : (middle // 4) * 8 + 8]

    tables(True)
    for load in loads:
        load.wait()

    def exchange(send, got, part, send_sem, recv_sem):
        first, count = part_rows(part, send.shape[1] // TILES)
        rows = pl.ds(first, count)
        pltpu.make_async_copy(send.at[sub, rows], got.at[sub, rows], recv_sem.at[part]).start()

        def one(n, _):
            to_sub = lax.rem(sub + n, subs)
            remote(
                send.at[to_sub, rows], got.at[sub, rows], send_sem.at[part], recv_sem.at[part], (slab, to_sub)
            ).start()
            return 0

        lax.fori_loop(1, subs, one, 0)

    def exchanged(got, part, recv_sem):
        first, count = part_rows(part, got.shape[1] // TILES)
        landed(got.at[:, pl.ds(first, count)], recv_sem.at[part])

    def iteration(it, _):
        density(
            slabs,
            subs,
            slab,
            r.mom.at[it],
            r.plane_t,
            r.plane_l,
            r.zhat,
            r.grid,
            lambda slot: landed(r.mom.at[it, slot], r.mom_recv.at[it, slot]),
        )
        got_a, got_b = r.got_a.at[it], r.got_b.at[it]
        first_frequency(
            slabs,
            subs,
            slab,
            r.grid,
            r.in_tx_t,
            r.in_tx_l,
            r.gather,
            r.send_a,
            r.mid_rows,
            lambda part: exchange(r.send_a, got_a, part, r.a_send, r.a_recv.at[it]),
        )

        @pl.when(it == 0)
        def _():
            @pl.when(sub != middle)
            def _():
                landed(r.mids, r.mid_recv)

            for slot in range(2):
                for source in range(slabs):
                    landed(r.planes.at[slot, pl.ds(source * rows, rows)], r.plane_recv.at[slot, source])
            kernel_planes(slabs, subs, slab, sub, r.planes, r.mids, r.even, r.odd, r.mid_tile)

        cells, ghosts = r.cells.shape[0], r.ghosts.shape[2]
        for q in range(4):
            landed(r.tables.at[it, pl.ds(cells + q * ghosts, ghosts)], r.ghost_recv.at[it, q])
        pair_field(r.cells, r.counts, r.tables.at[it], r.near, r.pair)
        for t in range(atoms // LANES):
            tile = r.pair[t * LANES : (t + 1) * LANES, :].T[:8]
            r.rest[:, t * LANES : (t + 1) * LANES] = tile
        r.rest[0:3] += r.perm[...]

        second(
            got_a,
            r.even,
            r.odd,
            r.mid_tile,
            r.in_ty_t,
            r.in_ty_l,
            r.in_by_t,
            r.in_by_l,
            r.send_b,
            lambda part: exchanged(got_a, part, r.a_recv.at[it]),
            lambda part: exchange(r.send_b, got_b, part, r.b_send, r.b_recv.at[it]),
        )
        sample(
            slabs,
            subs,
            slab,
            got_b,
            r.plane_t,
            r.plane_l,
            r.zhat,
            r.in_bx_t,
            r.in_bx_l,
            r.bm_t.at[slab // 2],
            r.bm_l.at[slab // 2],
            r.expand,
            r.share,
            r.field,
            r.here,
            r.lhs_t,
            r.lhs_l,
            lambda part: exchanged(got_b, part, r.b_recv.at[it]),
        )
        goals = [(t, sub, t, slab) for t in turns[1:]] + [(t, down, slabs + t, slabs + slab) for t in turns]
        shares = [
            remote(
                r.share.at[source],
                r.land.at[it, slot],
                r.share_send.at[n],
                r.share_recv.at[it, slot],
                (to_slab, to_sub),
            )
            for n, (to_slab, to_sub, source, slot) in enumerate(goals)
        ]
        for copy in shares:
            copy.start()
        total = r.rest[0:3] + r.share[slab, 0:3]
        for slot in [*turns[1:], *(slabs + k for k in range(slabs))]:
            landed(r.land.at[it, slot], r.share_recv.at[it, slot])
            total = total + r.land[it, slot, 0:3]
        for copy in to_group(r.own, r.mom.at[it], r.mom_send, r.mom_recv.at[it]):
            copy.wait_send()
        for copy in ghost_copies(it):
            copy.wait_send()
        r.own[0:3] = r.pol[...] * total

        @pl.when(it + 1 < ITERS)
        def _():
            send_moments(it + 1)

        for copy in shares:
            copy.wait_send()
        for part in range(2):
            rows_sent = pl.ds(*part_rows(part, r.send_a.shape[1] // TILES))
            landed(r.send_a.at[pl.ds(0, subs - 1), rows_sent], r.a_send.at[part])
            landed(r.send_b.at[pl.ds(0, subs - 1), rows_sent], r.b_send.at[part])
        return 0

    lax.fori_loop(0, ITERS, iteration, 0)
    r.out[...] = r.own[0:3]
    for copy in still_copies:
        copy.wait_send()

    @pl.when(sub == middle)
    def _():
        for n in range(1, slabs):
            hop(n).wait_send()
        for n in range(1, subs):
            mid(n).wait_send()

    for i in range(depth):
        far, slot, mine = plane(i)

        @pl.when(jnp.logical_not(mine))
        def _():
            far.wait_send()


def shards(
    positions,
    fraction,
    grid_base,
    polarizability,
    perm_field,
    influence,
    neighbour_cells,
    neighbour_count,
    send_cells,
):
    atoms = positions.shape[1]
    cells = neighbour_cells.shape[0]
    ghosts = send_cells.shape[2]
    slabs = lax.axis_size("slab")
    subs = lax.axis_size("sub")
    grid_x = G // slabs
    grid_y = G // subs
    depth = G // subs

    index = np.arange(G)
    angle = (index[:, None] * index[None, :] % G) * (2.0 * np.pi / G)
    kz_rows = np.arange(slabs)[:, None] + slabs * np.arange(subs)[None, :]
    turn = kz_rows[:, :, None] * index[None, None, :] % G * (2.0 * np.pi / G)
    ranks = 2 * subs + 8
    phase = np.zeros((slabs, ranks, G), np.float32)
    phase[:, :subs] = np.cos(turn)
    phase[:, subs : 2 * subs] = -np.sin(turn)
    phase[:, 2 * subs] = np.where(index % 2 == 0, 1.0, -1.0)
    cos_np, sin_np = np.cos(angle), np.sin(angle)
    halves = np.concatenate([index[:LANES], G + index[:LANES], index[LANES:], G + index[LANES:]])
    turn_x = parts_of(np.block([[cos_np, -sin_np], [sin_np, cos_np]])[:, halves])
    back_x = parts_of(np.block([[cos_np, sin_np], [-sin_np, cos_np]])[halves])
    turn_y = parts_of(np.concatenate([cos_np, sin_np], axis=1))
    back_y = parts_of(np.concatenate([cos_np, -sin_np], axis=1))
    wide = np.stack(
        [np.concatenate([cos_np[w : w + LANES], -sin_np[w : w + LANES]], axis=0) for w in range(0, G, LANES)]
    )
    phase, back_mid = parts_of(phase), parts_of(wide)
    select = np.zeros((4, LANES, LANES), np.float32)
    for q in range(4):
        for lane in range(LANES):
            select[q, lane, 2 + 2 * q + lane % 2] = 1.0
    gather = jnp.asarray(select.reshape(4 * LANES, LANES), jnp.bfloat16)
    expand = jnp.asarray(np.concatenate(list(select.transpose(0, 2, 1)), axis=1), jnp.bfloat16)

    operands = [
        neighbour_cells,
        neighbour_count,
        send_cells,
        polarizability[None, :],
        perm_field,
        positions,
        fraction,
        grid_base,
        *phase,
        *back_mid,
        gather,
        expand,
        influence,
        *turn_x,
        *back_x,
        *turn_y,
        *back_y,
    ]
    vmem = pl.BlockSpec(memory_space=pltpu.VMEM)
    smem = pl.BlockSpec(memory_space=pltpu.SMEM)
    far = len(TWIDDLES) + 1
    specs = [smem] * SMEM_INPUTS + [vmem] * (len(operands) - SMEM_INPUTS - far)
    specs += [pl.BlockSpec(memory_space=pl.ANY)] * far

    def held(*shape, dtype=jnp.float32):
        return pltpu.VMEM(shape, dtype)

    held16 = functools.partial(held, dtype=jnp.bfloat16)
    dma = pltpu.SemaphoreType.DMA
    chunk = (subs, TILES * grid_y, LANES)
    columns = 6 * subs + 16
    sends = 2 * slabs - 1
    planes = sum(plane_rows(slabs, subs))
    scratch = dict(
        mom=held(ITERS, 2 * slabs, 4, atoms),
        still=held(2 * slabs, 8, atoms),
        own=held(4, atoms),
        body=held(8, atoms),
        own_tiles=held(cells, 8, LANES),
        tables=held(ITERS, cells + 4 * ghosts, 8, LANES),
        ghosts=held(ITERS, 4, ghosts, 8, LANES),
        near=held(atoms, LANES),
        pair=held(atoms, LANES),
        rest=held(8, atoms),
        plane_t=held16(slabs, planes, atoms),
        plane_l=held16(slabs, planes, atoms),
        zhat=held(2 * slabs, ranks, atoms),
        moved=held(depth, grid_x, G),
        turned=held(G, LANES),
        hop=held(slabs, grid_x, LANES),
        planes=held(2, G, G),
        mids=held(slabs, 8, LANES),
        even=held(G, G),
        odd=held(G, G),
        mid_tile=held(G, LANES),
        grid=held(grid_y, G + 8, 256),
        mid_rows=held(4, grid_y, G),
        send_a=held(*chunk),
        got_a=held(ITERS, *chunk),
        send_b=held(*chunk),
        got_b=held(ITERS, *chunk),
        field=held(6 * G * G // LANES, LANES),
        here=held(grid_y, columns, G),
        lhs_t=held16(slabs, columns, plane_rows(slabs, subs)[0]),
        lhs_l=held16(slabs, columns, plane_rows(slabs, subs)[0]),
        share=held(2 * slabs, 4, atoms),
        land=held(ITERS, 2 * slabs, 4, atoms),
        **{
            "in_" + name: held16(*operand.shape)
            for name, operand in zip(TWIDDLES, operands[-len(TWIDDLES) :], strict=True)
        },
        load=dma((len(TWIDDLES),)),
        mom_send=dma((sends,)),
        mom_recv=dma((ITERS, 2 * slabs)),
        still_send=dma((sends,)),
        still_recv=dma((2 * slabs,)),
        ghost_send=dma((4,)),
        ghost_recv=dma((ITERS, 4)),
        move=dma((depth,)),
        plane_send=dma((depth,)),
        plane_recv=dma((2, slabs)),
        hop_send=dma((slabs - 1,)),
        hop_recv=dma((slabs,)),
        mid_send=dma((subs - 1,)),
        mid_recv=dma,
        a_send=dma((2,)),
        a_recv=dma((ITERS, 2)),
        b_send=dma((2,)),
        b_recv=dma((ITERS, 2)),
        share_send=dma((sends,)),
        share_recv=dma((ITERS, 2 * slabs)),
    )
    names = [*INPUTS, "out", *scratch]
    return pl.pallas_call(
        functools.partial(whole_kernel, slabs, subs, names),
        out_shape=jax.ShapeDtypeStruct((3, atoms), jnp.float32),
        in_specs=specs,
        out_specs=vmem,
        scratch_shapes=list(scratch.values()),
        compiler_params=pltpu.CompilerParams(vmem_limit_bytes=60 << 20, has_side_effects=True),
        name="dipoles",
    )(*operands)


def solution(mesh):
    in_specs = (
        P(None, ("slab", "sub")),
        P(None, ("slab", "sub")),
        P(None, ("slab", "sub")),
        P(("slab", "sub")),
        P(None, ("slab", "sub")),
        P("slab", "sub", None),
        P(("slab", "sub"), None),
        P(("slab", "sub")),
        P(("slab", "sub"), None, None),
    )
    out_specs = P(None, ("slab", "sub"))
    return jax.shard_map(shards, mesh=mesh, in_specs=in_specs, out_specs=out_specs, check_vma=False)
```

```python
import functools
import math

import jax
import jax.numpy as jnp
import numpy as np
from jax import lax
from jax.experimental import pallas as pl
from jax.experimental.pallas import tpu as pltpu
from jax.sharding import PartitionSpec as P

G = 256
ITERS = 2

damping = 1.0
recip_scale = 16.0
highest = lax.Precision.HIGHEST
LANES = 128
TILES = 4 * G // LANES + 1
MESH = pl.DeviceIdType.MESH


def spline_weights(fraction):
    square = fraction * fraction
    cube = square * fraction
    rest = 1.0 - fraction
    return [
        rest * rest * rest / 6.0,
        (3.0 * cube - 6.0 * square + 4.0) / 6.0,
        (-3.0 * cube + 3.0 * square + 3.0 * fraction + 1.0) / 6.0,
        cube / 6.0,
    ]


def split(x):
    top = x.astype(jnp.bfloat16)
    return top, (x - top.astype(jnp.float32)).astype(jnp.bfloat16)


def dot3(a, b, turned=False):
    dims = (((1,), (1 if turned else 0,)), ((), ()))

    def one(x, y):
        return lax.dot_general(x, y, dims, preferred_element_type=jnp.float32)

    return one(a[0], b[0]) + (one(a[1], b[0]) + one(a[0], b[1]))


def parts_of(table):
    table = np.asarray(table, np.float32)
    top = table.astype(jnp.bfloat16)
    low = (table - top.astype(np.float32)).astype(jnp.bfloat16)
    return jnp.asarray(top), jnp.asarray(low)


def lanes_of(shape):
    return lax.broadcasted_iota(jnp.int32, shape, len(shape) - 1)


def rows_of(shape):
    return lax.broadcasted_iota(jnp.int32, shape, len(shape) - 2)


def window_of(slabs):
    return G // slabs + 8


def plane_rows(slabs, subs):
    window = window_of(slabs)
    return tuple(-(-count * window // LANES) * LANES for count in (G // subs, 3))


def tables_of(slabs, subs, still_ref, block, before, phase, top_ref, low_ref, zh_ref):
    at = block + slabs if before else block
    still = still_ref[at]
    atoms = still.shape[1]

    def table(axis, length):
        offset = rows_of((length, atoms)) - still[3 + axis : 4 + axis].astype(jnp.int32)
        total = jnp.zeros(offset.shape, jnp.float32)
        for stencil, weight in enumerate(spline_weights(still[axis : 1 + axis])):
            total = jnp.where(offset == stencil, weight, total)
        return total

    along_x, along_y = table(0, window_of(slabs)), table(1, 16)
    grid_y = G // subs
    first, count = (grid_y, 3) if before else (0, grid_y)
    own, spilt = plane_rows(slabs, subs)
    start, rows = (own, spilt) if before else (0, own)
    blank = jnp.zeros((rows - count * along_x.shape[0], atoms), jnp.float32)
    plane = [along_x * along_y[first + y : first + y + 1] for y in range(count)]
    top, low = split(jnp.concatenate([*plane, blank], axis=0))
    top_ref[block, start : start + rows] = top
    low_ref[block, start : start + rows] = low
    z0 = still[5:6].astype(jnp.int32)
    chosen = (rows_of((G, atoms)) == z0).astype(jnp.float32).astype(jnp.bfloat16)
    start = jnp.dot(phase[0], chosen, preferred_element_type=jnp.float32) + jnp.dot(
        phase[1], chosen, preferred_element_type=jnp.float32
    )
    steps = phase[0][:, :LANES].astype(jnp.float32) + phase[1][:, :LANES].astype(jnp.float32)
    wide = [jnp.zeros((subs, atoms), jnp.float32)] * 2
    mid = jnp.zeros((1, atoms), jnp.float32)
    for t, weight in enumerate(spline_weights(still[2:3])):
        wide = [v + weight * steps[n * subs : (n + 1) * subs, t : t + 1] for n, v in enumerate(wide)]
        mid = mid + (weight if t % 2 == 0 else -weight)
    re, im = start[:subs], start[subs : 2 * subs]
    zh_ref[at, :subs] = re * wide[0] - im * wide[1]
    zh_ref[at, subs : 2 * subs] = re * wide[1] + im * wide[0]
    zh_ref[at, 2 * subs :] = start[2 * subs :] * mid


def frequency_rows(kind):
    k = lanes_of((1, G))
    signed = jnp.where(k < G // 2, k, k - G).astype(jnp.float32)
    if kind == "odd":
        return jnp.where(k == G // 2, 0.0, signed)
    if kind == "even":
        return jnp.where(k == G // 2, signed, 0.0)
    return signed


def frequency_columns(kind):
    k = lax.broadcasted_iota(jnp.int32, (G, 1), 0)
    signed = jnp.where(k < G // 2, k, k - G).astype(jnp.float32)
    if kind == "odd":
        return jnp.where(k == G // 2, 0.0, signed)
    if kind == "even":
        return jnp.where(k == G // 2, signed, 0.0)
    return signed


def density(slabs, subs, slab, mom_ref, top_ref, low_ref, zh_ref, grid_ref, wait_block):
    grid_y = G // subs
    grid_x = G // slabs
    window = window_of(slabs)
    own, _ = plane_rows(slabs, subs)
    grid_ref[...] = jnp.zeros_like(grid_ref)

    for part in range(2):

        def one(n, _):
            block = lax.rem(slab + n, slabs)
            at = block + part * slabs
            if part == 0:

                @pl.when(n > 0)
                def _():
                    wait_block(at)

            else:
                wait_block(at)
            mu = mom_ref[at]
            zh = zh_ref[at]
            row = rows_of((8, mu.shape[1]))
            last = jnp.where(row == 0, mu[0:1], jnp.where(row == 1, mu[1:2], mu[2:3]))
            values = jnp.concatenate(
                [zh[: 2 * subs] * mu[c : c + 1] for c in range(3)] + [last * zh[2 * subs : 2 * subs + 1]], axis=0
            )
            start, count = (0, grid_y) if part == 0 else (own, 3)
            rows = -(-count * window // 16) * 16
            plane = tuple(ref[block, start : start + rows] for ref in (top_ref, low_ref))
            got = dot3(plane, split(values), True)
            columns = values.shape[0]
            for y in range(count):
                where = pl.ds(pl.multiple_of(block * grid_x, grid_x), window)
                grid_ref[y, where, :columns] += got[y * window : (y + 1) * window]
            return 0

        lax.fori_loop(0, slabs, one, 0)
    for y in range(grid_y):
        grid_ref[y, :8] += grid_ref[y, G : G + 8]


def half_of(row, part):
    return row[:, part * LANES : (part + 1) * LANES]


def first_frequency(slabs, subs, slab, grid_ref, wt_ref, wl_ref, sel_ref, out_ref, mid_ref, send_part):
    grid_y = G // subs
    half = G // 2
    flat_ref = out_ref.reshape(subs * TILES * grid_y, LANES)
    rows = []
    for y in range(grid_y):
        turned = grid_ref[y, :G].T
        for c in range(3):
            base = 2 * subs * c
            rows.append(
                jnp.concatenate([turned[base : base + subs], turned[base + subs : base + 2 * subs]], axis=1)
            )
        mids = turned[6 * subs : 6 * subs + 8]
        rows.append(jnp.concatenate([mids, jnp.zeros_like(mids)], axis=1))
    lhs = split(jnp.concatenate(rows, axis=0))
    odd, signed = frequency_rows("odd"), frequency_rows("signed")
    kz = (slabs * lax.broadcasted_iota(jnp.int32, (subs, 1), 0) + slab).astype(jnp.float32)
    lane = lanes_of((subs, LANES))
    per_y = 3 * subs + 8

    def transformed(part):
        columns = slice(part * 2 * LANES, (part + 1) * 2 * LANES)
        spec = dot3(lhs, (wt_ref[:, columns], wl_ref[:, columns]))
        for y in range(grid_y):
            at = spec[y * per_y : (y + 1) * per_y]
            sx, sy, sz = (at[c * subs : (c + 1) * subs] for c in range(3))
            tiles = [
                half_of(odd, part) * half_of(sx, n) + kz * half_of(sz, n) for n in range(2)
            ] + [half_of(sy, 0), half_of(sy, 1)]
            if part == 1:
                tiles.append(
                    -float(half) * jnp.where(lane == 0, sx[:, :1], jnp.where(lane == 1, sx[:, LANES : LANES + 1], 0.0))
                )
            for t, value in enumerate(tiles):
                flat_ref[pl.ds((part * 4 + t) * grid_y + y, subs, stride=TILES * grid_y), :] = value
            mid = at[3 * subs :]
            lanes = slice(part * LANES, (part + 1) * LANES)
            for n in range(2):
                mx, my, mz = (half_of(mid[c : c + 1], n) for c in range(3))
                mid_ref[n, y : y + 1, lanes] = half_of(signed, part) * mx - float(half) * mz
                mid_ref[2 + n, y : y + 1, lanes] = my

    transformed(0)
    send_part(0)
    transformed(1)
    window = pl.ds(pl.multiple_of(slab // 2 * LANES, LANES), LANES)
    pair = (lanes_of((grid_y, LANES)) - lax.rem(slab, 2) * (2 * subs)) >> 1
    columns = []
    for q in range(4):
        value = mid_ref[q, :, window]
        columns.append(jnp.concatenate([jnp.where(pair == j, value, 0.0) for j in range(subs)], axis=0))
    top, low = split(jnp.concatenate(columns, axis=1))
    sel = sel_ref[...]
    more = jnp.dot(top, sel, preferred_element_type=jnp.float32) + jnp.dot(
        low, sel, preferred_element_type=jnp.float32
    )
    out_ref[:, (TILES - 1) * grid_y :, :] += more.reshape(subs, grid_y, LANES)
    send_part(1)


def part_rows(part, high):
    return (0, 4 * high) if part == 0 else (4 * high, (TILES - 4) * high)


def from_tiles(ref, part):
    blocks, rows, lanes = ref.shape
    high = rows // TILES
    first, count = part_rows(part, high)
    return jnp.concatenate(
        [ref[:, r : r + high, :].reshape(blocks * high, lanes) for r in range(first, first + count, high)], axis=1
    )


def to_tiles(value, ref, part):
    blocks, rows, lanes = ref.shape
    high = rows // TILES
    first, count = part_rows(part, high)
    for t in range(count // high):
        ref[:, first + t * high : first + (t + 1) * high, :] = value[:, t * lanes : (t + 1) * lanes].reshape(
            blocks, high, lanes
        )


def with_swapped(x):
    def tile(v, t):
        return v[:, t * LANES : (t + 1) * LANES]

    both = [
        jnp.concatenate([v, jnp.concatenate([tile(v, 1), -tile(v, 0), tile(v, 3), -tile(v, 2)], axis=1)], axis=0)
        for v in split(x[:, : 4 * LANES])
    ]
    if x.shape[1] > 4 * LANES:
        last = x[:, 4 * LANES :]
        lane = lanes_of(last.shape)
        back, on = pltpu.roll(last, LANES - 1, 1), pltpu.roll(last, 1, 1)
        back2, on2 = pltpu.roll(last, LANES - 2, 1), pltpu.roll(last, 2, 1)
        upper = ((lane - 2) & 2) == 0
        turned = jnp.where(lane == 0, back, jnp.where(lane == 1, -on, jnp.where(upper, back2, -on2)))
        more = split(jnp.concatenate([last, turned], axis=0))
        both = [jnp.concatenate([a, b], axis=1) for a, b in zip(both, more)]
    return tuple(both)


def second(got_ref, even_ref, odd_ref, mid_ref, ft_ref, fl_ref, bt_ref, bl_ref, out_ref, wait_part, send_part):
    forward, backward = (ft_ref[...], fl_ref[...]), (bt_ref[...], bl_ref[...])
    odd_y, even_y, full_y = (frequency_columns(k) for k in ("odd", "even", "signed"))
    for part in range(2):
        wait_part(part)
        spec = dot3(forward, with_swapped(from_tiles(got_ref, part)))
        lanes = slice(part * LANES, (part + 1) * LANES)
        kernel_even, kernel_odd = even_ref[:, lanes], odd_ref[:, lanes]
        lane = lanes_of(kernel_even.shape)
        last = spec[:, 4 * LANES :]
        tiles, columns = [None] * 4, []
        for n in range(2):
            a = spec[:, n * LANES : (n + 1) * LANES]
            b = spec[:, (2 + n) * LANES : (3 + n) * LANES]
            level = a + odd_y * b
            edge = even_y * b
            if part == 1:
                edge = edge + jnp.where(lane == 0, last[:, n : n + 1], 0.0)
            phi = kernel_even * level + kernel_odd * edge
            phi_edge = kernel_odd * level + kernel_even * edge
            tiles[n] = phi
            tiles[2 + n] = odd_y * phi + even_y * phi_edge
            columns.append(phi_edge[:, :1])
        if part == 1:
            mid = mid_ref[...] * (last + full_y * pltpu.roll(last, LANES - 4, 1))
            mid = mid + full_y * pltpu.roll(mid, 4, 1)
            tiles.append(jnp.where(lane == 0, columns[0], jnp.where(lane == 1, columns[1], mid)))
        to_tiles(dot3(backward, with_swapped(jnp.concatenate(tiles, axis=1))), out_ref, part)
        send_part(part)


def sample(
    slabs,
    subs,
    slab,
    got_ref,
    top_ref,
    low_ref,
    zh_ref,
    wt_ref,
    wl_ref,
    mt_ref,
    ml_ref,
    sel_ref,
    out_ref,
    field_ref,
    here_ref,
    lhs_ref,
    wait_part,
    send_share,
):
    grid_y = G // subs
    grid_x = G // slabs
    half = G // 2
    window = window_of(slabs)
    own, spilt = plane_rows(slabs, subs)
    odd, even = frequency_rows("odd"), frequency_rows("even")
    kz = (slabs * (lax.broadcasted_iota(jnp.int32, (G, 1), 0) // grid_y) + slab).astype(jnp.float32)
    for part in range(2):
        wait_part(part)
        got = from_tiles(got_ref, part)
        last = got[:, 4 * LANES :]
        phi = got[:, : 2 * LANES]
        along_x = [half_of(odd, part) * half_of(phi, n) for n in range(2)]
        if part == 1:
            along_x = [v + half_of(even, part) * last[:, n : n + 1] for n, v in enumerate(along_x)]
        lhs = jnp.concatenate([jnp.concatenate(along_x, axis=1), got[:, 2 * LANES : 4 * LANES], kz * phi], axis=0)
        rows = slice(part * 2 * LANES, (part + 1) * 2 * LANES)
        field = dot3(split(lhs), (wt_ref[rows], wl_ref[rows]))
        for t in range(2 * G // LANES):
            where = pl.ds(3 * t * G, 3 * G)
            value = field[:, t * LANES : (t + 1) * LANES]
            field_ref[where, :] = value if part == 0 else field_ref[where, :] + value
    sel = sel_ref[...]
    top, low = split(last)
    expanded = jnp.dot(top, sel, preferred_element_type=jnp.float32) + jnp.dot(
        low, sel, preferred_element_type=jnp.float32
    )
    pair = ((lanes_of((grid_y, 4 * LANES)) & (LANES - 1)) - lax.rem(slab, 2) * (2 * subs)) >> 1
    mids = jnp.zeros((grid_y, 4 * LANES), jnp.float32)
    for j in range(subs):
        mids = mids + jnp.where(pair == j, expanded[j * grid_y : (j + 1) * grid_y], 0.0)
    k = slab // 2 * LANES + (lanes_of((1, 2 * LANES)) & (LANES - 1))
    signed = jnp.where(k < half, k, k - G).astype(jnp.float32)
    mid_phi = mids[:, : 2 * LANES]
    mid_lhs = jnp.concatenate([signed * mid_phi, mids[:, 2 * LANES :], -float(half) * mid_phi], axis=0)
    mid_field = dot3(split(mid_lhs), (mt_ref[...], ml_ref[...]))
    row = rows_of((8, G))
    for y in range(grid_y):
        rows = []
        for c in range(3):
            for part in range(2):
                tiles = [
                    field_ref[pl.ds((3 * (part * G // LANES + t) + c) * G + y, subs, stride=grid_y), :]
                    for t in range(G // LANES)
                ]
                rows.append(jnp.concatenate(tiles, axis=1))
        mid = jnp.zeros((8, G), jnp.float32)
        for c in range(3):
            mid = jnp.where(row == c, mid_field[c * grid_y + y : c * grid_y + y + 1], mid)
        here_ref[y] = jnp.concatenate(rows + [mid, jnp.zeros((8, G), jnp.float32)], axis=0)
    lane = lanes_of((here_ref.shape[1], LANES))
    for block in range(slabs):
        turned = [pltpu.roll(here_ref[y], (window * y - grid_x * block) % G, 1) for y in range(grid_y)]
        tiles = []
        for t in range(own // LANES):
            value = jnp.zeros(lane.shape, jnp.float32)
            for y in range(grid_y):
                low_lane = window * y - LANES * t
                if low_lane + window <= 0 or low_lane >= LANES:
                    continue
                side = t * LANES % G
                inside = jnp.logical_and(lane >= low_lane, lane < low_lane + window)
                value = jnp.where(inside, turned[y][:, side : side + LANES], value)
            tiles.append(value)
        height = tiles[0].shape[0]
        lhs_ref[block, :height], lhs_ref[block, height:] = split(jnp.concatenate(tiles, axis=1))

    for part in (1, 0):
        start, rows = (own, spilt) if part else (0, own)

        def one(n, _):
            block = lax.rem(slab + n, slabs)
            at = part * slabs + block
            zh = zh_ref[at]
            lhs = lhs_ref[block, :, :rows]
            top, low = (ref[block, start : start + rows] for ref in (top_ref, low_ref))
            mixed = jnp.dot(lhs, top, preferred_element_type=jnp.float32)
            mixed = (mixed[:height] + mixed[height:]) + jnp.dot(
                lhs[:height], low, preferred_element_type=jnp.float32
            )
            for c in range(3):
                base = 2 * subs * c
                value = jnp.sum(mixed[base : base + 2 * subs] * zh[: 2 * subs], axis=0, keepdims=True)
                row = 6 * subs + c
                out_ref[at, c : c + 1] = value + mixed[row : row + 1] * zh[2 * subs : 2 * subs + 1]
            if part:
                send_share(part, n)
            else:

                @pl.when(n < slabs)
                def _():
                    send_share(part, n)

            return 0

        lax.fori_loop(1 - part, slabs + 1 - part, one, 0)


def kernel_planes(slabs, subs, slab, sub, planes_ref, mids_ref, even_ref, odd_ref, mid_ref):
    half = G // 2
    width_sq = G / 4.0 * (G / 4.0)
    scale = -recip_scale / (float(G) ** 3)
    flip = ((rows_of((G, G)) + lanes_of((G, G))) & (G - 1)) == 0
    flip = flip.astype(jnp.float32).astype(jnp.bfloat16)

    def product(a, b):
        return jnp.dot(a, b, preferred_element_type=jnp.float32)

    top, low = split(planes_ref[1])
    top, low = split(product(flip, top) + product(flip, low))
    mirrored = product(top, flip) + product(low, flip)
    first = planes_ref[0]
    kx, ky = frequency_rows("signed"), frequency_columns("signed")
    kz_here = slabs * sub + slab
    kz = kz_here.astype(jnp.float32)
    freq_sq = kx * kx + ky * ky + kz * kz
    anchor = freq_sq == 0.0
    gauss = jnp.where(
        anchor, 0.0, scale * jnp.exp(freq_sq * (-0.5 / width_sq)) / jnp.where(anchor, 1.0, freq_sq)
    )
    flat = kz_here == 0
    even_ref[...] = gauss * jnp.where(flat, first, first + mirrored)
    odd_ref[...] = gauss * jnp.where(flat, first, first - mirrored)
    rows = G // slabs
    tall = [
        jnp.concatenate([mids_ref[s]] * (LANES // 8), axis=0).T[:rows] for s in range(slabs)
    ]
    tall = jnp.concatenate(tall, axis=0)
    lane = lanes_of(tall.shape)
    chosen = lax.rem(2 * sub, 8)
    columns = [jnp.sum(jnp.where(lane == chosen + t, tall, 0.0), axis=1, keepdims=True) for t in range(2)]
    kx = 2 * (subs * slab + sub) + (lane & 1)
    kx = jnp.where(kx < half, kx, kx - G).astype(jnp.float32)
    mid_sq = kx * kx + ky * ky + float(half * half)
    value = jnp.where((lane & 1) == 0, columns[0], columns[1])
    value = jnp.where(jnp.logical_and(lane >= 2, lane < 6), value, 0.0)
    mid_ref[...] = value * (scale * jnp.exp(mid_sq * (-0.5 / width_sq)) / mid_sq)


def near_columns(positions, near_ref):
    for t in range(positions.shape[1] // LANES):
        tile = positions[:, t * LANES : (t + 1) * LANES]
        near_ref[t * LANES : (t + 1) * LANES, :] = jnp.concatenate([tile] * (LANES // 8), axis=0).T


def own_cells(own_ref, table_ref):
    for t in range(own_ref.shape[1] // LANES):
        tile = own_ref[:, t * LANES : (t + 1) * LANES]
        other = pltpu.roll(tile, LANES // 2, 1)
        first = lanes_of(tile.shape) < LANES // 2
        table_ref[2 * t] = jnp.where(first, tile, other)
        table_ref[2 * t + 1] = jnp.where(first, other, tile)


def pair_field(first, last, list_ref, count_ref, table_ref, near_ref, pair_ref):
    entries = list_ref.shape[1]
    width = LANES // 2
    first_half = lanes_of((8, LANES)) < width
    is_moment = rows_of((8, LANES)) < 3
    itself = rows_of((width, LANES)) == lanes_of((width, LANES))

    def one_cell(cell, _):
        base = pl.multiple_of(cell * width, width)
        near = near_ref[pl.ds(base, width), :]
        near_x, near_y, near_z = (
            jnp.broadcast_to(near[:, 3 + a : 4 + a], (width, LANES)) for a in range(3)
        )
        count = count_ref[cell]

        def terms(pair, masked):
            one = table_ref[list_ref[cell, 2 * pair]]
            two = table_ref[list_ref[cell, 2 * pair + 1]]
            live_one = jnp.where(2 * pair < count, 1.0, 0.0)
            live_two = jnp.where(2 * pair + 1 < count, 1.0, 0.0)
            far = jnp.where(first_half, one, two)
            far = jnp.where(is_moment, far * jnp.where(first_half, live_one, live_two), far)
            mx, my, mz = far[0:1], far[1:2], far[2:3]
            dx = near_x - far[3:4]
            dy = near_y - far[4:5]
            dz = near_z - far[5:6]
            softened = dx * dx + dy * dy + dz * dz + damping
            inverse = lax.rsqrt(softened)
            square = inverse * inverse
            cube = square * inverse
            if masked:
                cube = jnp.where(itself, 0.0, cube)
            radial = (3.0 * (dx * mx + dy * my + dz * mz)) * (cube * square)
            return radial * dx - cube * mx, radial * dy - cube * my, radial * dz - cube * mz

        def step(pair, totals):
            return tuple(t + a for t, a in zip(totals, terms(pair, False)))

        totals = lax.fori_loop(1, entries // 2, step, terms(0, True))
        sums = [jnp.sum(t, axis=1, keepdims=True) for t in totals]
        lane = lanes_of((width, LANES))
        pair_ref[pl.ds(base, width), :] = jnp.where(
            lane == 0, sums[0], jnp.where(lane == 1, sums[1], jnp.where(lane == 2, sums[2], 0.0))
        )
        return 0

    lax.fori_loop(first, last, one_cell, 0)


def around(slabs, subs):
    slab, sub = lax.axis_index("slab"), lax.axis_index("sub")
    up, down = lax.rem(sub + 1, subs), lax.rem(sub + subs - 1, subs)
    turns = [lax.rem(slab + k, slabs) for k in range(slabs)]
    return slab, sub, up, down, turns


def remote(source, target, send_sem, recv_sem, device):
    return pltpu.make_async_remote_copy(
        src_ref=source,
        dst_ref=target,
        send_sem=send_sem,
        recv_sem=recv_sem,
        device_id=device,
        device_id_type=MESH,
    )


def landed(ref, sem):
    pltpu.make_async_copy(ref, ref, sem).wait()


INPUTS = (
    ["cells", "counts", "sends", "pol", "perm", "pos", "frac", "base"]
    + ["phase_t", "phase_l", "bm_t", "bm_l", "gather", "expand", "influence"]
    + ["tx_t", "tx_l", "bx_t", "bx_l", "ty_t", "ty_l", "by_t", "by_l"]
)
TWIDDLES = INPUTS[-8:]
SMEM_INPUTS = 3


class Refs:
    def __init__(self, names, refs):
        for name, ref in zip(names, refs, strict=True):
            setattr(self, name, ref)


def whole_kernel(slabs, subs, names, *refs):
    r = Refs(names, refs)
    slab, sub, up, down, turns = around(slabs, subs)
    depth, rows = r.moved.shape[0], r.moved.shape[1]
    half = slabs * subs
    middle = subs // 2
    group = 2 * subs

    def to_group(source, target, send_sem, recv_sem):
        goals = [(t, sub, slab) for t in turns[1:]] + [(t, up, slabs + slab) for t in turns]
        return [
            remote(source, target.at[slot], send_sem.at[n], recv_sem.at[slot], (to_slab, to_sub))
            for n, (to_slab, to_sub, slot) in enumerate(goals)
        ]

    def ghost_copies(it):
        goals = [(slab, up), (slab, down), (turns[1], sub), (turns[-1], sub)]
        ghosts = r.ghosts.shape[2]
        return [
            remote(
                r.ghosts.at[it, q],
                r.landing.at[it, pl.ds(q * ghosts, ghosts)],
                r.ghost_send.at[q],
                r.ghost_recv.at[it, q],
                goal,
            )
            for q, goal in enumerate(goals)
        ]

    def send_cells(it):
        own_cells(r.body, r.own_tiles)
        r.tables[: r.cells.shape[0]] = r.own_tiles[...]
        ghosts = r.ghosts.shape[2]
        for q in range(4):
            for slot in range(ghosts):
                r.ghosts[it, q, slot] = r.own_tiles[r.sends[0, q, slot]]
        for copy in ghost_copies(it):
            copy.start()

    def send_moments(it):
        for copy in to_group(r.own, r.mom.at[it], r.mom_send, r.mom_recv.at[it]):
            copy.start()
        r.mom[it, slab] = r.own[...]
        r.body[0:3] = r.own[0:3]
        send_cells(it)

    moves = [pltpu.make_async_copy(r.influence.at[:, i, :], r.moved.at[i], r.move.at[i]) for i in range(depth)]
    loads = [
        pltpu.make_async_copy(getattr(r, name), getattr(r, "in_" + name), r.load.at[n])
        for n, name in enumerate(TWIDDLES)
    ]
    for move in [*moves, *loads]:
        move.start()
    atoms = r.own.shape[1]
    r.own[0:3] = r.pol[...] * r.perm[...]
    r.own[3:4] = jnp.zeros((1, atoms), jnp.float32)
    r.body[3:6] = r.pos[...]
    r.body[6:8] = jnp.zeros((2, atoms), jnp.float32)
    r.still[slab, 0:3] = r.frac[...]
    r.still[slab, 3:6] = r.base[...].astype(jnp.float32)
    r.still[slab, 6:8] = jnp.zeros((2, atoms), jnp.float32)
    still_copies = to_group(r.still.at[slab], r.still, r.still_send, r.still_recv)
    for copy in still_copies:
        copy.start()
    send_moments(0)

    def plane(i):
        kz = depth * sub + i
        upper = kz >= half
        folded = jnp.where(upper, lax.rem(2 * half - kz, half), kz)
        slot = jnp.where(upper, 1, 0)
        to_slab, to_sub = lax.rem(folded, slabs), lax.div(folded, slabs)
        target = r.planes.at[slot, pl.ds(slab * rows, rows)]
        far = remote(
            r.moved.at[i], target, r.plane_send.at[i], r.plane_recv.at[slot, slab], (to_slab, to_sub)
        )
        return far, slot, jnp.logical_and(to_slab == slab, to_sub == sub)

    def here(i, slot):
        return pltpu.make_async_copy(
            r.moved.at[i], r.planes.at[slot, pl.ds(slab * rows, rows)], r.plane_recv.at[slot, slab]
        )

    for i in range(depth):
        moves[i].wait()
        far, slot, mine = plane(i)

        @pl.when(mine)
        def _():
            here(i, slot).start()

        @pl.when(jnp.logical_not(mine))
        def _():
            far.start()

    first = r.moved[0]
    r.turned[...] = jnp.concatenate([first] * (LANES // rows), axis=0).T

    def hop(n):
        return remote(
            r.turned.at[pl.ds(turns[n] * group, group)],
            r.hop.at[slab],
            r.hop_send.at[n - 1],
            r.hop_recv.at[slab],
            (turns[n], sub),
        )

    def mid(n):
        to_sub = lax.rem(middle + n, subs)
        return remote(
            r.hop.at[:, pl.ds(lax.div(to_sub, 4) * 8, 8)],
            r.mids,
            r.mid_send.at[n - 1],
            r.mid_recv,
            (slab, to_sub),
        )

    @pl.when(sub == middle)
    def _():
        for n in range(1, slabs):
            hop(n).start()
        r.hop[slab] = r.turned[pl.ds(pl.multiple_of(slab * group, group), group)]

    near_columns(r.body[...], r.near)
    phase = (r.phase_t[slab], r.phase_l[slab])

    def tables(before):
        def one(n, _):
            block = lax.rem(slab + n, slabs)
            at = block + slabs if before else block

            @pl.when(jnp.logical_or(before, n > 0))
            def _():
                landed(r.still.at[at], r.still_recv.at[at])

            tables_of(slabs, subs, r.still, block, before, phase, r.plane_t, r.plane_l, r.zhat)
            return 0

        lax.fori_loop(0, slabs, one, 0)

    tables(False)

    @pl.when(sub == middle)
    def _():
        for t in turns[1:]:
            landed(r.hop.at[t], r.hop_recv.at[t])
        for n in range(1, subs):
            mid(n).start()
        r.mids[...] = r.hop[:, (middle // 4) * 8 : (middle // 4) * 8 + 8]

    tables(True)
    for load in loads:
        load.wait()

    def exchange(send, got, part, send_sem, recv_sem):
        first, count = part_rows(part, send.shape[1] // TILES)
        rows = pl.ds(first, count)
        pltpu.make_async_copy(send.at[sub, rows], got.at[sub, rows], recv_sem.at[part]).start()

        def one(n, _):
            to_sub = lax.rem(sub + n, subs)
            remote(
                send.at[to_sub, rows], got.at[sub, rows], send_sem.at[part], recv_sem.at[part], (slab, to_sub)
            ).start()
            return 0

        lax.fori_loop(1, subs, one, 0)

    def exchanged(got, part, recv_sem):
        first, count = part_rows(part, got.shape[1] // TILES)
        landed(got.at[:, pl.ds(first, count)], recv_sem.at[part])

    def iteration(it, _):
        density(
            slabs,
            subs,
            slab,
            r.mom.at[it],
            r.plane_t,
            r.plane_l,
            r.zhat,
            r.grid,
            lambda slot: landed(r.mom.at[it, slot], r.mom_recv.at[it, slot]),
        )
        got_a, got_b = r.got_a.at[it], r.got_b.at[it]
        first_frequency(
            slabs,
            subs,
            slab,
            r.grid,
            r.in_tx_t,
            r.in_tx_l,
            r.gather,
            r.send_a,
            r.mid_rows,
            lambda part: exchange(r.send_a, got_a, part, r.a_send, r.a_recv.at[it]),
        )

        @pl.when(it == 0)
        def _():
            @pl.when(sub != middle)
            def _():
                landed(r.mids, r.mid_recv)

            for slot in range(2):
                for source in range(slabs):
                    landed(r.planes.at[slot, pl.ds(source * rows, rows)], r.plane_recv.at[slot, source])
            kernel_planes(slabs, subs, slab, sub, r.planes, r.mids, r.even, r.odd, r.mid_tile)

        cells, ghosts = r.cells.shape[0], r.ghosts.shape[2]
        for q in range(4):
            landed(r.landing.at[it, pl.ds(q * ghosts, ghosts)], r.ghost_recv.at[it, q])
        r.tables[cells:] = r.landing[it]
        cuts = [0, 3 * cells // 8, 5 * cells // 8, cells]

        def pairs(step):
            pair_field(cuts[step], cuts[step + 1], r.cells, r.counts, r.tables, r.near, r.pair)

        def sent_back(part):
            exchange(r.send_b, got_b, part, r.b_send, r.b_recv.at[it])
            pairs(1 + part)

        pairs(0)

        second(
            got_a,
            r.even,
            r.odd,
            r.mid_tile,
            r.in_ty_t,
            r.in_ty_l,
            r.in_by_t,
            r.in_by_l,
            r.send_b,
            lambda part: exchanged(got_a, part, r.a_recv.at[it]),
            sent_back,
        )
        for t in range(atoms // LANES):
            tile = r.pair[t * LANES : (t + 1) * LANES, :].T[:8]
            r.rest[:, t * LANES : (t + 1) * LANES] = tile
        r.rest[0:3] += r.perm[...]

        def share_copy(part, n):
            to_slab = lax.rem(slab + n, slabs)
            slot = part * slabs + slab
            return remote(
                r.share.at[part * slabs + to_slab],
                r.land.at[it, slot],
                r.share_send.at[part * (slabs - 1) + n - 1 + part],
                r.share_recv.at[it, slot],
                (to_slab, down if part else sub),
            )

        sample(
            slabs,
            subs,
            slab,
            got_b,
            r.plane_t,
            r.plane_l,
            r.zhat,
            r.in_bx_t,
            r.in_bx_l,
            r.bm_t.at[slab // 2],
            r.bm_l.at[slab // 2],
            r.expand,
            r.share,
            r.field,
            r.here,
            r.lhs,
            lambda part: exchanged(got_b, part, r.b_recv.at[it]),
            lambda part, n: share_copy(part, n).start(),
        )
        total = r.rest[0:3] + r.share[slab, 0:3]
        for slot in [*turns[1:], *(slabs + k for k in range(slabs))]:
            landed(r.land.at[it, slot], r.share_recv.at[it, slot])
            total = total + r.land[it, slot, 0:3]
        for copy in to_group(r.own, r.mom.at[it], r.mom_send, r.mom_recv.at[it]):
            copy.wait_send()
        for copy in ghost_copies(it):
            copy.wait_send()
        r.own[0:3] = r.pol[...] * total

        @pl.when(it + 1 < ITERS)
        def _():
            send_moments(it + 1)

        for n in range(1, slabs):
            share_copy(0, n).wait_send()
        for n in range(slabs):
            share_copy(1, n).wait_send()
        for part in range(2):
            rows_sent = pl.ds(*part_rows(part, r.send_a.shape[1] // TILES))
            landed(r.send_a.at[pl.ds(0, subs - 1), rows_sent], r.a_send.at[part])
            landed(r.send_b.at[pl.ds(0, subs - 1), rows_sent], r.b_send.at[part])
        return 0

    lax.fori_loop(0, ITERS, iteration, 0)
    r.out[...] = r.own[0:3]
    for copy in still_copies:
        copy.wait_send()

    @pl.when(sub == middle)
    def _():
        for n in range(1, slabs):
            hop(n).wait_send()
        for n in range(1, subs):
            mid(n).wait_send()

    for i in range(depth):
        far, slot, mine = plane(i)

        @pl.when(jnp.logical_not(mine))
        def _():
            far.wait_send()


def shards(
    positions,
    fraction,
    grid_base,
    polarizability,
    perm_field,
    influence,
    neighbour_cells,
    neighbour_count,
    send_cells,
):
    atoms = positions.shape[1]
    cells = neighbour_cells.shape[0]
    ghosts = send_cells.shape[2]
    slabs = lax.axis_size("slab")
    subs = lax.axis_size("sub")
    grid_x = G // slabs
    grid_y = G // subs
    depth = G // subs

    index = np.arange(G)
    angle = (index[:, None] * index[None, :] % G) * (2.0 * np.pi / G)
    kz_rows = np.arange(slabs)[:, None] + slabs * np.arange(subs)[None, :]
    turn = kz_rows[:, :, None] * index[None, None, :] % G * (2.0 * np.pi / G)
    ranks = 2 * subs + 8
    phase = np.zeros((slabs, ranks, G), np.float32)
    phase[:, :subs] = np.cos(turn)
    phase[:, subs : 2 * subs] = -np.sin(turn)
    phase[:, 2 * subs] = np.where(index % 2 == 0, 1.0, -1.0)
    cos_np, sin_np = np.cos(angle), np.sin(angle)
    halves = np.concatenate([index[:LANES], G + index[:LANES], index[LANES:], G + index[LANES:]])
    turn_x = parts_of(np.block([[cos_np, -sin_np], [sin_np, cos_np]])[:, halves])
    back_x = parts_of(np.block([[cos_np, sin_np], [-sin_np, cos_np]])[halves])
    turn_y = parts_of(np.concatenate([cos_np, sin_np], axis=1))
    back_y = parts_of(np.concatenate([cos_np, -sin_np], axis=1))
    wide = np.stack(
        [np.concatenate([cos_np[w : w + LANES], -sin_np[w : w + LANES]], axis=0) for w in range(0, G, LANES)]
    )
    phase, back_mid = parts_of(phase), parts_of(wide)
    select = np.zeros((4, LANES, LANES), np.float32)
    for q in range(4):
        for lane in range(LANES):
            select[q, lane, 2 + 2 * q + lane % 2] = 1.0
    gather = jnp.asarray(select.reshape(4 * LANES, LANES), jnp.bfloat16)
    expand = jnp.asarray(np.concatenate(list(select.transpose(0, 2, 1)), axis=1), jnp.bfloat16)

    operands = [
        neighbour_cells,
        neighbour_count,
        send_cells,
        polarizability[None, :],
        perm_field,
        positions,
        fraction,
        grid_base,
        *phase,
        *back_mid,
        gather,
        expand,
        influence,
        *turn_x,
        *back_x,
        *turn_y,
        *back_y,
    ]
    vmem = pl.BlockSpec(memory_space=pltpu.VMEM)
    smem = pl.BlockSpec(memory_space=pltpu.SMEM)
    far = len(TWIDDLES) + 1
    specs = [smem] * SMEM_INPUTS + [vmem] * (len(operands) - SMEM_INPUTS - far)
    specs += [pl.BlockSpec(memory_space=pl.ANY)] * far

    def held(*shape, dtype=jnp.float32):
        return pltpu.VMEM(shape, dtype)

    held16 = functools.partial(held, dtype=jnp.bfloat16)
    dma = pltpu.SemaphoreType.DMA
    chunk = (subs, TILES * grid_y, LANES)
    columns = 6 * subs + 16
    sends = 2 * slabs - 1
    planes = sum(plane_rows(slabs, subs))
    scratch = dict(
        mom=held(ITERS, 2 * slabs, 4, atoms),
        still=held(2 * slabs, 8, atoms),
        own=held(4, atoms),
        body=held(8, atoms),
        own_tiles=held(cells, 8, LANES),
        tables=held(cells + 4 * ghosts, 8, LANES),
        landing=held(ITERS, 4 * ghosts, 8, LANES),
        ghosts=held(ITERS, 4, ghosts, 8, LANES),
        near=held(atoms, LANES),
        pair=held(atoms, LANES),
        rest=held(8, atoms),
        plane_t=held16(slabs, planes, atoms),
        plane_l=held16(slabs, planes, atoms),
        zhat=held(2 * slabs, ranks, atoms),
        moved=held(depth, grid_x, G),
        turned=held(G, LANES),
        hop=held(slabs, grid_x, LANES),
        planes=held(2, G, G),
        mids=held(slabs, 8, LANES),
        even=held(G, G),
        odd=held(G, G),
        mid_tile=held(G, LANES),
        grid=held(grid_y, G + 8, 256),
        mid_rows=held(4, grid_y, G),
        send_a=held(*chunk),
        got_a=held(ITERS, *chunk),
        send_b=held(*chunk),
        got_b=held(ITERS, *chunk),
        field=held(6 * G * G // LANES, LANES),
        here=held(grid_y, columns, G),
        lhs=held16(slabs, 2 * columns, plane_rows(slabs, subs)[0]),
        share=held(2 * slabs, 4, atoms),
        land=held(ITERS, 2 * slabs, 4, atoms),
        **{
            "in_" + name: held16(*operand.shape)
            for name, operand in zip(TWIDDLES, operands[-len(TWIDDLES) :], strict=True)
        },
        load=dma((len(TWIDDLES),)),
        mom_send=dma((sends,)),
        mom_recv=dma((ITERS, 2 * slabs)),
        still_send=dma((sends,)),
        still_recv=dma((2 * slabs,)),
        ghost_send=dma((4,)),
        ghost_recv=dma((ITERS, 4)),
        move=dma((depth,)),
        plane_send=dma((depth,)),
        plane_recv=dma((2, slabs)),
        hop_send=dma((slabs - 1,)),
        hop_recv=dma((slabs,)),
        mid_send=dma((subs - 1,)),
        mid_recv=dma,
        a_send=dma((2,)),
        a_recv=dma((ITERS, 2)),
        b_send=dma((2,)),
        b_recv=dma((ITERS, 2)),
        share_send=dma((sends,)),
        share_recv=dma((ITERS, 2 * slabs)),
    )
    names = [*INPUTS, "out", *scratch]
    return pl.pallas_call(
        functools.partial(whole_kernel, slabs, subs, names),
        out_shape=jax.ShapeDtypeStruct((3, atoms), jnp.float32),
        in_specs=specs,
        out_specs=vmem,
        scratch_shapes=list(scratch.values()),
        compiler_params=pltpu.CompilerParams(vmem_limit_bytes=60 << 20, has_side_effects=True),
        name="dipoles",
    )(*operands)


def solution(mesh):
    in_specs = (
        P(None, ("slab", "sub")),
        P(None, ("slab", "sub")),
        P(None, ("slab", "sub")),
        P(("slab", "sub")),
        P(None, ("slab", "sub")),
        P("slab", "sub", None),
        P(("slab", "sub"), None),
        P(("slab", "sub")),
        P(("slab", "sub"), None, None),
    )
    out_specs = P(None, ("slab", "sub"))
    return jax.shard_map(shards, mesh=mesh, in_specs=in_specs, out_specs=out_specs, check_vma=False)
```

```python
import functools
import math

import jax
import jax.numpy as jnp
import numpy as np
from jax import lax
from jax.experimental import pallas as pl
from jax.experimental.pallas import tpu as pltpu
from jax.sharding import PartitionSpec as P

G = 256
ITERS = 2

damping = 1.0
recip_scale = 16.0
highest = lax.Precision.HIGHEST
LANES = 128
TILES = 4 * G // LANES
MESH = pl.DeviceIdType.MESH


def spline_weights(fraction):
    square = fraction * fraction
    cube = square * fraction
    rest = 1.0 - fraction
    return [
        rest * rest * rest / 6.0,
        (3.0 * cube - 6.0 * square + 4.0) / 6.0,
        (-3.0 * cube + 3.0 * square + 3.0 * fraction + 1.0) / 6.0,
        cube / 6.0,
    ]


def split(x):
    top = x.astype(jnp.bfloat16)
    return top, (x - top.astype(jnp.float32)).astype(jnp.bfloat16)


def dot3(a, b, turned=False):
    dims = (((1,), (1 if turned else 0,)), ((), ()))

    def one(x, y):
        return lax.dot_general(x, y, dims, preferred_element_type=jnp.float32)

    return one(a[0], b[0]) + (one(a[1], b[0]) + one(a[0], b[1]))


def parts_of(table):
    table = np.asarray(table, np.float32)
    top = table.astype(jnp.bfloat16)
    low = (table - top.astype(np.float32)).astype(jnp.bfloat16)
    return jnp.asarray(top), jnp.asarray(low)


def lanes_of(shape):
    return lax.broadcasted_iota(jnp.int32, shape, len(shape) - 1)


def rows_of(shape):
    return lax.broadcasted_iota(jnp.int32, shape, len(shape) - 2)


def window_of(slabs):
    return G // slabs + 8


def plane_rows(slabs, subs):
    window = window_of(slabs)
    return tuple(-(-count * window // LANES) * LANES for count in (G // subs, 3))


def tables_of(slabs, subs, still_ref, block, before, phase, top_ref, low_ref, zh_ref):
    at = block + slabs if before else block
    still = still_ref[at]
    atoms = still.shape[1]

    def table(axis, length):
        offset = rows_of((length, atoms)) - still[3 + axis : 4 + axis].astype(jnp.int32)
        total = jnp.zeros(offset.shape, jnp.float32)
        for stencil, weight in enumerate(spline_weights(still[axis : 1 + axis])):
            total = jnp.where(offset == stencil, weight, total)
        return total

    along_x, along_y = table(0, window_of(slabs)), table(1, 16)
    grid_y = G // subs
    first, count = (grid_y, 3) if before else (0, grid_y)
    own, spilt = plane_rows(slabs, subs)
    start, rows = (own, spilt) if before else (0, own)
    blank = jnp.zeros((rows - count * along_x.shape[0], atoms), jnp.float32)
    plane = [along_x * along_y[first + y : first + y + 1] for y in range(count)]
    top, low = split(jnp.concatenate([*plane, blank], axis=0))
    top_ref[block, start : start + rows] = top
    low_ref[block, start : start + rows] = low
    z0 = still[5:6].astype(jnp.int32)
    chosen = (rows_of((G, atoms)) == z0).astype(jnp.float32).astype(jnp.bfloat16)
    start = jnp.dot(phase[0], chosen, preferred_element_type=jnp.float32) + jnp.dot(
        phase[1], chosen, preferred_element_type=jnp.float32
    )
    steps = phase[0][:, :LANES].astype(jnp.float32) + phase[1][:, :LANES].astype(jnp.float32)
    wide = [jnp.zeros((subs, atoms), jnp.float32)] * 2
    mid = jnp.zeros((1, atoms), jnp.float32)
    for t, weight in enumerate(spline_weights(still[2:3])):
        wide = [v + weight * steps[n * subs : (n + 1) * subs, t : t + 1] for n, v in enumerate(wide)]
        mid = mid + (weight if t % 2 == 0 else -weight)
    re, im = start[:subs], start[subs : 2 * subs]
    zh_ref[at, :subs] = re * wide[0] - im * wide[1]
    zh_ref[at, subs : 2 * subs] = re * wide[1] + im * wide[0]
    zh_ref[at, 2 * subs :] = start[2 * subs :] * mid


def frequency_rows(kind):
    k = lanes_of((1, G))
    signed = jnp.where(k < G // 2, k, k - G).astype(jnp.float32)
    if kind == "odd":
        return jnp.where(k == G // 2, 0.0, signed)
    if kind == "even":
        return jnp.where(k == G // 2, signed, 0.0)
    return signed


def frequency_columns(kind):
    k = lax.broadcasted_iota(jnp.int32, (G, 1), 0)
    signed = jnp.where(k < G // 2, k, k - G).astype(jnp.float32)
    if kind == "odd":
        return jnp.where(k == G // 2, 0.0, signed)
    if kind == "even":
        return jnp.where(k == G // 2, signed, 0.0)
    return signed


def density(slabs, subs, slab, mom_ref, top_ref, low_ref, zh_ref, grid_ref, wait_block):
    grid_y = G // subs
    grid_x = G // slabs
    window = window_of(slabs)
    own, _ = plane_rows(slabs, subs)
    grid_ref[...] = jnp.zeros_like(grid_ref)

    for part in range(2):

        def one(n, _):
            block = lax.rem(slab + n, slabs)
            at = block + part * slabs
            if part == 0:

                @pl.when(n > 0)
                def _():
                    wait_block(at)

            else:
                wait_block(at)
            mu = mom_ref[at]
            zh = zh_ref[at]
            row = rows_of((8, mu.shape[1]))
            last = jnp.where(row == 0, mu[0:1], jnp.where(row == 1, mu[1:2], mu[2:3]))
            values = jnp.concatenate(
                [zh[: 2 * subs] * mu[c : c + 1] for c in range(3)] + [last * zh[2 * subs : 2 * subs + 1]], axis=0
            )
            start, count = (0, grid_y) if part == 0 else (own, 3)
            rows = -(-count * window // 16) * 16
            plane = tuple(ref[block, start : start + rows] for ref in (top_ref, low_ref))
            got = dot3(plane, split(values), True)
            columns = values.shape[0]
            for y in range(count):
                where = pl.ds(pl.multiple_of(block * grid_x, grid_x), window)
                grid_ref[y, where, :columns] += got[y * window : (y + 1) * window]
            return 0

        lax.fori_loop(0, slabs, one, 0)
    for y in range(grid_y):
        grid_ref[y, :8] += grid_ref[y, G : G + 8]


def half_of(row, part):
    return row[:, part * LANES : (part + 1) * LANES]


def first_frequency(slabs, subs, slab, grid_ref, wt_ref, wl_ref, sel_ref, out_ref, few_ref, edge_ref, mid_ref, send_part):
    grid_y = G // subs
    half = G // 2
    flat_ref = out_ref.reshape(subs * TILES * grid_y, LANES)
    rows = []
    for y in range(grid_y):
        turned = grid_ref[y, :G].T
        for c in range(3):
            base = 2 * subs * c
            rows.append(
                jnp.concatenate([turned[base : base + subs], turned[base + subs : base + 2 * subs]], axis=1)
            )
        mids = turned[6 * subs : 6 * subs + 8]
        rows.append(jnp.concatenate([mids, jnp.zeros_like(mids)], axis=1))
    lhs = split(jnp.concatenate(rows, axis=0))
    odd, signed = frequency_rows("odd"), frequency_rows("signed")
    kz = (slabs * lax.broadcasted_iota(jnp.int32, (subs, 1), 0) + slab).astype(jnp.float32)
    lane = lanes_of((subs, LANES))
    per_y = 3 * subs + 8

    def transformed(part):
        columns = slice(part * 2 * LANES, (part + 1) * 2 * LANES)
        spec = dot3(lhs, (wt_ref[:, columns], wl_ref[:, columns]))
        for y in range(grid_y):
            at = spec[y * per_y : (y + 1) * per_y]
            sx, sy, sz = (at[c * subs : (c + 1) * subs] for c in range(3))
            tiles = [
                half_of(odd, part) * half_of(sx, n) + kz * half_of(sz, n) for n in range(2)
            ] + [half_of(sy, 0), half_of(sy, 1)]
            if part == 1:
                edge_ref[pl.ds(y, subs, stride=grid_y), :] = -float(half) * jnp.where(
                    lane == 0, sx[:, :1], jnp.where(lane == 1, sx[:, LANES : LANES + 1], 0.0)
                )
            for t, value in enumerate(tiles):
                flat_ref[pl.ds((part * 4 + t) * grid_y + y, subs, stride=TILES * grid_y), :] = value
            mid = at[3 * subs :]
            lanes = slice(part * LANES, (part + 1) * LANES)
            for n in range(2):
                mx, my, mz = (half_of(mid[c : c + 1], n) for c in range(3))
                mid_ref[n, y : y + 1, lanes] = half_of(signed, part) * mx - float(half) * mz
                mid_ref[2 + n, y : y + 1, lanes] = my

    transformed(0)
    send_part(0)
    transformed(1)
    window = pl.ds(pl.multiple_of(slab // 2 * LANES, LANES), LANES)
    pair = (lanes_of((grid_y, LANES)) - lax.rem(slab, 2) * (2 * subs)) >> 1
    columns = []
    for q in range(4):
        value = mid_ref[q, :, window]
        columns.append(jnp.concatenate([jnp.where(pair == j, value, 0.0) for j in range(subs)], axis=0))
    top, low = split(jnp.concatenate(columns, axis=1))
    sel = sel_ref[...]
    more = jnp.dot(top, sel, preferred_element_type=jnp.float32) + jnp.dot(
        low, sel, preferred_element_type=jnp.float32
    )
    pack_columns(edge_ref[...] + more, few_ref)
    send_part(1)


def part_rows(part, high):
    return part * 4 * high, 4 * high


def pack_columns(value, ref):
    spread = pltpu.roll(value, 0, 1, stride=LANES // 8, stride_axis=0)
    rows = jnp.sum(spread.reshape(ref.shape[0], 8, LANES), axis=1)
    for block in range(ref.shape[0]):
        ref[block] = rows[block : block + 1]


def unpack_columns(ref):
    rows = jnp.concatenate([jnp.broadcast_to(ref[block], (8, LANES)) for block in range(ref.shape[0])], axis=0)
    y = rows_of(rows.shape) & 7
    back = rows
    for n in range(1, 8):
        back = jnp.where(y == n, pltpu.roll(rows, LANES - n * (LANES // 8), 1), back)
    return jnp.where(lanes_of(back.shape) < LANES // 8, back, 0.0)


def from_tiles(ref, part):
    blocks, rows, lanes = ref.shape
    high = rows // TILES
    first, count = part_rows(part, high)
    return jnp.concatenate(
        [ref[:, r : r + high, :].reshape(blocks * high, lanes) for r in range(first, first + count, high)], axis=1
    )


def to_tiles(value, ref, part):
    blocks, rows, lanes = ref.shape
    high = rows // TILES
    first, count = part_rows(part, high)
    for t in range(count // high):
        ref[:, first + t * high : first + (t + 1) * high, :] = value[:, t * lanes : (t + 1) * lanes].reshape(
            blocks, high, lanes
        )


def with_swapped(x):
    def tile(v, t):
        return v[:, t * LANES : (t + 1) * LANES]

    both = [
        jnp.concatenate([v, jnp.concatenate([tile(v, 1), -tile(v, 0), tile(v, 3), -tile(v, 2)], axis=1)], axis=0)
        for v in split(x[:, : 4 * LANES])
    ]
    if x.shape[1] > 4 * LANES:
        last = x[:, 4 * LANES :]
        lane = lanes_of(last.shape)
        back, on = pltpu.roll(last, LANES - 1, 1), pltpu.roll(last, 1, 1)
        back2, on2 = pltpu.roll(last, LANES - 2, 1), pltpu.roll(last, 2, 1)
        upper = ((lane - 2) & 2) == 0
        turned = jnp.where(lane == 0, back, jnp.where(lane == 1, -on, jnp.where(upper, back2, -on2)))
        more = split(jnp.concatenate([last, turned], axis=0))
        both = [jnp.concatenate([a, b], axis=1) for a, b in zip(both, more)]
    return tuple(both)


def second(got_ref, few_ref, even_ref, odd_ref, mid_ref, ft_ref, fl_ref, bt_ref, bl_ref, out_ref, few_out_ref, wait_part, send_part):
    forward, backward = (ft_ref[...], fl_ref[...]), (bt_ref[...], bl_ref[...])
    odd_y, even_y, full_y = (frequency_columns(k) for k in ("odd", "even", "signed"))
    for part in range(2):
        wait_part(part)
        got = from_tiles(got_ref, part)
        if part == 1:
            got = jnp.concatenate([got, unpack_columns(few_ref)], axis=1)
        spec = dot3(forward, with_swapped(got))
        lanes = slice(part * LANES, (part + 1) * LANES)
        kernel_even, kernel_odd = even_ref[:, lanes], odd_ref[:, lanes]
        lane = lanes_of(kernel_even.shape)
        last = spec[:, 4 * LANES :]
        tiles, columns = [None] * 4, []
        for n in range(2):
            a = spec[:, n * LANES : (n + 1) * LANES]
            b = spec[:, (2 + n) * LANES : (3 + n) * LANES]
            level = a + odd_y * b
            edge = even_y * b
            if part == 1:
                edge = edge + jnp.where(lane == 0, last[:, n : n + 1], 0.0)
            phi = kernel_even * level + kernel_odd * edge
            phi_edge = kernel_odd * level + kernel_even * edge
            tiles[n] = phi
            tiles[2 + n] = odd_y * phi + even_y * phi_edge
            columns.append(phi_edge[:, :1])
        if part == 1:
            mid = mid_ref[...] * (last + full_y * pltpu.roll(last, LANES - 4, 1))
            mid = mid + full_y * pltpu.roll(mid, 4, 1)
            tiles.append(jnp.where(lane == 0, columns[0], jnp.where(lane == 1, columns[1], mid)))
        back = dot3(backward, with_swapped(jnp.concatenate(tiles, axis=1)))
        to_tiles(back, out_ref, part)
        if part == 1:
            pack_columns(back[:, 4 * LANES :], few_out_ref)
        send_part(part)


def sample(
    slabs,
    subs,
    slab,
    got_ref,
    few_ref,
    top_ref,
    low_ref,
    zh_ref,
    wt_ref,
    wl_ref,
    mt_ref,
    ml_ref,
    sel_ref,
    out_ref,
    field_ref,
    here_ref,
    lhs_ref,
    wait_part,
    send_share,
):
    grid_y = G // subs
    grid_x = G // slabs
    half = G // 2
    window = window_of(slabs)
    own, spilt = plane_rows(slabs, subs)
    odd, even = frequency_rows("odd"), frequency_rows("even")
    kz = (slabs * (lax.broadcasted_iota(jnp.int32, (G, 1), 0) // grid_y) + slab).astype(jnp.float32)
    for part in range(2):
        wait_part(part)
        got = from_tiles(got_ref, part)
        phi = got[:, : 2 * LANES]
        along_x = [half_of(odd, part) * half_of(phi, n) for n in range(2)]
        if part == 1:
            last = unpack_columns(few_ref)
            along_x = [v + half_of(even, part) * last[:, n : n + 1] for n, v in enumerate(along_x)]
        lhs = jnp.concatenate([jnp.concatenate(along_x, axis=1), got[:, 2 * LANES : 4 * LANES], kz * phi], axis=0)
        rows = slice(part * 2 * LANES, (part + 1) * 2 * LANES)
        field = dot3(split(lhs), (wt_ref[rows], wl_ref[rows]))
        for t in range(2 * G // LANES):
            where = pl.ds(3 * t * G, 3 * G)
            value = field[:, t * LANES : (t + 1) * LANES]
            field_ref[where, :] = value if part == 0 else field_ref[where, :] + value
    sel = sel_ref[...]
    top, low = split(last)
    expanded = jnp.dot(top, sel, preferred_element_type=jnp.float32) + jnp.dot(
        low, sel, preferred_element_type=jnp.float32
    )
    pair = ((lanes_of((grid_y, 4 * LANES)) & (LANES - 1)) - lax.rem(slab, 2) * (2 * subs)) >> 1
    mids = jnp.zeros((grid_y, 4 * LANES), jnp.float32)
    for j in range(subs):
        mids = mids + jnp.where(pair == j, expanded[j * grid_y : (j + 1) * grid_y], 0.0)
    k = slab // 2 * LANES + (lanes_of((1, 2 * LANES)) & (LANES - 1))
    signed = jnp.where(k < half, k, k - G).astype(jnp.float32)
    mid_phi = mids[:, : 2 * LANES]
    mid_lhs = jnp.concatenate([signed * mid_phi, mids[:, 2 * LANES :], -float(half) * mid_phi], axis=0)
    mid_field = dot3(split(mid_lhs), (mt_ref[...], ml_ref[...]))
    row = rows_of((8, G))
    for y in range(grid_y):
        rows = []
        for c in range(3):
            for part in range(2):
                tiles = [
                    field_ref[pl.ds((3 * (part * G // LANES + t) + c) * G + y, subs, stride=grid_y), :]
                    for t in range(G // LANES)
                ]
                rows.append(jnp.concatenate(tiles, axis=1))
        mid = jnp.zeros((8, G), jnp.float32)
        for c in range(3):
            mid = jnp.where(row == c, mid_field[c * grid_y + y : c * grid_y + y + 1], mid)
        here_ref[y] = jnp.concatenate(rows + [mid, jnp.zeros((8, G), jnp.float32)], axis=0)
    lane = lanes_of((here_ref.shape[1], LANES))
    for block in range(slabs):
        turned = [pltpu.roll(here_ref[y], (window * y - grid_x * block) % G, 1) for y in range(grid_y)]
        tiles = []
        for t in range(own // LANES):
            value = jnp.zeros(lane.shape, jnp.float32)
            for y in range(grid_y):
                low_lane = window * y - LANES * t
                if low_lane + window <= 0 or low_lane >= LANES:
                    continue
                side = t * LANES % G
                inside = jnp.logical_and(lane >= low_lane, lane < low_lane + window)
                value = jnp.where(inside, turned[y][:, side : side + LANES], value)
            tiles.append(value)
        height = tiles[0].shape[0]
        lhs_ref[block, :height], lhs_ref[block, height:] = split(jnp.concatenate(tiles, axis=1))

    for part in (1, 0):
        start, rows = (own, spilt) if part else (0, own)

        def one(n, _):
            block = lax.rem(slab + n, slabs)
            at = part * slabs + block
            zh = zh_ref[at]
            lhs = lhs_ref[block, :, :rows]
            top, low = (ref[block, start : start + rows] for ref in (top_ref, low_ref))
            mixed = jnp.dot(lhs, top, preferred_element_type=jnp.float32)
            mixed = (mixed[:height] + mixed[height:]) + jnp.dot(
                lhs[:height], low, preferred_element_type=jnp.float32
            )
            for c in range(3):
                base = 2 * subs * c
                value = jnp.sum(mixed[base : base + 2 * subs] * zh[: 2 * subs], axis=0, keepdims=True)
                row = 6 * subs + c
                out_ref[at, c : c + 1] = value + mixed[row : row + 1] * zh[2 * subs : 2 * subs + 1]
            if part:
                send_share(part, n)
            else:

                @pl.when(n < slabs)
                def _():
                    send_share(part, n)

            return 0

        lax.fori_loop(1 - part, slabs + 1 - part, one, 0)


def kernel_planes(slabs, subs, slab, sub, planes_ref, mids_ref, even_ref, odd_ref, mid_ref):
    half = G // 2
    width_sq = G / 4.0 * (G / 4.0)
    scale = -recip_scale / (float(G) ** 3)
    flip = ((rows_of((G, G)) + lanes_of((G, G))) & (G - 1)) == 0
    flip = flip.astype(jnp.float32).astype(jnp.bfloat16)

    def product(a, b):
        return jnp.dot(a, b, preferred_element_type=jnp.float32)

    top, low = split(planes_ref[1])
    top, low = split(product(flip, top) + product(flip, low))
    mirrored = product(top, flip) + product(low, flip)
    first = planes_ref[0]
    kx, ky = frequency_rows("signed"), frequency_columns("signed")
    kz_here = slabs * sub + slab
    kz = kz_here.astype(jnp.float32)
    freq_sq = kx * kx + ky * ky + kz * kz
    anchor = freq_sq == 0.0
    gauss = jnp.where(
        anchor, 0.0, scale * jnp.exp(freq_sq * (-0.5 / width_sq)) / jnp.where(anchor, 1.0, freq_sq)
    )
    flat = kz_here == 0
    even_ref[...] = gauss * jnp.where(flat, first, first + mirrored)
    odd_ref[...] = gauss * jnp.where(flat, first, first - mirrored)
    rows = G // slabs
    tall = [
        jnp.concatenate([mids_ref[s]] * (LANES // 8), axis=0).T[:rows] for s in range(slabs)
    ]
    tall = jnp.concatenate(tall, axis=0)
    lane = lanes_of(tall.shape)
    chosen = lax.rem(2 * sub, 8)
    columns = [jnp.sum(jnp.where(lane == chosen + t, tall, 0.0), axis=1, keepdims=True) for t in range(2)]
    kx = 2 * (subs * slab + sub) + (lane & 1)
    kx = jnp.where(kx < half, kx, kx - G).astype(jnp.float32)
    mid_sq = kx * kx + ky * ky + float(half * half)
    value = jnp.where((lane & 1) == 0, columns[0], columns[1])
    value = jnp.where(jnp.logical_and(lane >= 2, lane < 6), value, 0.0)
    mid_ref[...] = value * (scale * jnp.exp(mid_sq * (-0.5 / width_sq)) / mid_sq)


def near_columns(positions, near_ref):
    for t in range(positions.shape[1] // LANES):
        tile = positions[:, t * LANES : (t + 1) * LANES]
        near_ref[t * LANES : (t + 1) * LANES, :] = jnp.concatenate([tile] * (LANES // 8), axis=0).T


def own_cells(own_ref, table_ref):
    for t in range(own_ref.shape[1] // LANES):
        tile = own_ref[:, t * LANES : (t + 1) * LANES]
        other = pltpu.roll(tile, LANES // 2, 1)
        first = lanes_of(tile.shape) < LANES // 2
        table_ref[2 * t] = jnp.where(first, tile, other)
        table_ref[2 * t + 1] = jnp.where(first, other, tile)


def pair_field(first, last, list_ref, count_ref, table_ref, near_ref, pair_ref):
    entries = list_ref.shape[1]
    width = LANES // 2
    first_half = lanes_of((8, LANES)) < width
    is_moment = rows_of((8, LANES)) < 3
    itself = rows_of((width, LANES)) == lanes_of((width, LANES))

    def one_cell(cell, _):
        base = pl.multiple_of(cell * width, width)
        near = near_ref[pl.ds(base, width), :]
        near_x, near_y, near_z = (
            jnp.broadcast_to(near[:, 3 + a : 4 + a], (width, LANES)) for a in range(3)
        )
        count = count_ref[cell]

        def terms(pair, masked):
            one = table_ref[list_ref[cell, 2 * pair]]
            two = table_ref[list_ref[cell, 2 * pair + 1]]
            live_one = jnp.where(2 * pair < count, 1.0, 0.0)
            live_two = jnp.where(2 * pair + 1 < count, 1.0, 0.0)
            far = jnp.where(first_half, one, two)
            far = jnp.where(is_moment, far * jnp.where(first_half, live_one, live_two), far)
            mx, my, mz = far[0:1], far[1:2], far[2:3]
            dx = near_x - far[3:4]
            dy = near_y - far[4:5]
            dz = near_z - far[5:6]
            softened = dx * dx + dy * dy + dz * dz + damping
            inverse = lax.rsqrt(softened)
            square = inverse * inverse
            cube = square * inverse
            if masked:
                cube = jnp.where(itself, 0.0, cube)
            radial = (3.0 * (dx * mx + dy * my + dz * mz)) * (cube * square)
            return radial * dx - cube * mx, radial * dy - cube * my, radial * dz - cube * mz

        def step(pair, totals):
            return tuple(t + a for t, a in zip(totals, terms(pair, False)))

        totals = lax.fori_loop(1, entries // 2, step, terms(0, True))
        sums = [jnp.sum(t, axis=1, keepdims=True) for t in totals]
        lane = lanes_of((width, LANES))
        pair_ref[pl.ds(base, width), :] = jnp.where(
            lane == 0, sums[0], jnp.where(lane == 1, sums[1], jnp.where(lane == 2, sums[2], 0.0))
        )
        return 0

    lax.fori_loop(first, last, one_cell, 0)


def around(slabs, subs):
    slab, sub = lax.axis_index("slab"), lax.axis_index("sub")
    up, down = lax.rem(sub + 1, subs), lax.rem(sub + subs - 1, subs)
    turns = [lax.rem(slab + k, slabs) for k in range(slabs)]
    return slab, sub, up, down, turns


def remote(source, target, send_sem, recv_sem, device):
    return pltpu.make_async_remote_copy(
        src_ref=source,
        dst_ref=target,
        send_sem=send_sem,
        recv_sem=recv_sem,
        device_id=device,
        device_id_type=MESH,
    )


def landed(ref, sem):
    pltpu.make_async_copy(ref, ref, sem).wait()


INPUTS = (
    ["cells", "counts", "sends", "pol", "perm", "pos", "frac", "base"]
    + ["phase_t", "phase_l", "bm_t", "bm_l", "gather", "expand", "influence"]
    + ["tx_t", "tx_l", "bx_t", "bx_l", "ty_t", "ty_l", "by_t", "by_l"]
)
TWIDDLES = INPUTS[-8:]
SMEM_INPUTS = 3


class Refs:
    def __init__(self, names, refs):
        for name, ref in zip(names, refs, strict=True):
            setattr(self, name, ref)


def whole_kernel(slabs, subs, names, *refs):
    r = Refs(names, refs)
    slab, sub, up, down, turns = around(slabs, subs)
    depth, rows = r.moved.shape[0], r.moved.shape[1]
    half = slabs * subs
    middle = subs // 2
    group = 2 * subs

    def to_group(source, target, send_sem, recv_sem):
        goals = [(t, sub, slab) for t in turns[1:]] + [(t, up, slabs + slab) for t in turns]
        return [
            remote(source, target.at[slot], send_sem.at[n], recv_sem.at[slot], (to_slab, to_sub))
            for n, (to_slab, to_sub, slot) in enumerate(goals)
        ]

    def ghost_copies(it):
        goals = [(slab, up), (slab, down), (turns[1], sub), (turns[-1], sub)]
        ghosts = r.ghosts.shape[2]
        return [
            remote(
                r.ghosts.at[it, q],
                r.landing.at[it, pl.ds(q * ghosts, ghosts)],
                r.ghost_send.at[q],
                r.ghost_recv.at[it, q],
                goal,
            )
            for q, goal in enumerate(goals)
        ]

    def send_cells(it):
        own_cells(r.body, r.own_tiles)
        r.tables[: r.cells.shape[0]] = r.own_tiles[...]
        ghosts = r.ghosts.shape[2]
        for q in range(4):
            for slot in range(ghosts):
                r.ghosts[it, q, slot] = r.own_tiles[r.sends[0, q, slot]]
        for copy in ghost_copies(it):
            copy.start()

    def send_moments(it):
        for copy in to_group(r.own, r.mom.at[it], r.mom_send, r.mom_recv.at[it]):
            copy.start()
        r.mom[it, slab] = r.own[...]
        r.body[0:3] = r.own[0:3]
        send_cells(it)

    moves = [
        pltpu.make_async_copy(r.influence.at[:, :, pl.ds(h * LANES, LANES)], r.raw.at[h], r.move.at[h])
        for h in range(G // LANES)
    ]
    loads = [
        pltpu.make_async_copy(getattr(r, name), getattr(r, "in_" + name), r.load.at[n])
        for n, name in enumerate(TWIDDLES)
    ]
    for move in [*moves, *loads]:
        move.start()
    atoms = r.own.shape[1]
    r.own[0:3] = r.pol[...] * r.perm[...]
    r.own[3:4] = jnp.zeros((1, atoms), jnp.float32)
    r.body[3:6] = r.pos[...]
    r.body[6:8] = jnp.zeros((2, atoms), jnp.float32)
    r.still[slab, 0:3] = r.frac[...]
    r.still[slab, 3:6] = r.base[...].astype(jnp.float32)
    r.still[slab, 6:8] = jnp.zeros((2, atoms), jnp.float32)
    still_copies = to_group(r.still.at[slab], r.still, r.still_send, r.still_recv)
    for copy in still_copies:
        copy.start()
    send_moments(0)

    def plane(i):
        kz = depth * sub + i
        upper = kz >= half
        folded = jnp.where(upper, lax.rem(2 * half - kz, half), kz)
        slot = jnp.where(upper, 1, 0)
        to_slab, to_sub = lax.rem(folded, slabs), lax.div(folded, slabs)
        target = r.planes.at[slot, pl.ds(slab * rows, rows)]
        far = remote(
            r.moved.at[i], target, r.plane_send.at[i], r.plane_recv.at[slot, slab], (to_slab, to_sub)
        )
        return far, slot, jnp.logical_and(to_slab == slab, to_sub == sub)

    def here(i, slot):
        return pltpu.make_async_copy(
            r.moved.at[i], r.planes.at[slot, pl.ds(slab * rows, rows)], r.plane_recv.at[slot, slab]
        )

    for move in moves:
        move.wait()
    raw = r.raw.reshape(G // LANES * rows * depth, LANES)
    for i in range(depth):
        for h in range(G // LANES):
            r.moved[i, :, h * LANES : (h + 1) * LANES] = raw[pl.ds(h * rows * depth + i, rows, stride=depth), :]
        far, slot, mine = plane(i)

        @pl.when(mine)
        def _():
            here(i, slot).start()

        @pl.when(jnp.logical_not(mine))
        def _():
            far.start()

    first = r.moved[0]
    r.turned[...] = jnp.concatenate([first] * (LANES // rows), axis=0).T

    def hop(n):
        return remote(
            r.turned.at[pl.ds(turns[n] * group, group)],
            r.hop.at[slab],
            r.hop_send.at[n - 1],
            r.hop_recv.at[slab],
            (turns[n], sub),
        )

    def mid(n):
        to_sub = lax.rem(middle + n, subs)
        return remote(
            r.hop.at[:, pl.ds(lax.div(to_sub, 4) * 8, 8)],
            r.mids,
            r.mid_send.at[n - 1],
            r.mid_recv,
            (slab, to_sub),
        )

    @pl.when(sub == middle)
    def _():
        for n in range(1, slabs):
            hop(n).start()
        r.hop[slab] = r.turned[pl.ds(pl.multiple_of(slab * group, group), group)]

    near_columns(r.body[...], r.near)
    phase = (r.phase_t[slab], r.phase_l[slab])

    def tables(before):
        def one(n, _):
            block = lax.rem(slab + n, slabs)
            at = block + slabs if before else block

            @pl.when(jnp.logical_or(before, n > 0))
            def _():
                landed(r.still.at[at], r.still_recv.at[at])

            tables_of(slabs, subs, r.still, block, before, phase, r.plane_t, r.plane_l, r.zhat)
            return 0

        lax.fori_loop(0, slabs, one, 0)

    tables(False)

    @pl.when(sub == middle)
    def _():
        for t in turns[1:]:
            landed(r.hop.at[t], r.hop_recv.at[t])
        for n in range(1, subs):
            mid(n).start()
        r.mids[...] = r.hop[:, (middle // 4) * 8 : (middle // 4) * 8 + 8]

    tables(True)
    for load in loads:
        load.wait()

    def exchange(send, few, got, got_few, part, send_sem, recv_sem):
        first, count = part_rows(part, send.shape[1] // TILES)
        rows = pl.ds(first, count)

        def all_to_all(sources, targets, n):
            pltpu.make_async_copy(sources(sub), targets, recv_sem.at[n]).start()

            def one(k, _):
                to_sub = lax.rem(sub + k, subs)
                remote(sources(to_sub), targets, send_sem.at[n], recv_sem.at[n], (slab, to_sub)).start()
                return 0

            lax.fori_loop(1, subs, one, 0)

        if part == 1:
            all_to_all(lambda to: few.at[to], got_few.at[sub], 2)
        all_to_all(lambda to: send.at[to, rows], got.at[sub, rows], part)

    def exchanged(got, got_few, part, recv_sem):
        first, count = part_rows(part, got.shape[1] // TILES)
        landed(got.at[:, pl.ds(first, count)], recv_sem.at[part])
        if part == 1:
            landed(got_few, recv_sem.at[2])

    def iteration(it, _):
        density(
            slabs,
            subs,
            slab,
            r.mom.at[it],
            r.plane_t,
            r.plane_l,
            r.zhat,
            r.grid,
            lambda slot: landed(r.mom.at[it, slot], r.mom_recv.at[it, slot]),
        )
        got_a, got_b = r.got_a.at[it], r.got_b.at[it]
        few_a, few_b = r.got_few_a.at[it], r.got_few_b.at[it]
        first_frequency(
            slabs,
            subs,
            slab,
            r.grid,
            r.in_tx_t,
            r.in_tx_l,
            r.gather,
            r.send_a,
            r.few_a,
            r.edge,
            r.mid_rows,
            lambda part: exchange(r.send_a, r.few_a, got_a, few_a, part, r.a_send, r.a_recv.at[it]),
        )

        @pl.when(it == 0)
        def _():
            @pl.when(sub != middle)
            def _():
                landed(r.mids, r.mid_recv)

            for slot in range(2):
                for source in range(slabs):
                    landed(r.planes.at[slot, pl.ds(source * rows, rows)], r.plane_recv.at[slot, source])
            kernel_planes(slabs, subs, slab, sub, r.planes, r.mids, r.even, r.odd, r.mid_tile)

        cells, ghosts = r.cells.shape[0], r.ghosts.shape[2]
        for q in range(4):
            landed(r.landing.at[it, pl.ds(q * ghosts, ghosts)], r.ghost_recv.at[it, q])
        r.tables[cells:] = r.landing[it]
        cuts = [0, 3 * cells // 8, 5 * cells // 8, cells]

        def pairs(step):
            pair_field(cuts[step], cuts[step + 1], r.cells, r.counts, r.tables, r.near, r.pair)

        def sent_back(part):
            exchange(r.send_b, r.few_b, got_b, few_b, part, r.b_send, r.b_recv.at[it])
            pairs(1 + part)

        pairs(0)

        second(
            got_a,
            few_a,
            r.even,
            r.odd,
            r.mid_tile,
            r.in_ty_t,
            r.in_ty_l,
            r.in_by_t,
            r.in_by_l,
            r.send_b,
            r.few_b,
            lambda part: exchanged(got_a, few_a, part, r.a_recv.at[it]),
            sent_back,
        )
        for t in range(atoms // LANES):
            tile = r.pair[t * LANES : (t + 1) * LANES, :].T[:8]
            r.rest[:, t * LANES : (t + 1) * LANES] = tile
        r.rest[0:3] += r.perm[...]

        def share_copy(part, n):
            to_slab = lax.rem(slab + n, slabs)
            slot = part * slabs + slab
            return remote(
                r.share.at[part * slabs + to_slab],
                r.land.at[it, slot],
                r.share_send.at[part * (slabs - 1) + n - 1 + part],
                r.share_recv.at[it, slot],
                (to_slab, down if part else sub),
            )

        sample(
            slabs,
            subs,
            slab,
            got_b,
            few_b,
            r.plane_t,
            r.plane_l,
            r.zhat,
            r.in_bx_t,
            r.in_bx_l,
            r.bm_t.at[slab // 2],
            r.bm_l.at[slab // 2],
            r.expand,
            r.share,
            r.field,
            r.here,
            r.lhs,
            lambda part: exchanged(got_b, few_b, part, r.b_recv.at[it]),
            lambda part, n: share_copy(part, n).start(),
        )
        total = r.rest[0:3] + r.share[slab, 0:3]
        for slot in [*turns[1:], *(slabs + k for k in range(slabs))]:
            landed(r.land.at[it, slot], r.share_recv.at[it, slot])
            total = total + r.land[it, slot, 0:3]
        for copy in to_group(r.own, r.mom.at[it], r.mom_send, r.mom_recv.at[it]):
            copy.wait_send()
        for copy in ghost_copies(it):
            copy.wait_send()
        r.own[0:3] = r.pol[...] * total

        @pl.when(it + 1 < ITERS)
        def _():
            send_moments(it + 1)

        for n in range(1, slabs):
            share_copy(0, n).wait_send()
        for n in range(slabs):
            share_copy(1, n).wait_send()
        for part in range(2):
            rows_sent = pl.ds(*part_rows(part, r.send_a.shape[1] // TILES))
            landed(r.send_a.at[pl.ds(0, subs - 1), rows_sent], r.a_send.at[part])
            landed(r.send_b.at[pl.ds(0, subs - 1), rows_sent], r.b_send.at[part])
        landed(r.few_a.at[pl.ds(0, subs - 1)], r.a_send.at[2])
        landed(r.few_b.at[pl.ds(0, subs - 1)], r.b_send.at[2])
        return 0

    lax.fori_loop(0, ITERS, iteration, 0)
    r.out[...] = r.own[0:3]
    for copy in still_copies:
        copy.wait_send()

    @pl.when(sub == middle)
    def _():
        for n in range(1, slabs):
            hop(n).wait_send()
        for n in range(1, subs):
            mid(n).wait_send()

    for i in range(depth):
        far, slot, mine = plane(i)

        @pl.when(jnp.logical_not(mine))
        def _():
            far.wait_send()


def shards(
    positions,
    fraction,
    grid_base,
    polarizability,
    perm_field,
    influence,
    neighbour_cells,
    neighbour_count,
    send_cells,
):
    atoms = positions.shape[1]
    cells = neighbour_cells.shape[0]
    ghosts = send_cells.shape[2]
    slabs = lax.axis_size("slab")
    subs = lax.axis_size("sub")
    grid_x = G // slabs
    grid_y = G // subs
    depth = G // subs

    index = np.arange(G)
    angle = (index[:, None] * index[None, :] % G) * (2.0 * np.pi / G)
    kz_rows = np.arange(slabs)[:, None] + slabs * np.arange(subs)[None, :]
    turn = kz_rows[:, :, None] * index[None, None, :] % G * (2.0 * np.pi / G)
    ranks = 2 * subs + 8
    phase = np.zeros((slabs, ranks, G), np.float32)
    phase[:, :subs] = np.cos(turn)
    phase[:, subs : 2 * subs] = -np.sin(turn)
    phase[:, 2 * subs] = np.where(index % 2 == 0, 1.0, -1.0)
    cos_np, sin_np = np.cos(angle), np.sin(angle)
    halves = np.concatenate([index[:LANES], G + index[:LANES], index[LANES:], G + index[LANES:]])
    turn_x = parts_of(np.block([[cos_np, -sin_np], [sin_np, cos_np]])[:, halves])
    back_x = parts_of(np.block([[cos_np, sin_np], [-sin_np, cos_np]])[halves])
    turn_y = parts_of(np.concatenate([cos_np, sin_np], axis=1))
    back_y = parts_of(np.concatenate([cos_np, -sin_np], axis=1))
    wide = np.stack(
        [np.concatenate([cos_np[w : w + LANES], -sin_np[w : w + LANES]], axis=0) for w in range(0, G, LANES)]
    )
    phase, back_mid = parts_of(phase), parts_of(wide)
    select = np.zeros((4, LANES, LANES), np.float32)
    for q in range(4):
        for lane in range(LANES):
            select[q, lane, 2 + 2 * q + lane % 2] = 1.0
    gather = jnp.asarray(select.reshape(4 * LANES, LANES), jnp.bfloat16)
    expand = jnp.asarray(np.concatenate(list(select.transpose(0, 2, 1)), axis=1), jnp.bfloat16)

    operands = [
        neighbour_cells,
        neighbour_count,
        send_cells,
        polarizability[None, :],
        perm_field,
        positions,
        fraction,
        grid_base,
        *phase,
        *back_mid,
        gather,
        expand,
        influence,
        *turn_x,
        *back_x,
        *turn_y,
        *back_y,
    ]
    vmem = pl.BlockSpec(memory_space=pltpu.VMEM)
    smem = pl.BlockSpec(memory_space=pltpu.SMEM)
    far = len(TWIDDLES) + 1
    specs = [smem] * SMEM_INPUTS + [vmem] * (len(operands) - SMEM_INPUTS - far)
    specs += [pl.BlockSpec(memory_space=pl.ANY)] * far

    def held(*shape, dtype=jnp.float32):
        return pltpu.VMEM(shape, dtype)

    held16 = functools.partial(held, dtype=jnp.bfloat16)
    dma = pltpu.SemaphoreType.DMA
    chunk = (subs, TILES * grid_y, LANES)
    columns = 6 * subs + 16
    sends = 2 * slabs - 1
    planes = sum(plane_rows(slabs, subs))
    scratch = dict(
        mom=held(ITERS, 2 * slabs, 4, atoms),
        still=held(2 * slabs, 8, atoms),
        own=held(4, atoms),
        body=held(8, atoms),
        own_tiles=held(cells, 8, LANES),
        tables=held(cells + 4 * ghosts, 8, LANES),
        landing=held(ITERS, 4 * ghosts, 8, LANES),
        ghosts=held(ITERS, 4, ghosts, 8, LANES),
        near=held(atoms, LANES),
        pair=held(atoms, LANES),
        rest=held(8, atoms),
        plane_t=held16(slabs, planes, atoms),
        plane_l=held16(slabs, planes, atoms),
        zhat=held(2 * slabs, ranks, atoms),
        raw=held(G // LANES, grid_x, depth, LANES),
        moved=held(depth, grid_x, G),
        turned=held(G, LANES),
        hop=held(slabs, grid_x, LANES),
        planes=held(2, G, G),
        mids=held(slabs, 8, LANES),
        even=held(G, G),
        odd=held(G, G),
        mid_tile=held(G, LANES),
        grid=held(grid_y, G + 8, 256),
        mid_rows=held(4, grid_y, G),
        send_a=held(*chunk),
        got_a=held(ITERS, *chunk),
        few_a=held(subs, 1, LANES),
        got_few_a=held(ITERS, subs, 1, LANES),
        few_b=held(subs, 1, LANES),
        got_few_b=held(ITERS, subs, 1, LANES),
        edge=held(G, LANES),
        send_b=held(*chunk),
        got_b=held(ITERS, *chunk),
        field=held(6 * G * G // LANES, LANES),
        here=held(grid_y, columns, G),
        lhs=held16(slabs, 2 * columns, plane_rows(slabs, subs)[0]),
        share=held(2 * slabs, 4, atoms),
        land=held(ITERS, 2 * slabs, 4, atoms),
        **{
            "in_" + name: held16(*operand.shape)
            for name, operand in zip(TWIDDLES, operands[-len(TWIDDLES) :], strict=True)
        },
        load=dma((len(TWIDDLES),)),
        mom_send=dma((sends,)),
        mom_recv=dma((ITERS, 2 * slabs)),
        still_send=dma((sends,)),
        still_recv=dma((2 * slabs,)),
        ghost_send=dma((4,)),
        ghost_recv=dma((ITERS, 4)),
        move=dma((G // LANES,)),
        plane_send=dma((depth,)),
        plane_recv=dma((2, slabs)),
        hop_send=dma((slabs - 1,)),
        hop_recv=dma((slabs,)),
        mid_send=dma((subs - 1,)),
        mid_recv=dma,
        a_send=dma((3,)),
        a_recv=dma((ITERS, 3)),
        b_send=dma((3,)),
        b_recv=dma((ITERS, 3)),
        share_send=dma((sends,)),
        share_recv=dma((ITERS, 2 * slabs)),
    )
    names = [*INPUTS, "out", *scratch]
    return pl.pallas_call(
        functools.partial(whole_kernel, slabs, subs, names),
        out_shape=jax.ShapeDtypeStruct((3, atoms), jnp.float32),
        in_specs=specs,
        out_specs=vmem,
        scratch_shapes=list(scratch.values()),
        compiler_params=pltpu.CompilerParams(vmem_limit_bytes=60 << 20, has_side_effects=True),
        name="dipoles",
    )(*operands)


def solution(mesh):
    in_specs = (
        P(None, ("slab", "sub")),
        P(None, ("slab", "sub")),
        P(None, ("slab", "sub")),
        P(("slab", "sub")),
        P(None, ("slab", "sub")),
        P("slab", "sub", None),
        P(("slab", "sub"), None),
        P(("slab", "sub")),
        P(("slab", "sub"), None, None),
    )
    out_specs = P(None, ("slab", "sub"))
    return jax.shard_map(shards, mesh=mesh, in_specs=in_specs, out_specs=out_specs, check_vma=False)
```

```python
import functools
import math

import jax
import jax.numpy as jnp
import numpy as np
from jax import lax
from jax.experimental import pallas as pl
from jax.experimental.pallas import tpu as pltpu
from jax.sharding import PartitionSpec as P

G = 256
ITERS = 2

damping = 1.0
recip_scale = 16.0
highest = lax.Precision.HIGHEST
LANES = 128
TILES = 4 * G // LANES
MESH = pl.DeviceIdType.MESH


def spline_weights(fraction):
    square = fraction * fraction
    cube = square * fraction
    rest = 1.0 - fraction
    return [
        rest * rest * rest / 6.0,
        (3.0 * cube - 6.0 * square + 4.0) / 6.0,
        (-3.0 * cube + 3.0 * square + 3.0 * fraction + 1.0) / 6.0,
        cube / 6.0,
    ]


def split(x):
    top = x.astype(jnp.bfloat16)
    return top, (x - top.astype(jnp.float32)).astype(jnp.bfloat16)


def dot3(a, b, turned=False):
    dims = (((1,), (1 if turned else 0,)), ((), ()))

    def one(x, y):
        return lax.dot_general(x, y, dims, preferred_element_type=jnp.float32)

    return one(a[0], b[0]) + (one(a[1], b[0]) + one(a[0], b[1]))


def parts_of(table):
    table = np.asarray(table, np.float32)
    top = table.astype(jnp.bfloat16)
    low = (table - top.astype(np.float32)).astype(jnp.bfloat16)
    return jnp.asarray(top), jnp.asarray(low)


def lanes_of(shape):
    return lax.broadcasted_iota(jnp.int32, shape, len(shape) - 1)


def rows_of(shape):
    return lax.broadcasted_iota(jnp.int32, shape, len(shape) - 2)


def window_of(slabs):
    return G // slabs + 8


def plane_rows(slabs, subs):
    window = window_of(slabs)
    return tuple(-(-count * window // LANES) * LANES for count in (G // subs, 3))


def tables_of(slabs, subs, still_ref, block, before, phase, top_ref, low_ref, zh_ref):
    at = block + slabs if before else block
    still = still_ref[at]
    atoms = still.shape[1]

    def table(axis, length):
        offset = rows_of((length, atoms)) - still[3 + axis : 4 + axis].astype(jnp.int32)
        total = jnp.zeros(offset.shape, jnp.float32)
        for stencil, weight in enumerate(spline_weights(still[axis : 1 + axis])):
            total = jnp.where(offset == stencil, weight, total)
        return total

    along_x, along_y = table(0, window_of(slabs)), table(1, 16)
    grid_y = G // subs
    first, count = (grid_y, 3) if before else (0, grid_y)
    own, spilt = plane_rows(slabs, subs)
    start, rows = (own, spilt) if before else (0, own)
    blank = jnp.zeros((rows - count * along_x.shape[0], atoms), jnp.float32)
    plane = [along_x * along_y[first + y : first + y + 1] for y in range(count)]
    top, low = split(jnp.concatenate([*plane, blank], axis=0))
    top_ref[block, start : start + rows] = top
    low_ref[block, start : start + rows] = low
    z0 = still[5:6].astype(jnp.int32)
    chosen = (rows_of((G, atoms)) == z0).astype(jnp.float32).astype(jnp.bfloat16)
    start = jnp.dot(phase[0], chosen, preferred_element_type=jnp.float32) + jnp.dot(
        phase[1], chosen, preferred_element_type=jnp.float32
    )
    steps = phase[0][:, :LANES].astype(jnp.float32) + phase[1][:, :LANES].astype(jnp.float32)
    wide = [jnp.zeros((subs, atoms), jnp.float32)] * 2
    mid = jnp.zeros((1, atoms), jnp.float32)
    for t, weight in enumerate(spline_weights(still[2:3])):
        wide = [v + weight * steps[n * subs : (n + 1) * subs, t : t + 1] for n, v in enumerate(wide)]
        mid = mid + (weight if t % 2 == 0 else -weight)
    re, im = start[:subs], start[subs : 2 * subs]
    zh_ref[at, :subs] = re * wide[0] - im * wide[1]
    zh_ref[at, subs : 2 * subs] = re * wide[1] + im * wide[0]
    zh_ref[at, 2 * subs :] = start[2 * subs :] * mid


def frequency_rows(kind):
    k = lanes_of((1, G))
    signed = jnp.where(k < G // 2, k, k - G).astype(jnp.float32)
    if kind == "odd":
        return jnp.where(k == G // 2, 0.0, signed)
    if kind == "even":
        return jnp.where(k == G // 2, signed, 0.0)
    return signed


def frequency_columns(kind):
    k = lax.broadcasted_iota(jnp.int32, (G, 1), 0)
    signed = jnp.where(k < G // 2, k, k - G).astype(jnp.float32)
    if kind == "odd":
        return jnp.where(k == G // 2, 0.0, signed)
    if kind == "even":
        return jnp.where(k == G // 2, signed, 0.0)
    return signed


def density(slabs, subs, slab, mom_ref, top_ref, low_ref, zh_ref, grid_ref, wait_block):
    grid_y = G // subs
    grid_x = G // slabs
    window = window_of(slabs)
    own, _ = plane_rows(slabs, subs)
    grid_ref[...] = jnp.zeros_like(grid_ref)

    for part in range(2):

        def one(n, _):
            block = lax.rem(slab + n, slabs)
            at = block + part * slabs
            if part == 0:

                @pl.when(n > 0)
                def _():
                    wait_block(at)

            else:
                wait_block(at)
            mu = mom_ref[at]
            zh = zh_ref[at]
            row = rows_of((8, mu.shape[1]))
            last = jnp.where(row == 0, mu[0:1], jnp.where(row == 1, mu[1:2], mu[2:3]))
            values = jnp.concatenate(
                [zh[: 2 * subs] * mu[c : c + 1] for c in range(3)] + [last * zh[2 * subs : 2 * subs + 1]], axis=0
            )
            start, count = (0, grid_y) if part == 0 else (own, 3)
            rows = -(-count * window // 16) * 16
            plane = tuple(ref[block, start : start + rows] for ref in (top_ref, low_ref))
            got = dot3(plane, split(values), True)
            columns = values.shape[0]
            for y in range(count):
                where = pl.ds(pl.multiple_of(block * grid_x, grid_x), window)
                grid_ref[y, where, :columns] += got[y * window : (y + 1) * window]
            return 0

        lax.fori_loop(0, slabs, one, 0)
    for y in range(grid_y):
        grid_ref[y, :8] += grid_ref[y, G : G + 8]


def half_of(row, part):
    return row[:, part * LANES : (part + 1) * LANES]


def first_frequency(slabs, subs, slab, grid_ref, wt_ref, wl_ref, sel_ref, out_ref, few_ref, edge_ref, mid_ref, send_part):
    grid_y = G // subs
    half = G // 2
    flat_ref = out_ref.reshape(subs * TILES * grid_y, LANES)
    rows = []
    for y in range(grid_y):
        turned = grid_ref[y, :G].T
        for c in range(3):
            base = 2 * subs * c
            rows.append(
                jnp.concatenate([turned[base : base + subs], turned[base + subs : base + 2 * subs]], axis=1)
            )
        mids = turned[6 * subs : 6 * subs + 8]
        rows.append(jnp.concatenate([mids, jnp.zeros_like(mids)], axis=1))
    lhs = split(jnp.concatenate(rows, axis=0))
    odd, signed = frequency_rows("odd"), frequency_rows("signed")
    kz = (slabs * lax.broadcasted_iota(jnp.int32, (subs, 1), 0) + slab).astype(jnp.float32)
    lane = lanes_of((subs, LANES))
    per_y = 3 * subs + 8

    def transformed(part):
        columns = slice(part * 2 * LANES, (part + 1) * 2 * LANES)
        spec = dot3(lhs, (wt_ref[:, columns], wl_ref[:, columns]))
        for y in range(grid_y):
            at = spec[y * per_y : (y + 1) * per_y]
            sx, sy, sz = (at[c * subs : (c + 1) * subs] for c in range(3))
            tiles = [
                half_of(odd, part) * half_of(sx, n) + kz * half_of(sz, n) for n in range(2)
            ] + [half_of(sy, 0), half_of(sy, 1)]
            if part == 1:
                edge_ref[pl.ds(y, subs, stride=grid_y), :] = -float(half) * jnp.where(
                    lane == 0, sx[:, :1], jnp.where(lane == 1, sx[:, LANES : LANES + 1], 0.0)
                )
            for t, value in enumerate(tiles):
                flat_ref[pl.ds((part * 4 + t) * grid_y + y, subs, stride=TILES * grid_y), :] = value
            mid = at[3 * subs :]
            lanes = slice(part * LANES, (part + 1) * LANES)
            for n in range(2):
                mx, my, mz = (half_of(mid[c : c + 1], n) for c in range(3))
                mid_ref[n, y : y + 1, lanes] = half_of(signed, part) * mx - float(half) * mz
                mid_ref[2 + n, y : y + 1, lanes] = my

    transformed(0)
    send_part(0)
    transformed(1)
    window = pl.ds(pl.multiple_of(slab // 2 * LANES, LANES), LANES)
    pair = (lanes_of((grid_y, LANES)) - lax.rem(slab, 2) * (2 * subs)) >> 1
    columns = []
    for q in range(4):
        value = mid_ref[q, :, window]
        columns.append(jnp.concatenate([jnp.where(pair == j, value, 0.0) for j in range(subs)], axis=0))
    top, low = split(jnp.concatenate(columns, axis=1))
    sel = sel_ref[...]
    more = jnp.dot(top, sel, preferred_element_type=jnp.float32) + jnp.dot(
        low, sel, preferred_element_type=jnp.float32
    )
    pack_columns(edge_ref[...] + more, few_ref)
    send_part(1)


def part_rows(part, high):
    return part * 4 * high, 4 * high


def pack_columns(value, ref):
    spread = pltpu.roll(value, 0, 1, stride=LANES // 8, stride_axis=0)
    rows = jnp.sum(spread.reshape(ref.shape[0], 8, LANES), axis=1)
    for block in range(ref.shape[0]):
        ref[block] = rows[block : block + 1]


def unpack_columns(ref):
    rows = jnp.concatenate([jnp.broadcast_to(ref[block], (8, LANES)) for block in range(ref.shape[0])], axis=0)
    y = rows_of(rows.shape) & 7
    back = rows
    for n in range(1, 8):
        back = jnp.where(y == n, pltpu.roll(rows, LANES - n * (LANES // 8), 1), back)
    return jnp.where(lanes_of(back.shape) < LANES // 8, back, 0.0)


def from_tiles(ref, part):
    blocks, rows, lanes = ref.shape
    high = rows // TILES
    first, count = part_rows(part, high)
    return jnp.concatenate(
        [ref[:, r : r + high, :].reshape(blocks * high, lanes) for r in range(first, first + count, high)], axis=1
    )


def to_tiles(value, ref, part):
    blocks, rows, lanes = ref.shape
    high = rows // TILES
    first, count = part_rows(part, high)
    for t in range(count // high):
        ref[:, first + t * high : first + (t + 1) * high, :] = value[:, t * lanes : (t + 1) * lanes].reshape(
            blocks, high, lanes
        )


def with_swapped(x):
    def tile(v, t):
        return v[:, t * LANES : (t + 1) * LANES]

    both = [
        jnp.concatenate([v, jnp.concatenate([tile(v, 1), -tile(v, 0), tile(v, 3), -tile(v, 2)], axis=1)], axis=0)
        for v in split(x[:, : 4 * LANES])
    ]
    if x.shape[1] > 4 * LANES:
        last = x[:, 4 * LANES :]
        lane = lanes_of(last.shape)
        back, on = pltpu.roll(last, LANES - 1, 1), pltpu.roll(last, 1, 1)
        back2, on2 = pltpu.roll(last, LANES - 2, 1), pltpu.roll(last, 2, 1)
        upper = ((lane - 2) & 2) == 0
        turned = jnp.where(lane == 0, back, jnp.where(lane == 1, -on, jnp.where(upper, back2, -on2)))
        more = split(jnp.concatenate([last, turned], axis=0))
        both = [jnp.concatenate([a, b], axis=1) for a, b in zip(both, more)]
    return tuple(both)


def second(got_ref, few_ref, even_ref, odd_ref, mid_ref, ft_ref, fl_ref, bt_ref, bl_ref, out_ref, few_out_ref, wait_part, send_part):
    forward, backward = (ft_ref[...], fl_ref[...]), (bt_ref[...], bl_ref[...])
    odd_y, even_y, full_y = (frequency_columns(k) for k in ("odd", "even", "signed"))
    for part in range(2):
        wait_part(part)
        got = from_tiles(got_ref, part)
        if part == 1:
            got = jnp.concatenate([got, unpack_columns(few_ref)], axis=1)
        spec = dot3(forward, with_swapped(got))
        lanes = slice(part * LANES, (part + 1) * LANES)
        kernel_even, kernel_odd = even_ref[:, lanes], odd_ref[:, lanes]
        lane = lanes_of(kernel_even.shape)
        last = spec[:, 4 * LANES :]
        tiles, columns = [None] * 4, []
        for n in range(2):
            a = spec[:, n * LANES : (n + 1) * LANES]
            b = spec[:, (2 + n) * LANES : (3 + n) * LANES]
            level = a + odd_y * b
            edge = even_y * b
            if part == 1:
                edge = edge + jnp.where(lane == 0, last[:, n : n + 1], 0.0)
            phi = kernel_even * level + kernel_odd * edge
            phi_edge = kernel_odd * level + kernel_even * edge
            tiles[n] = phi
            tiles[2 + n] = odd_y * phi + even_y * phi_edge
            columns.append(phi_edge[:, :1])
        if part == 1:
            mid = mid_ref[...] * (last + full_y * pltpu.roll(last, LANES - 4, 1))
            mid = mid + full_y * pltpu.roll(mid, 4, 1)
            tiles.append(jnp.where(lane == 0, columns[0], jnp.where(lane == 1, columns[1], mid)))
        back = dot3(backward, with_swapped(jnp.concatenate(tiles, axis=1)))
        to_tiles(back, out_ref, part)
        if part == 1:
            pack_columns(back[:, 4 * LANES :], few_out_ref)
        send_part(part)


def sample(
    slabs,
    subs,
    slab,
    got_ref,
    few_ref,
    top_ref,
    low_ref,
    zh_ref,
    wt_ref,
    wl_ref,
    mt_ref,
    ml_ref,
    sel_ref,
    out_ref,
    field_ref,
    here_ref,
    lhs_ref,
    wait_part,
    send_share,
):
    grid_y = G // subs
    grid_x = G // slabs
    half = G // 2
    window = window_of(slabs)
    own, spilt = plane_rows(slabs, subs)
    odd, even = frequency_rows("odd"), frequency_rows("even")
    kz = (slabs * (lax.broadcasted_iota(jnp.int32, (G, 1), 0) // grid_y) + slab).astype(jnp.float32)
    for part in range(2):
        wait_part(part)
        got = from_tiles(got_ref, part)
        phi = got[:, : 2 * LANES]
        along_x = [half_of(odd, part) * half_of(phi, n) for n in range(2)]
        if part == 1:
            last = unpack_columns(few_ref)
            along_x = [v + half_of(even, part) * last[:, n : n + 1] for n, v in enumerate(along_x)]
        lhs = jnp.concatenate([jnp.concatenate(along_x, axis=1), got[:, 2 * LANES : 4 * LANES], kz * phi], axis=0)
        rows = slice(part * 2 * LANES, (part + 1) * 2 * LANES)
        field = dot3(split(lhs), (wt_ref[rows], wl_ref[rows]))
        for t in range(2 * G // LANES):
            where = pl.ds(3 * t * G, 3 * G)
            value = field[:, t * LANES : (t + 1) * LANES]
            field_ref[where, :] = value if part == 0 else field_ref[where, :] + value
    sel = sel_ref[...]
    top, low = split(last)
    expanded = jnp.dot(top, sel, preferred_element_type=jnp.float32) + jnp.dot(
        low, sel, preferred_element_type=jnp.float32
    )
    pair = ((lanes_of((grid_y, 4 * LANES)) & (LANES - 1)) - lax.rem(slab, 2) * (2 * subs)) >> 1
    mids = jnp.zeros((grid_y, 4 * LANES), jnp.float32)
    for j in range(subs):
        mids = mids + jnp.where(pair == j, expanded[j * grid_y : (j + 1) * grid_y], 0.0)
    k = slab // 2 * LANES + (lanes_of((1, 2 * LANES)) & (LANES - 1))
    signed = jnp.where(k < half, k, k - G).astype(jnp.float32)
    mid_phi = mids[:, : 2 * LANES]
    mid_lhs = jnp.concatenate([signed * mid_phi, mids[:, 2 * LANES :], -float(half) * mid_phi], axis=0)
    mid_field = dot3(split(mid_lhs), (mt_ref[...], ml_ref[...]))
    row = rows_of((8, G))
    for y in range(grid_y):
        rows = []
        for c in range(3):
            for part in range(2):
                tiles = [
                    field_ref[pl.ds((3 * (part * G // LANES + t) + c) * G + y, subs, stride=grid_y), :]
                    for t in range(G // LANES)
                ]
                rows.append(jnp.concatenate(tiles, axis=1))
        mid = jnp.zeros((8, G), jnp.float32)
        for c in range(3):
            mid = jnp.where(row == c, mid_field[c * grid_y + y : c * grid_y + y + 1], mid)
        here_ref[y] = jnp.concatenate(rows + [mid, jnp.zeros((8, G), jnp.float32)], axis=0)
    lane = lanes_of((here_ref.shape[1], LANES))
    for block in range(slabs):
        turned = [pltpu.roll(here_ref[y], (window * y - grid_x * block) % G, 1) for y in range(grid_y)]
        tiles = []
        for t in range(own // LANES):
            value = jnp.zeros(lane.shape, jnp.float32)
            for y in range(grid_y):
                low_lane = window * y - LANES * t
                if low_lane + window <= 0 or low_lane >= LANES:
                    continue
                side = t * LANES % G
                inside = jnp.logical_and(lane >= low_lane, lane < low_lane + window)
                value = jnp.where(inside, turned[y][:, side : side + LANES], value)
            tiles.append(value)
        height = tiles[0].shape[0]
        lhs_ref[block, :height], lhs_ref[block, height:] = split(jnp.concatenate(tiles, axis=1))

    for part in (1, 0):
        start, rows = (own, spilt) if part else (0, own)

        def one(n, _):
            block = lax.rem(slab + n, slabs)
            at = part * slabs + block
            zh = zh_ref[at]
            lhs = lhs_ref[block, :, :rows]
            top, low = (ref[block, start : start + rows] for ref in (top_ref, low_ref))
            mixed = jnp.dot(lhs, top, preferred_element_type=jnp.float32)
            mixed = (mixed[:height] + mixed[height:]) + jnp.dot(
                lhs[:height], low, preferred_element_type=jnp.float32
            )
            for c in range(3):
                base = 2 * subs * c
                value = jnp.sum(mixed[base : base + 2 * subs] * zh[: 2 * subs], axis=0, keepdims=True)
                row = 6 * subs + c
                out_ref[at, c : c + 1] = value + mixed[row : row + 1] * zh[2 * subs : 2 * subs + 1]
            if part:
                send_share(part, n)
            else:

                @pl.when(n < slabs)
                def _():
                    send_share(part, n)

            return 0

        lax.fori_loop(1 - part, slabs + 1 - part, one, 0)


def kernel_planes(slabs, subs, slab, sub, planes_ref, mids_ref, even_ref, odd_ref, mid_ref):
    half = G // 2
    width_sq = G / 4.0 * (G / 4.0)
    scale = -recip_scale / (float(G) ** 3)
    flip = ((rows_of((G, G)) + lanes_of((G, G))) & (G - 1)) == 0
    flip = flip.astype(jnp.float32).astype(jnp.bfloat16)

    def product(a, b):
        return jnp.dot(a, b, preferred_element_type=jnp.float32)

    top, low = split(planes_ref[1])
    top, low = split(product(flip, top) + product(flip, low))
    mirrored = product(top, flip) + product(low, flip)
    first = planes_ref[0]
    kx, ky = frequency_rows("signed"), frequency_columns("signed")
    kz_here = slabs * sub + slab
    kz = kz_here.astype(jnp.float32)
    freq_sq = kx * kx + ky * ky + kz * kz
    anchor = freq_sq == 0.0
    gauss = jnp.where(
        anchor, 0.0, scale * jnp.exp(freq_sq * (-0.5 / width_sq)) / jnp.where(anchor, 1.0, freq_sq)
    )
    flat = kz_here == 0
    even_ref[...] = gauss * jnp.where(flat, first, first + mirrored)
    odd_ref[...] = gauss * jnp.where(flat, first, first - mirrored)
    rows = G // slabs
    tall = [
        jnp.concatenate([mids_ref[s]] * (LANES // 8), axis=0).T[:rows] for s in range(slabs)
    ]
    tall = jnp.concatenate(tall, axis=0)
    lane = lanes_of(tall.shape)
    chosen = lax.rem(2 * sub, 8)
    columns = [jnp.sum(jnp.where(lane == chosen + t, tall, 0.0), axis=1, keepdims=True) for t in range(2)]
    kx = 2 * (subs * slab + sub) + (lane & 1)
    kx = jnp.where(kx < half, kx, kx - G).astype(jnp.float32)
    mid_sq = kx * kx + ky * ky + float(half * half)
    value = jnp.where((lane & 1) == 0, columns[0], columns[1])
    value = jnp.where(jnp.logical_and(lane >= 2, lane < 6), value, 0.0)
    mid_ref[...] = value * (scale * jnp.exp(mid_sq * (-0.5 / width_sq)) / mid_sq)


def near_columns(positions, near_ref):
    for t in range(positions.shape[1] // LANES):
        tile = positions[:, t * LANES : (t + 1) * LANES]
        near_ref[t * LANES : (t + 1) * LANES, :] = jnp.concatenate([tile] * (LANES // 8), axis=0).T


def own_cells(own_ref, table_ref):
    for t in range(own_ref.shape[1] // LANES):
        tile = own_ref[:, t * LANES : (t + 1) * LANES]
        other = pltpu.roll(tile, LANES // 2, 1)
        first = lanes_of(tile.shape) < LANES // 2
        table_ref[2 * t] = jnp.where(first, tile, other)
        table_ref[2 * t + 1] = jnp.where(first, other, tile)


def pair_field(first, last, list_ref, count_ref, table_ref, near_ref, pair_ref):
    entries = list_ref.shape[1]
    width = LANES // 2
    first_half = lanes_of((8, LANES)) < width
    is_moment = rows_of((8, LANES)) < 3
    itself = rows_of((width, LANES)) == lanes_of((width, LANES))

    def one_cell(cell, _):
        base = pl.multiple_of(cell * width, width)
        near = near_ref[pl.ds(base, width), :]
        near_x, near_y, near_z = (
            jnp.broadcast_to(near[:, 3 + a : 4 + a], (width, LANES)) for a in range(3)
        )
        count = count_ref[cell]

        def terms(pair, masked):
            one = table_ref[list_ref[cell, 2 * pair]]
            two = table_ref[list_ref[cell, 2 * pair + 1]]
            live_one = jnp.where(2 * pair < count, 1.0, 0.0)
            live_two = jnp.where(2 * pair + 1 < count, 1.0, 0.0)
            far = jnp.where(first_half, one, two)
            far = jnp.where(is_moment, far * jnp.where(first_half, live_one, live_two), far)
            mx, my, mz = far[0:1], far[1:2], far[2:3]
            dx = near_x - far[3:4]
            dy = near_y - far[4:5]
            dz = near_z - far[5:6]
            softened = dx * dx + dy * dy + dz * dz + damping
            inverse = lax.rsqrt(softened)
            square = inverse * inverse
            cube = square * inverse
            if masked:
                cube = jnp.where(itself, 0.0, cube)
            radial = (3.0 * (dx * mx + dy * my + dz * mz)) * (cube * square)
            return radial * dx - cube * mx, radial * dy - cube * my, radial * dz - cube * mz

        def step(pair, totals):
            return tuple(t + a for t, a in zip(totals, terms(pair, False)))

        totals = lax.fori_loop(1, entries // 2, step, terms(0, True))
        sums = [jnp.sum(t, axis=1, keepdims=True) for t in totals]
        lane = lanes_of((width, LANES))
        pair_ref[pl.ds(base, width), :] = jnp.where(
            lane == 0, sums[0], jnp.where(lane == 1, sums[1], jnp.where(lane == 2, sums[2], 0.0))
        )
        return 0

    lax.fori_loop(first, last, one_cell, 0)


def around(slabs, subs):
    slab, sub = lax.axis_index("slab"), lax.axis_index("sub")
    up, down = lax.rem(sub + 1, subs), lax.rem(sub + subs - 1, subs)
    turns = [lax.rem(slab + k, slabs) for k in range(slabs)]
    return slab, sub, up, down, turns


def remote(source, target, send_sem, recv_sem, device):
    return pltpu.make_async_remote_copy(
        src_ref=source,
        dst_ref=target,
        send_sem=send_sem,
        recv_sem=recv_sem,
        device_id=device,
        device_id_type=MESH,
    )


def landed(ref, sem):
    pltpu.make_async_copy(ref, ref, sem).wait()


INPUTS = (
    ["cells", "counts", "sends", "pol", "perm", "pos", "frac", "base"]
    + ["phase_t", "phase_l", "bm_t", "bm_l", "gather", "expand", "influence"]
    + ["tx_t", "tx_l", "bx_t", "bx_l", "ty_t", "ty_l", "by_t", "by_l"]
)
TWIDDLES = INPUTS[-8:]
SMEM_INPUTS = 3


class Refs:
    def __init__(self, names, refs):
        for name, ref in zip(names, refs, strict=True):
            setattr(self, name, ref)


def whole_kernel(slabs, subs, names, *refs):
    r = Refs(names, refs)
    slab, sub, up, down, turns = around(slabs, subs)
    depth, rows = r.moved.shape[0], r.moved.shape[1]
    half = slabs * subs
    middle = subs // 2
    group = 2 * subs

    barrier = pltpu.get_barrier_semaphore()

    def greet(to_slab, to_sub):
        pl.semaphore_signal(barrier, inc=1, device_id=(to_slab, to_sub), device_id_type=MESH)

    def folded_of(kz):
        upper = kz >= half
        folded = jnp.where(upper, lax.rem(2 * half - kz, half), kz)
        return folded, jnp.where(upper, 1, 0)

    for t in turns[1:]:
        greet(t, sub)
    for t in turns:
        greet(t, up)
        greet(t, down)

    def greet_sub(k, _):
        greet(slab, lax.rem(sub + k, subs))
        return 0

    lax.fori_loop(2, subs - 1, greet_sub, 0)
    here_kz = slabs * sub + slab
    expected = 3 * slabs - 1 + subs - 3
    for kz in (here_kz, jnp.where(here_kz == 0, half, 2 * half - here_kz)):
        from_sub = lax.div(kz, depth)
        for t in range(slabs):
            other = jnp.logical_or(from_sub != sub, slab != t)

            @pl.when(other)
            def _():
                greet(t, from_sub)

    for i in range(depth):
        folded, _ = folded_of(depth * sub + i)
        mine = jnp.logical_and(lax.rem(folded, slabs) == slab, lax.div(folded, slabs) == sub)
        expected = expected + jnp.where(mine, 0, 1)
    moves = [
        pltpu.make_async_copy(r.influence.at[:, :, pl.ds(h * LANES, LANES)], r.raw.at[h], r.move.at[h])
        for h in range(G // LANES)
    ]
    loads = [
        pltpu.make_async_copy(getattr(r, name), getattr(r, "in_" + name), r.load.at[n])
        for n, name in enumerate(TWIDDLES)
    ]
    for move in [*moves, *loads]:
        move.start()
    pl.semaphore_wait(barrier, expected)

    def to_group(source, target, send_sem, recv_sem):
        goals = [(t, sub, slab) for t in turns[1:]] + [(t, up, slabs + slab) for t in turns]
        return [
            remote(source, target.at[slot], send_sem.at[n], recv_sem.at[slot], (to_slab, to_sub))
            for n, (to_slab, to_sub, slot) in enumerate(goals)
        ]

    def ghost_copies(it):
        goals = [(slab, up), (slab, down), (turns[1], sub), (turns[-1], sub)]
        ghosts = r.ghosts.shape[2]
        return [
            remote(
                r.ghosts.at[it, q],
                r.landing.at[it, pl.ds(q * ghosts, ghosts)],
                r.ghost_send.at[q],
                r.ghost_recv.at[it, q],
                goal,
            )
            for q, goal in enumerate(goals)
        ]

    def send_cells(it):
        own_cells(r.body, r.own_tiles)
        r.tables[: r.cells.shape[0]] = r.own_tiles[...]
        ghosts = r.ghosts.shape[2]
        for q in range(4):
            for slot in range(ghosts):
                r.ghosts[it, q, slot] = r.own_tiles[r.sends[0, q, slot]]
        for copy in ghost_copies(it):
            copy.start()

    def send_moments(it):
        for copy in to_group(r.own, r.mom.at[it], r.mom_send, r.mom_recv.at[it]):
            copy.start()
        r.mom[it, slab] = r.own[...]
        r.body[0:3] = r.own[0:3]
        send_cells(it)

    atoms = r.own.shape[1]
    r.own[0:3] = r.pol[...] * r.perm[...]
    r.own[3:4] = jnp.zeros((1, atoms), jnp.float32)
    r.body[3:6] = r.pos[...]
    r.body[6:8] = jnp.zeros((2, atoms), jnp.float32)
    r.still[slab, 0:3] = r.frac[...]
    r.still[slab, 3:6] = r.base[...].astype(jnp.float32)
    r.still[slab, 6:8] = jnp.zeros((2, atoms), jnp.float32)
    still_copies = to_group(r.still.at[slab], r.still, r.still_send, r.still_recv)
    for copy in still_copies:
        copy.start()
    send_moments(0)

    def plane(i):
        folded, slot = folded_of(depth * sub + i)
        to_slab, to_sub = lax.rem(folded, slabs), lax.div(folded, slabs)
        target = r.planes.at[slot, pl.ds(slab * rows, rows)]
        far = remote(
            r.moved.at[i], target, r.plane_send.at[i], r.plane_recv.at[slot, slab], (to_slab, to_sub)
        )
        return far, slot, jnp.logical_and(to_slab == slab, to_sub == sub)

    def here(i, slot):
        return pltpu.make_async_copy(
            r.moved.at[i], r.planes.at[slot, pl.ds(slab * rows, rows)], r.plane_recv.at[slot, slab]
        )

    for move in moves:
        move.wait()
    raw = r.raw.reshape(G // LANES * rows * depth, LANES)
    for i in range(depth):
        for h in range(G // LANES):
            r.moved[i, :, h * LANES : (h + 1) * LANES] = raw[pl.ds(h * rows * depth + i, rows, stride=depth), :]
        far, slot, mine = plane(i)

        @pl.when(mine)
        def _():
            here(i, slot).start()

        @pl.when(jnp.logical_not(mine))
        def _():
            far.start()

    first = r.moved[0]
    r.turned[...] = jnp.concatenate([first] * (LANES // rows), axis=0).T

    def hop(n):
        return remote(
            r.turned.at[pl.ds(turns[n] * group, group)],
            r.hop.at[slab],
            r.hop_send.at[n - 1],
            r.hop_recv.at[slab],
            (turns[n], sub),
        )

    def mid(n):
        to_sub = lax.rem(middle + n, subs)
        return remote(
            r.hop.at[:, pl.ds(lax.div(to_sub, 4) * 8, 8)],
            r.mids,
            r.mid_send.at[n - 1],
            r.mid_recv,
            (slab, to_sub),
        )

    @pl.when(sub == middle)
    def _():
        for n in range(1, slabs):
            hop(n).start()
        r.hop[slab] = r.turned[pl.ds(pl.multiple_of(slab * group, group), group)]

    near_columns(r.body[...], r.near)
    phase = (r.phase_t[slab], r.phase_l[slab])

    def tables(before):
        def one(n, _):
            block = lax.rem(slab + n, slabs)
            at = block + slabs if before else block

            @pl.when(jnp.logical_or(before, n > 0))
            def _():
                landed(r.still.at[at], r.still_recv.at[at])

            tables_of(slabs, subs, r.still, block, before, phase, r.plane_t, r.plane_l, r.zhat)
            return 0

        lax.fori_loop(0, slabs, one, 0)

    tables(False)

    @pl.when(sub == middle)
    def _():
        for t in turns[1:]:
            landed(r.hop.at[t], r.hop_recv.at[t])
        for n in range(1, subs):
            mid(n).start()
        r.mids[...] = r.hop[:, (middle // 4) * 8 : (middle // 4) * 8 + 8]

    tables(True)
    for load in loads:
        load.wait()

    def exchange(send, few, got, got_few, part, send_sem, recv_sem):
        first, count = part_rows(part, send.shape[1] // TILES)
        rows = pl.ds(first, count)

        def all_to_all(sources, targets, n):
            pltpu.make_async_copy(sources(sub), targets, recv_sem.at[n]).start()

            def one(k, _):
                to_sub = lax.rem(sub + k, subs)
                remote(sources(to_sub), targets, send_sem.at[n], recv_sem.at[n], (slab, to_sub)).start()
                return 0

            lax.fori_loop(1, subs, one, 0)

        if part == 1:
            all_to_all(lambda to: few.at[to], got_few.at[sub], 2)
        all_to_all(lambda to: send.at[to, rows], got.at[sub, rows], part)

    def exchanged(got, got_few, part, recv_sem):
        first, count = part_rows(part, got.shape[1] // TILES)
        landed(got.at[:, pl.ds(first, count)], recv_sem.at[part])
        if part == 1:
            landed(got_few, recv_sem.at[2])

    def iteration(it, _):
        density(
            slabs,
            subs,
            slab,
            r.mom.at[it],
            r.plane_t,
            r.plane_l,
            r.zhat,
            r.grid,
            lambda slot: landed(r.mom.at[it, slot], r.mom_recv.at[it, slot]),
        )
        got_a, got_b = r.got_a.at[it], r.got_b.at[it]
        few_a, few_b = r.got_few_a.at[it], r.got_few_b.at[it]
        first_frequency(
            slabs,
            subs,
            slab,
            r.grid,
            r.in_tx_t,
            r.in_tx_l,
            r.gather,
            r.send_a,
            r.few_a,
            r.edge,
            r.mid_rows,
            lambda part: exchange(r.send_a, r.few_a, got_a, few_a, part, r.a_send, r.a_recv.at[it]),
        )

        @pl.when(it == 0)
        def _():
            @pl.when(sub != middle)
            def _():
                landed(r.mids, r.mid_recv)

            for slot in range(2):
                for source in range(slabs):
                    landed(r.planes.at[slot, pl.ds(source * rows, rows)], r.plane_recv.at[slot, source])
            kernel_planes(slabs, subs, slab, sub, r.planes, r.mids, r.even, r.odd, r.mid_tile)

        cells, ghosts = r.cells.shape[0], r.ghosts.shape[2]
        for q in range(4):
            landed(r.landing.at[it, pl.ds(q * ghosts, ghosts)], r.ghost_recv.at[it, q])
        r.tables[cells:] = r.landing[it]
        cuts = [0, 3 * cells // 8, 5 * cells // 8, cells]

        def pairs(step):
            pair_field(cuts[step], cuts[step + 1], r.cells, r.counts, r.tables, r.near, r.pair)

        def sent_back(part):
            exchange(r.send_b, r.few_b, got_b, few_b, part, r.b_send, r.b_recv.at[it])
            pairs(1 + part)

        pairs(0)

        second(
            got_a,
            few_a,
            r.even,
            r.odd,
            r.mid_tile,
            r.in_ty_t,
            r.in_ty_l,
            r.in_by_t,
            r.in_by_l,
            r.send_b,
            r.few_b,
            lambda part: exchanged(got_a, few_a, part, r.a_recv.at[it]),
            sent_back,
        )
        for t in range(atoms // LANES):
            tile = r.pair[t * LANES : (t + 1) * LANES, :].T[:8]
            r.rest[:, t * LANES : (t + 1) * LANES] = tile
        r.rest[0:3] += r.perm[...]

        def share_copy(part, n):
            to_slab = lax.rem(slab + n, slabs)
            slot = part * slabs + slab
            return remote(
                r.share.at[part * slabs + to_slab],
                r.land.at[it, slot],
                r.share_send.at[part * (slabs - 1) + n - 1 + part],
                r.share_recv.at[it, slot],
                (to_slab, down if part else sub),
            )

        sample(
            slabs,
            subs,
            slab,
            got_b,
            few_b,
            r.plane_t,
            r.plane_l,
            r.zhat,
            r.in_bx_t,
            r.in_bx_l,
            r.bm_t.at[slab // 2],
            r.bm_l.at[slab // 2],
            r.expand,
            r.share,
            r.field,
            r.here,
            r.lhs,
            lambda part: exchanged(got_b, few_b, part, r.b_recv.at[it]),
            lambda part, n: share_copy(part, n).start(),
        )
        total = r.rest[0:3] + r.share[slab, 0:3]
        for slot in [*turns[1:], *(slabs + k for k in range(slabs))]:
            landed(r.land.at[it, slot], r.share_recv.at[it, slot])
            total = total + r.land[it, slot, 0:3]
        for copy in to_group(r.own, r.mom.at[it], r.mom_send, r.mom_recv.at[it]):
            copy.wait_send()
        for copy in ghost_copies(it):
            copy.wait_send()
        r.own[0:3] = r.pol[...] * total

        @pl.when(it + 1 < ITERS)
        def _():
            send_moments(it + 1)

        for n in range(1, slabs):
            share_copy(0, n).wait_send()
        for n in range(slabs):
            share_copy(1, n).wait_send()
        for part in range(2):
            rows_sent = pl.ds(*part_rows(part, r.send_a.shape[1] // TILES))
            landed(r.send_a.at[pl.ds(0, subs - 1), rows_sent], r.a_send.at[part])
            landed(r.send_b.at[pl.ds(0, subs - 1), rows_sent], r.b_send.at[part])
        landed(r.few_a.at[pl.ds(0, subs - 1)], r.a_send.at[2])
        landed(r.few_b.at[pl.ds(0, subs - 1)], r.b_send.at[2])
        return 0

    lax.fori_loop(0, ITERS, iteration, 0)
    r.out[...] = r.own[0:3]
    for copy in still_copies:
        copy.wait_send()

    @pl.when(sub == middle)
    def _():
        for n in range(1, slabs):
            hop(n).wait_send()
        for n in range(1, subs):
            mid(n).wait_send()

    for i in range(depth):
        far, slot, mine = plane(i)

        @pl.when(jnp.logical_not(mine))
        def _():
            far.wait_send()


def shards(
    positions,
    fraction,
    grid_base,
    polarizability,
    perm_field,
    influence,
    neighbour_cells,
    neighbour_count,
    send_cells,
):
    atoms = positions.shape[1]
    cells = neighbour_cells.shape[0]
    ghosts = send_cells.shape[2]
    slabs = lax.axis_size("slab")
    subs = lax.axis_size("sub")
    grid_x = G // slabs
    grid_y = G // subs
    depth = G // subs

    index = np.arange(G)
    angle = (index[:, None] * index[None, :] % G) * (2.0 * np.pi / G)
    kz_rows = np.arange(slabs)[:, None] + slabs * np.arange(subs)[None, :]
    turn = kz_rows[:, :, None] * index[None, None, :] % G * (2.0 * np.pi / G)
    ranks = 2 * subs + 8
    phase = np.zeros((slabs, ranks, G), np.float32)
    phase[:, :subs] = np.cos(turn)
    phase[:, subs : 2 * subs] = -np.sin(turn)
    phase[:, 2 * subs] = np.where(index % 2 == 0, 1.0, -1.0)
    cos_np, sin_np = np.cos(angle), np.sin(angle)
    halves = np.concatenate([index[:LANES], G + index[:LANES], index[LANES:], G + index[LANES:]])
    turn_x = parts_of(np.block([[cos_np, -sin_np], [sin_np, cos_np]])[:, halves])
    back_x = parts_of(np.block([[cos_np, sin_np], [-sin_np, cos_np]])[halves])
    turn_y = parts_of(np.concatenate([cos_np, sin_np], axis=1))
    back_y = parts_of(np.concatenate([cos_np, -sin_np], axis=1))
    wide = np.stack(
        [np.concatenate([cos_np[w : w + LANES], -sin_np[w : w + LANES]], axis=0) for w in range(0, G, LANES)]
    )
    phase, back_mid = parts_of(phase), parts_of(wide)
    select = np.zeros((4, LANES, LANES), np.float32)
    for q in range(4):
        for lane in range(LANES):
            select[q, lane, 2 + 2 * q + lane % 2] = 1.0
    gather = jnp.asarray(select.reshape(4 * LANES, LANES), jnp.bfloat16)
    expand = jnp.asarray(np.concatenate(list(select.transpose(0, 2, 1)), axis=1), jnp.bfloat16)

    operands = [
        neighbour_cells,
        neighbour_count,
        send_cells,
        polarizability[None, :],
        perm_field,
        positions,
        fraction,
        grid_base,
        *phase,
        *back_mid,
        gather,
        expand,
        influence,
        *turn_x,
        *back_x,
        *turn_y,
        *back_y,
    ]
    vmem = pl.BlockSpec(memory_space=pltpu.VMEM)
    smem = pl.BlockSpec(memory_space=pltpu.SMEM)
    far = len(TWIDDLES) + 1
    specs = [smem] * SMEM_INPUTS + [vmem] * (len(operands) - SMEM_INPUTS - far)
    specs += [pl.BlockSpec(memory_space=pl.ANY)] * far

    def held(*shape, dtype=jnp.float32):
        return pltpu.VMEM(shape, dtype)

    held16 = functools.partial(held, dtype=jnp.bfloat16)
    dma = pltpu.SemaphoreType.DMA
    chunk = (subs, TILES * grid_y, LANES)
    columns = 6 * subs + 16
    sends = 2 * slabs - 1
    planes = sum(plane_rows(slabs, subs))
    scratch = dict(
        mom=held(ITERS, 2 * slabs, 4, atoms),
        still=held(2 * slabs, 8, atoms),
        own=held(4, atoms),
        body=held(8, atoms),
        own_tiles=held(cells, 8, LANES),
        tables=held(cells + 4 * ghosts, 8, LANES),
        landing=held(ITERS, 4 * ghosts, 8, LANES),
        ghosts=held(ITERS, 4, ghosts, 8, LANES),
        near=held(atoms, LANES),
        pair=held(atoms, LANES),
        rest=held(8, atoms),
        plane_t=held16(slabs, planes, atoms),
        plane_l=held16(slabs, planes, atoms),
        zhat=held(2 * slabs, ranks, atoms),
        raw=held(G // LANES, grid_x, depth, LANES),
        moved=held(depth, grid_x, G),
        turned=held(G, LANES),
        hop=held(slabs, grid_x, LANES),
        planes=held(2, G, G),
        mids=held(slabs, 8, LANES),
        even=held(G, G),
        odd=held(G, G),
        mid_tile=held(G, LANES),
        grid=held(grid_y, G + 8, 256),
        mid_rows=held(4, grid_y, G),
        send_a=held(*chunk),
        got_a=held(ITERS, *chunk),
        few_a=held(subs, 1, LANES),
        got_few_a=held(ITERS, subs, 1, LANES),
        few_b=held(subs, 1, LANES),
        got_few_b=held(ITERS, subs, 1, LANES),
        edge=held(G, LANES),
        send_b=held(*chunk),
        got_b=held(ITERS, *chunk),
        field=held(6 * G * G // LANES, LANES),
        here=held(grid_y, columns, G),
        lhs=held16(slabs, 2 * columns, plane_rows(slabs, subs)[0]),
        share=held(2 * slabs, 4, atoms),
        land=held(ITERS, 2 * slabs, 4, atoms),
        **{
            "in_" + name: held16(*operand.shape)
            for name, operand in zip(TWIDDLES, operands[-len(TWIDDLES) :], strict=True)
        },
        load=dma((len(TWIDDLES),)),
        mom_send=dma((sends,)),
        mom_recv=dma((ITERS, 2 * slabs)),
        still_send=dma((sends,)),
        still_recv=dma((2 * slabs,)),
        ghost_send=dma((4,)),
        ghost_recv=dma((ITERS, 4)),
        move=dma((G // LANES,)),
        plane_send=dma((depth,)),
        plane_recv=dma((2, slabs)),
        hop_send=dma((slabs - 1,)),
        hop_recv=dma((slabs,)),
        mid_send=dma((subs - 1,)),
        mid_recv=dma,
        a_send=dma((3,)),
        a_recv=dma((ITERS, 3)),
        b_send=dma((3,)),
        b_recv=dma((ITERS, 3)),
        share_send=dma((sends,)),
        share_recv=dma((ITERS, 2 * slabs)),
    )
    names = [*INPUTS, "out", *scratch]
    return pl.pallas_call(
        functools.partial(whole_kernel, slabs, subs, names),
        out_shape=jax.ShapeDtypeStruct((3, atoms), jnp.float32),
        in_specs=specs,
        out_specs=vmem,
        scratch_shapes=list(scratch.values()),
        compiler_params=pltpu.CompilerParams(vmem_limit_bytes=60 << 20, collective_id=0, has_side_effects=True),
        name="dipoles",
    )(*operands)


def solution(mesh):
    in_specs = (
        P(None, ("slab", "sub")),
        P(None, ("slab", "sub")),
        P(None, ("slab", "sub")),
        P(("slab", "sub")),
        P(None, ("slab", "sub")),
        P("slab", "sub", None),
        P(("slab", "sub"), None),
        P(("slab", "sub")),
        P(("slab", "sub"), None, None),
    )
    out_specs = P(None, ("slab", "sub"))
    return jax.shard_map(shards, mesh=mesh, in_specs=in_specs, out_specs=out_specs, check_vma=False)
```

```python
import functools
import math

import jax
import jax.numpy as jnp
import numpy as np
from jax import lax
from jax.experimental import pallas as pl
from jax.experimental.pallas import tpu as pltpu
from jax.sharding import PartitionSpec as P

G = 256
ITERS = 2

damping = 1.0
recip_scale = 16.0
highest = lax.Precision.HIGHEST
LANES = 128
TILES = 4 * G // LANES
MESH = pl.DeviceIdType.MESH


def spline_weights(fraction):
    square = fraction * fraction
    cube = square * fraction
    rest = 1.0 - fraction
    return [
        rest * rest * rest / 6.0,
        (3.0 * cube - 6.0 * square + 4.0) / 6.0,
        (-3.0 * cube + 3.0 * square + 3.0 * fraction + 1.0) / 6.0,
        cube / 6.0,
    ]


def split(x):
    top = x.astype(jnp.bfloat16)
    return top, (x - top.astype(jnp.float32)).astype(jnp.bfloat16)


def dot3(a, b, turned=False):
    dims = (((1,), (1 if turned else 0,)), ((), ()))

    def one(x, y):
        return lax.dot_general(x, y, dims, preferred_element_type=jnp.float32)

    return one(a[0], b[0]) + (one(a[1], b[0]) + one(a[0], b[1]))


def parts_of(table):
    table = np.asarray(table, np.float32)
    top = table.astype(jnp.bfloat16)
    low = (table - top.astype(np.float32)).astype(jnp.bfloat16)
    return jnp.asarray(top), jnp.asarray(low)


def lanes_of(shape):
    return lax.broadcasted_iota(jnp.int32, shape, len(shape) - 1)


def rows_of(shape):
    return lax.broadcasted_iota(jnp.int32, shape, len(shape) - 2)


def window_of(slabs):
    return G // slabs + 8


def plane_rows(slabs, subs):
    window = window_of(slabs)
    return tuple(-(-count * window // LANES) * LANES for count in (G // subs, 3))


def tables_of(slabs, subs, still_ref, block, before, phase, top_ref, low_ref, zh_ref):
    at = block + slabs if before else block
    still = still_ref[at]
    atoms = still.shape[1]

    def table(axis, length):
        offset = rows_of((length, atoms)) - still[3 + axis : 4 + axis].astype(jnp.int32)
        total = jnp.zeros(offset.shape, jnp.float32)
        for stencil, weight in enumerate(spline_weights(still[axis : 1 + axis])):
            total = jnp.where(offset == stencil, weight, total)
        return total

    along_x, along_y = table(0, window_of(slabs)), table(1, 16)
    grid_y = G // subs
    first, count = (grid_y, 3) if before else (0, grid_y)
    own, spilt = plane_rows(slabs, subs)
    start, rows = (own, spilt) if before else (0, own)
    blank = jnp.zeros((rows - count * along_x.shape[0], atoms), jnp.float32)
    plane = [along_x * along_y[first + y : first + y + 1] for y in range(count)]
    top, low = split(jnp.concatenate([*plane, blank], axis=0))
    top_ref[block, start : start + rows] = top
    low_ref[block, start : start + rows] = low
    z0 = still[5:6].astype(jnp.int32)
    chosen = (rows_of((G, atoms)) == z0).astype(jnp.float32).astype(jnp.bfloat16)
    start = jnp.dot(phase[0], chosen, preferred_element_type=jnp.float32) + jnp.dot(
        phase[1], chosen, preferred_element_type=jnp.float32
    )
    steps = phase[0][:, :LANES].astype(jnp.float32) + phase[1][:, :LANES].astype(jnp.float32)
    wide = [jnp.zeros((subs, atoms), jnp.float32)] * 2
    mid = jnp.zeros((1, atoms), jnp.float32)
    for t, weight in enumerate(spline_weights(still[2:3])):
        wide = [v + weight * steps[n * subs : (n + 1) * subs, t : t + 1] for n, v in enumerate(wide)]
        mid = mid + (weight if t % 2 == 0 else -weight)
    re, im = start[:subs], start[subs : 2 * subs]
    zh_ref[at, :subs] = re * wide[0] - im * wide[1]
    zh_ref[at, subs : 2 * subs] = re * wide[1] + im * wide[0]
    zh_ref[at, 2 * subs :] = start[2 * subs :] * mid


def frequency_rows(kind):
    k = lanes_of((1, G))
    signed = jnp.where(k < G // 2, k, k - G).astype(jnp.float32)
    if kind == "odd":
        return jnp.where(k == G // 2, 0.0, signed)
    if kind == "even":
        return jnp.where(k == G // 2, signed, 0.0)
    return signed


def frequency_columns(kind):
    k = lax.broadcasted_iota(jnp.int32, (G, 1), 0)
    signed = jnp.where(k < G // 2, k, k - G).astype(jnp.float32)
    if kind == "odd":
        return jnp.where(k == G // 2, 0.0, signed)
    if kind == "even":
        return jnp.where(k == G // 2, signed, 0.0)
    return signed


def density(slabs, subs, slab, mom_ref, top_ref, low_ref, zh_ref, grid_ref, wait_block):
    grid_y = G // subs
    grid_x = G // slabs
    window = window_of(slabs)
    own, _ = plane_rows(slabs, subs)
    grid_ref[...] = jnp.zeros_like(grid_ref)

    for part in range(2):

        def one(n, _):
            block = lax.rem(slab + n, slabs)
            at = block + part * slabs
            if part == 0:

                @pl.when(n > 0)
                def _():
                    wait_block(at)

            else:
                wait_block(at)
            mu = mom_ref[at]
            zh = zh_ref[at]
            row = rows_of((8, mu.shape[1]))
            last = jnp.where(row == 0, mu[0:1], jnp.where(row == 1, mu[1:2], mu[2:3]))
            values = jnp.concatenate(
                [zh[: 2 * subs] * mu[c : c + 1] for c in range(3)] + [last * zh[2 * subs : 2 * subs + 1]], axis=0
            )
            start, count = (0, grid_y) if part == 0 else (own, 3)
            rows = -(-count * window // 16) * 16
            plane = tuple(ref[block, start : start + rows] for ref in (top_ref, low_ref))
            got = dot3(plane, split(values), True)
            columns = values.shape[0]
            for y in range(count):
                where = pl.ds(pl.multiple_of(block * grid_x, grid_x), window)
                grid_ref[y, where, :columns] += got[y * window : (y + 1) * window]
            return 0

        lax.fori_loop(0, slabs, one, 0)
    for y in range(grid_y):
        grid_ref[y, :8] += grid_ref[y, G : G + 8]


def half_of(row, part):
    return row[:, part * LANES : (part + 1) * LANES]


def first_frequency(slabs, subs, slab, grid_ref, wt_ref, wl_ref, sel_ref, out_ref, few_ref, edge_ref, mid_ref, send_part):
    grid_y = G // subs
    half = G // 2
    flat_ref = out_ref.reshape(subs * TILES * grid_y, LANES)
    rows = []
    for y in range(grid_y):
        turned = grid_ref[y, :G].T
        for c in range(3):
            base = 2 * subs * c
            rows.append(
                jnp.concatenate([turned[base : base + subs], turned[base + subs : base + 2 * subs]], axis=1)
            )
        mids = turned[6 * subs : 6 * subs + 8]
        rows.append(jnp.concatenate([mids, jnp.zeros_like(mids)], axis=1))
    lhs = split(jnp.concatenate(rows, axis=0))
    odd, signed = frequency_rows("odd"), frequency_rows("signed")
    kz = (slabs * lax.broadcasted_iota(jnp.int32, (subs, 1), 0) + slab).astype(jnp.float32)
    lane = lanes_of((subs, LANES))
    per_y = 3 * subs + 8

    def transformed(part):
        columns = slice(part * 2 * LANES, (part + 1) * 2 * LANES)
        spec = dot3(lhs, (wt_ref[:, columns], wl_ref[:, columns]))
        for y in range(grid_y):
            at = spec[y * per_y : (y + 1) * per_y]
            sx, sy, sz = (at[c * subs : (c + 1) * subs] for c in range(3))
            tiles = [
                half_of(odd, part) * half_of(sx, n) + kz * half_of(sz, n) for n in range(2)
            ] + [half_of(sy, 0), half_of(sy, 1)]
            if part == 1:
                edge_ref[pl.ds(y, subs, stride=grid_y), :] = -float(half) * jnp.where(
                    lane == 0, sx[:, :1], jnp.where(lane == 1, sx[:, LANES : LANES + 1], 0.0)
                )
            for t, value in enumerate(tiles):
                flat_ref[pl.ds((part * 4 + t) * grid_y + y, subs, stride=TILES * grid_y), :] = value
            mid = at[3 * subs :]
            lanes = slice(part * LANES, (part + 1) * LANES)
            for n in range(2):
                mx, my, mz = (half_of(mid[c : c + 1], n) for c in range(3))
                mid_ref[n, y : y + 1, lanes] = half_of(signed, part) * mx - float(half) * mz
                mid_ref[2 + n, y : y + 1, lanes] = my

    transformed(0)
    send_part(0)
    transformed(1)
    window = pl.ds(pl.multiple_of(slab // 2 * LANES, LANES), LANES)
    pair = (lanes_of((grid_y, LANES)) - lax.rem(slab, 2) * (2 * subs)) >> 1
    columns = []
    for q in range(4):
        value = mid_ref[q, :, window]
        columns.append(jnp.concatenate([jnp.where(pair == j, value, 0.0) for j in range(subs)], axis=0))
    top, low = split(jnp.concatenate(columns, axis=1))
    sel = sel_ref[...]
    more = jnp.dot(top, sel, preferred_element_type=jnp.float32) + jnp.dot(
        low, sel, preferred_element_type=jnp.float32
    )
    pack_columns(edge_ref[...] + more, few_ref)
    send_part(1)


def part_rows(part, high):
    return part * 4 * high, 4 * high


def pack_columns(value, ref):
    spread = pltpu.roll(value, 0, 1, stride=LANES // 8, stride_axis=0)
    rows = jnp.sum(spread.reshape(ref.shape[0], 8, LANES), axis=1)
    for block in range(ref.shape[0]):
        ref[block] = rows[block : block + 1]


def unpack_columns(ref):
    rows = jnp.concatenate([jnp.broadcast_to(ref[block], (8, LANES)) for block in range(ref.shape[0])], axis=0)
    y = rows_of(rows.shape) & 7
    back = rows
    for n in range(1, 8):
        back = jnp.where(y == n, pltpu.roll(rows, LANES - n * (LANES // 8), 1), back)
    return jnp.where(lanes_of(back.shape) < LANES // 8, back, 0.0)


def from_tiles(ref, part):
    blocks, rows, lanes = ref.shape
    high = rows // TILES
    first, count = part_rows(part, high)
    return jnp.concatenate(
        [ref[:, r : r + high, :].reshape(blocks * high, lanes) for r in range(first, first + count, high)], axis=1
    )


def to_tiles(value, ref, part):
    blocks, rows, lanes = ref.shape
    high = rows // TILES
    first, count = part_rows(part, high)
    for t in range(count // high):
        ref[:, first + t * high : first + (t + 1) * high, :] = value[:, t * lanes : (t + 1) * lanes].reshape(
            blocks, high, lanes
        )


def with_swapped(x):
    def tile(v, t):
        return v[:, t * LANES : (t + 1) * LANES]

    both = [
        jnp.concatenate([v, jnp.concatenate([tile(v, 1), -tile(v, 0), tile(v, 3), -tile(v, 2)], axis=1)], axis=0)
        for v in split(x[:, : 4 * LANES])
    ]
    if x.shape[1] > 4 * LANES:
        last = x[:, 4 * LANES :]
        lane = lanes_of(last.shape)
        back, on = pltpu.roll(last, LANES - 1, 1), pltpu.roll(last, 1, 1)
        back2, on2 = pltpu.roll(last, LANES - 2, 1), pltpu.roll(last, 2, 1)
        upper = ((lane - 2) & 2) == 0
        turned = jnp.where(lane == 0, back, jnp.where(lane == 1, -on, jnp.where(upper, back2, -on2)))
        more = split(jnp.concatenate([last, turned], axis=0))
        both = [jnp.concatenate([a, b], axis=1) for a, b in zip(both, more)]
    return tuple(both)


def second(got_ref, few_ref, even_ref, odd_ref, mid_ref, ft_ref, fl_ref, bt_ref, bl_ref, out_ref, few_out_ref, wait_part, send_part):
    forward, backward = (ft_ref[...], fl_ref[...]), (bt_ref[...], bl_ref[...])
    odd_y, even_y, full_y = (frequency_columns(k) for k in ("odd", "even", "signed"))
    for part in range(2):
        wait_part(part)
        got = from_tiles(got_ref, part)
        if part == 1:
            got = jnp.concatenate([got, unpack_columns(few_ref)], axis=1)
        spec = dot3(forward, with_swapped(got))
        lanes = slice(part * LANES, (part + 1) * LANES)
        kernel_even, kernel_odd = even_ref[:, lanes], odd_ref[:, lanes]
        lane = lanes_of(kernel_even.shape)
        last = spec[:, 4 * LANES :]
        tiles, columns = [None] * 4, []
        for n in range(2):
            a = spec[:, n * LANES : (n + 1) * LANES]
            b = spec[:, (2 + n) * LANES : (3 + n) * LANES]
            level = a + odd_y * b
            edge = even_y * b
            if part == 1:
                edge = edge + jnp.where(lane == 0, last[:, n : n + 1], 0.0)
            phi = kernel_even * level + kernel_odd * edge
            phi_edge = kernel_odd * level + kernel_even * edge
            tiles[n] = phi
            tiles[2 + n] = odd_y * phi + even_y * phi_edge
            columns.append(phi_edge[:, :1])
        if part == 1:
            mid = mid_ref[...] * (last + full_y * pltpu.roll(last, LANES - 4, 1))
            mid = mid + full_y * pltpu.roll(mid, 4, 1)
            tiles.append(jnp.where(lane == 0, columns[0], jnp.where(lane == 1, columns[1], mid)))
        back = dot3(backward, with_swapped(jnp.concatenate(tiles, axis=1)))
        to_tiles(back, out_ref, part)
        if part == 1:
            pack_columns(back[:, 4 * LANES :], few_out_ref)
        send_part(part)


def sample(
    slabs,
    subs,
    slab,
    got_ref,
    few_ref,
    top_ref,
    low_ref,
    zh_ref,
    wt_ref,
    wl_ref,
    mt_ref,
    ml_ref,
    sel_ref,
    out_ref,
    field_ref,
    here_ref,
    lhs_ref,
    wait_part,
    send_share,
):
    grid_y = G // subs
    grid_x = G // slabs
    half = G // 2
    window = window_of(slabs)
    own, spilt = plane_rows(slabs, subs)
    odd, even = frequency_rows("odd"), frequency_rows("even")
    kz = (slabs * (lax.broadcasted_iota(jnp.int32, (G, 1), 0) // grid_y) + slab).astype(jnp.float32)
    for part in range(2):
        wait_part(part)
        got = from_tiles(got_ref, part)
        phi = got[:, : 2 * LANES]
        along_x = [half_of(odd, part) * half_of(phi, n) for n in range(2)]
        if part == 1:
            last = unpack_columns(few_ref)
            along_x = [v + half_of(even, part) * last[:, n : n + 1] for n, v in enumerate(along_x)]
        lhs = jnp.concatenate([jnp.concatenate(along_x, axis=1), got[:, 2 * LANES : 4 * LANES], kz * phi], axis=0)
        rows = slice(part * 2 * LANES, (part + 1) * 2 * LANES)
        field = dot3(split(lhs), (wt_ref[rows], wl_ref[rows]))
        for t in range(2 * G // LANES):
            where = pl.ds(3 * t * G, 3 * G)
            value = field[:, t * LANES : (t + 1) * LANES]
            field_ref[where, :] = value if part == 0 else field_ref[where, :] + value
    sel = sel_ref[...]
    top, low = split(last)
    expanded = jnp.dot(top, sel, preferred_element_type=jnp.float32) + jnp.dot(
        low, sel, preferred_element_type=jnp.float32
    )
    pair = ((lanes_of((grid_y, 4 * LANES)) & (LANES - 1)) - lax.rem(slab, 2) * (2 * subs)) >> 1
    mids = jnp.zeros((grid_y, 4 * LANES), jnp.float32)
    for j in range(subs):
        mids = mids + jnp.where(pair == j, expanded[j * grid_y : (j + 1) * grid_y], 0.0)
    k = slab // 2 * LANES + (lanes_of((1, 2 * LANES)) & (LANES - 1))
    signed = jnp.where(k < half, k, k - G).astype(jnp.float32)
    mid_phi = mids[:, : 2 * LANES]
    mid_lhs = jnp.concatenate([signed * mid_phi, mids[:, 2 * LANES :], -float(half) * mid_phi], axis=0)
    mid_field = dot3(split(mid_lhs), (mt_ref[...], ml_ref[...]))
    row = rows_of((8, G))
    for y in range(grid_y):
        rows = []
        for c in range(3):
            for part in range(2):
                tiles = [
                    field_ref[pl.ds((3 * (part * G // LANES + t) + c) * G + y, subs, stride=grid_y), :]
                    for t in range(G // LANES)
                ]
                rows.append(jnp.concatenate(tiles, axis=1))
        mid = jnp.zeros((8, G), jnp.float32)
        for c in range(3):
            mid = jnp.where(row == c, mid_field[c * grid_y + y : c * grid_y + y + 1], mid)
        here_ref[y] = jnp.concatenate(rows + [mid, jnp.zeros((8, G), jnp.float32)], axis=0)
    lane = lanes_of((here_ref.shape[1], LANES))
    for block in range(slabs):
        turned = [pltpu.roll(here_ref[y], (window * y - grid_x * block) % G, 1) for y in range(grid_y)]
        tiles = []
        for t in range(own // LANES):
            value = jnp.zeros(lane.shape, jnp.float32)
            for y in range(grid_y):
                low_lane = window * y - LANES * t
                if low_lane + window <= 0 or low_lane >= LANES:
                    continue
                side = t * LANES % G
                inside = jnp.logical_and(lane >= low_lane, lane < low_lane + window)
                value = jnp.where(inside, turned[y][:, side : side + LANES], value)
            tiles.append(value)
        height = tiles[0].shape[0]
        lhs_ref[block, :height], lhs_ref[block, height:] = split(jnp.concatenate(tiles, axis=1))

    for part in (1, 0):
        start, rows = (own, spilt) if part else (0, own)

        def one(n, _):
            block = lax.rem(slab + n, slabs)
            at = part * slabs + block
            zh = zh_ref[at]
            lhs = lhs_ref[block, :, :rows]
            top, low = (ref[block, start : start + rows] for ref in (top_ref, low_ref))
            mixed = jnp.dot(lhs, top, preferred_element_type=jnp.float32)
            mixed = (mixed[:height] + mixed[height:]) + jnp.dot(
                lhs[:height], low, preferred_element_type=jnp.float32
            )
            for c in range(3):
                base = 2 * subs * c
                value = jnp.sum(mixed[base : base + 2 * subs] * zh[: 2 * subs], axis=0, keepdims=True)
                row = 6 * subs + c
                out_ref[at, c : c + 1] = value + mixed[row : row + 1] * zh[2 * subs : 2 * subs + 1]
            if part:
                send_share(part, n)
            else:

                @pl.when(n < slabs)
                def _():
                    send_share(part, n)

            return 0

        lax.fori_loop(1 - part, slabs + 1 - part, one, 0)


def kernel_planes(slabs, subs, slab, sub, planes_ref, mids_ref, even_ref, odd_ref, mid_ref):
    half = G // 2
    width_sq = G / 4.0 * (G / 4.0)
    scale = -recip_scale / (float(G) ** 3)
    flip = ((rows_of((G, G)) + lanes_of((G, G))) & (G - 1)) == 0
    flip = flip.astype(jnp.float32).astype(jnp.bfloat16)

    def product(a, b):
        return jnp.dot(a, b, preferred_element_type=jnp.float32)

    top, low = split(planes_ref[1])
    top, low = split(product(flip, top) + product(flip, low))
    mirrored = product(top, flip) + product(low, flip)
    first = planes_ref[0]
    kx, ky = frequency_rows("signed"), frequency_columns("signed")
    kz_here = slabs * sub + slab
    kz = kz_here.astype(jnp.float32)
    freq_sq = kx * kx + ky * ky + kz * kz
    anchor = freq_sq == 0.0
    gauss = jnp.where(
        anchor, 0.0, scale * jnp.exp(freq_sq * (-0.5 / width_sq)) / jnp.where(anchor, 1.0, freq_sq)
    )
    flat = kz_here == 0
    even_ref[...] = gauss * jnp.where(flat, first, first + mirrored)
    odd_ref[...] = gauss * jnp.where(flat, first, first - mirrored)
    rows = G // slabs
    tall = [
        jnp.concatenate([mids_ref[s]] * (LANES // 8), axis=0).T[:rows] for s in range(slabs)
    ]
    tall = jnp.concatenate(tall, axis=0)
    lane = lanes_of(tall.shape)
    chosen = lax.rem(2 * sub, 8)
    columns = [jnp.sum(jnp.where(lane == chosen + t, tall, 0.0), axis=1, keepdims=True) for t in range(2)]
    kx = 2 * (subs * slab + sub) + (lane & 1)
    kx = jnp.where(kx < half, kx, kx - G).astype(jnp.float32)
    mid_sq = kx * kx + ky * ky + float(half * half)
    value = jnp.where((lane & 1) == 0, columns[0], columns[1])
    value = jnp.where(jnp.logical_and(lane >= 2, lane < 6), value, 0.0)
    mid_ref[...] = value * (scale * jnp.exp(mid_sq * (-0.5 / width_sq)) / mid_sq)


def near_columns(positions, near_ref):
    for t in range(positions.shape[1] // LANES):
        tile = positions[:, t * LANES : (t + 1) * LANES]
        near_ref[t * LANES : (t + 1) * LANES, :] = jnp.concatenate([tile] * (LANES // 8), axis=0).T


def own_cells(own_ref, table_ref):
    for t in range(own_ref.shape[1] // LANES):
        tile = own_ref[:, t * LANES : (t + 1) * LANES]
        other = pltpu.roll(tile, LANES // 2, 1)
        first = lanes_of(tile.shape) < LANES // 2
        table_ref[2 * t] = jnp.where(first, tile, other)
        table_ref[2 * t + 1] = jnp.where(first, other, tile)


def pair_field(first, last, list_ref, count_ref, table_ref, near_ref, pair_ref):
    entries = list_ref.shape[1]
    width = LANES // 2
    first_half = lanes_of((8, LANES)) < width
    is_moment = rows_of((8, LANES)) < 3
    itself = rows_of((width, LANES)) == lanes_of((width, LANES))

    def one_cell(cell, _):
        base = pl.multiple_of(cell * width, width)
        near = near_ref[pl.ds(base, width), :]
        near_x, near_y, near_z = (
            jnp.broadcast_to(near[:, 3 + a : 4 + a], (width, LANES)) for a in range(3)
        )
        count = count_ref[cell]

        def terms(pair, masked):
            one = table_ref[list_ref[cell, 2 * pair]]
            two = table_ref[list_ref[cell, 2 * pair + 1]]
            live_one = jnp.where(2 * pair < count, 1.0, 0.0)
            live_two = jnp.where(2 * pair + 1 < count, 1.0, 0.0)
            far = jnp.where(first_half, one, two)
            far = jnp.where(is_moment, far * jnp.where(first_half, live_one, live_two), far)
            mx, my, mz = far[0:1], far[1:2], far[2:3]
            dx = near_x - far[3:4]
            dy = near_y - far[4:5]
            dz = near_z - far[5:6]
            softened = dx * dx + dy * dy + dz * dz + damping
            inverse = lax.rsqrt(softened)
            square = inverse * inverse
            cube = square * inverse
            if masked:
                cube = jnp.where(itself, 0.0, cube)
            radial = (3.0 * (dx * mx + dy * my + dz * mz)) * (cube * square)
            return radial * dx - cube * mx, radial * dy - cube * my, radial * dz - cube * mz

        def step(pair, totals):
            return tuple(t + a for t, a in zip(totals, terms(pair, False)))

        totals = lax.fori_loop(1, entries // 2, step, terms(0, True))
        sums = [jnp.sum(t, axis=1, keepdims=True) for t in totals]
        lane = lanes_of((width, LANES))
        pair_ref[pl.ds(base, width), :] = jnp.where(
            lane == 0, sums[0], jnp.where(lane == 1, sums[1], jnp.where(lane == 2, sums[2], 0.0))
        )
        return 0

    lax.fori_loop(first, last, one_cell, 0)


def around(slabs, subs):
    slab, sub = lax.axis_index("slab"), lax.axis_index("sub")
    up, down = lax.rem(sub + 1, subs), lax.rem(sub + subs - 1, subs)
    turns = [lax.rem(slab + k, slabs) for k in range(slabs)]
    return slab, sub, up, down, turns


def remote(source, target, send_sem, recv_sem, device):
    return pltpu.make_async_remote_copy(
        src_ref=source,
        dst_ref=target,
        send_sem=send_sem,
        recv_sem=recv_sem,
        device_id=device,
        device_id_type=MESH,
    )


def landed(ref, sem):
    pltpu.make_async_copy(ref, ref, sem).wait()


INPUTS = (
    ["cells", "counts", "sends", "pol", "perm", "pos", "frac", "base"]
    + ["phase_t", "phase_l", "bm_t", "bm_l", "gather", "expand", "influence"]
    + ["tx_t", "tx_l", "bx_t", "bx_l", "ty_t", "ty_l", "by_t", "by_l"]
)
TWIDDLES = INPUTS[-8:]
SMEM_INPUTS = 3


class Refs:
    def __init__(self, names, refs):
        for name, ref in zip(names, refs, strict=True):
            setattr(self, name, ref)


def whole_kernel(slabs, subs, names, *refs):
    r = Refs(names, refs)
    slab, sub, up, down, turns = around(slabs, subs)
    depth, rows = r.moved.shape[0], r.moved.shape[1]
    half = slabs * subs
    middle = subs // 2
    group = 2 * subs

    barrier = pltpu.get_barrier_semaphore()

    def greet(to_slab, to_sub):
        pl.semaphore_signal(barrier, inc=1, device_id=(to_slab, to_sub), device_id_type=MESH)

    def folded_of(kz):
        upper = kz >= half
        folded = jnp.where(upper, lax.rem(2 * half - kz, half), kz)
        return folded, jnp.where(upper, 1, 0)

    for t in turns[1:]:
        greet(t, sub)
    for t in turns:
        greet(t, up)
        greet(t, down)

    def greet_sub(k, _):
        greet(slab, lax.rem(sub + k, subs))
        return 0

    lax.fori_loop(2, subs - 1, greet_sub, 0)
    here_kz = slabs * sub + slab
    expected = 3 * slabs - 1 + subs - 3
    for kz in (here_kz, jnp.where(here_kz == 0, half, 2 * half - here_kz)):
        from_sub = lax.div(kz, depth)
        for t in range(slabs):
            other = jnp.logical_or(from_sub != sub, slab != t)

            @pl.when(other)
            def _():
                greet(t, from_sub)

    for i in range(depth):
        folded, _ = folded_of(depth * sub + i)
        mine = jnp.logical_and(lax.rem(folded, slabs) == slab, lax.div(folded, slabs) == sub)
        expected = expected + jnp.where(mine, 0, 1)
    moves = [
        pltpu.make_async_copy(r.influence.at[:, :, pl.ds(h * LANES, LANES)], r.raw.at[h], r.move.at[h])
        for h in range(G // LANES)
    ]
    loads = [
        pltpu.make_async_copy(getattr(r, name), getattr(r, "in_" + name), r.load.at[n])
        for n, name in enumerate(TWIDDLES)
    ]
    for move in [*moves, *loads]:
        move.start()

    def to_group(source, target, send_sem, recv_sem):
        goals = [(t, sub, slab) for t in turns[1:]] + [(t, up, slabs + slab) for t in turns]
        return [
            remote(source, target.at[slot], send_sem.at[n], recv_sem.at[slot], (to_slab, to_sub))
            for n, (to_slab, to_sub, slot) in enumerate(goals)
        ]

    def ghost_copies(it):
        goals = [(slab, up), (slab, down), (turns[1], sub), (turns[-1], sub)]
        ghosts = r.ghosts.shape[2]
        return [
            remote(
                r.ghosts.at[it, q],
                r.landing.at[it, pl.ds(q * ghosts, ghosts)],
                r.ghost_send.at[q],
                r.ghost_recv.at[it, q],
                goal,
            )
            for q, goal in enumerate(goals)
        ]

    def build_cells(it):
        r.body[0:3] = r.own[0:3]
        own_cells(r.body, r.own_tiles)
        r.tables[: r.cells.shape[0]] = r.own_tiles[...]
        ghosts = r.ghosts.shape[2]
        for q in range(4):
            for slot in range(ghosts):
                r.ghosts[it, q, slot] = r.own_tiles[r.sends[0, q, slot]]

    def send_ghosts(it):
        for copy in ghost_copies(it):
            copy.start()

    def send_moments(it):
        for copy in to_group(r.own, r.mom.at[it], r.mom_send, r.mom_recv.at[it]):
            copy.start()
        r.mom[it, slab] = r.own[...]

    atoms = r.own.shape[1]
    r.own[0:3] = r.pol[...] * r.perm[...]
    r.own[3:4] = jnp.zeros((1, atoms), jnp.float32)
    r.body[3:6] = r.pos[...]
    r.body[6:8] = jnp.zeros((2, atoms), jnp.float32)
    r.still[slab, 0:3] = r.frac[...]
    r.still[slab, 3:6] = r.base[...].astype(jnp.float32)
    r.still[slab, 6:8] = jnp.zeros((2, atoms), jnp.float32)

    def plane(i):
        folded, slot = folded_of(depth * sub + i)
        to_slab, to_sub = lax.rem(folded, slabs), lax.div(folded, slabs)
        target = r.planes.at[slot, pl.ds(slab * rows, rows)]
        far = remote(
            r.moved.at[i], target, r.plane_send.at[i], r.plane_recv.at[slot, slab], (to_slab, to_sub)
        )
        return far, slot, jnp.logical_and(to_slab == slab, to_sub == sub)

    def here(i, slot):
        return pltpu.make_async_copy(
            r.moved.at[i], r.planes.at[slot, pl.ds(slab * rows, rows)], r.plane_recv.at[slot, slab]
        )

    build_cells(0)
    near_columns(r.body[...], r.near)
    phase = (r.phase_t[slab], r.phase_l[slab])

    def own_table(at):
        tables_of(slabs, subs, r.still, at, False, phase, r.plane_t, r.plane_l, r.zhat)

    own_table(slab)
    for move in moves:
        move.wait()
    raw = r.raw.reshape(G // LANES * rows * depth, LANES)
    for i in range(depth):
        for h in range(G // LANES):
            r.moved[i, :, h * LANES : (h + 1) * LANES] = raw[pl.ds(h * rows * depth + i, rows, stride=depth), :]
    first = r.moved[0]
    r.turned[...] = jnp.concatenate([first] * (LANES // rows), axis=0).T

    pl.semaphore_wait(barrier, expected)
    still_copies = to_group(r.still.at[slab], r.still, r.still_send, r.still_recv)
    for copy in still_copies:
        copy.start()
    send_moments(0)
    send_ghosts(0)
    for i in range(depth):
        far, slot, mine = plane(i)

        @pl.when(mine)
        def _():
            here(i, slot).start()

        @pl.when(jnp.logical_not(mine))
        def _():
            far.start()

    def hop(n):
        return remote(
            r.turned.at[pl.ds(turns[n] * group, group)],
            r.hop.at[slab],
            r.hop_send.at[n - 1],
            r.hop_recv.at[slab],
            (turns[n], sub),
        )

    def mid(n):
        to_sub = lax.rem(middle + n, subs)
        return remote(
            r.hop.at[:, pl.ds(lax.div(to_sub, 4) * 8, 8)],
            r.mids,
            r.mid_send.at[n - 1],
            r.mid_recv,
            (slab, to_sub),
        )

    @pl.when(sub == middle)
    def _():
        for n in range(1, slabs):
            hop(n).start()
        r.hop[slab] = r.turned[pl.ds(pl.multiple_of(slab * group, group), group)]

    def tables(before):
        def one(n, _):
            block = lax.rem(slab + n, slabs)
            at = block + slabs if before else block

            landed(r.still.at[at], r.still_recv.at[at])
            tables_of(slabs, subs, r.still, block, before, phase, r.plane_t, r.plane_l, r.zhat)
            return 0

        lax.fori_loop(0 if before else 1, slabs, one, 0)

    tables(False)

    @pl.when(sub == middle)
    def _():
        for t in turns[1:]:
            landed(r.hop.at[t], r.hop_recv.at[t])
        for n in range(1, subs):
            mid(n).start()
        r.mids[...] = r.hop[:, (middle // 4) * 8 : (middle // 4) * 8 + 8]

    tables(True)
    for load in loads:
        load.wait()

    def exchange(send, few, got, got_few, part, send_sem, recv_sem):
        first, count = part_rows(part, send.shape[1] // TILES)
        rows = pl.ds(first, count)

        def all_to_all(sources, targets, n):
            pltpu.make_async_copy(sources(sub), targets, recv_sem.at[n]).start()

            def one(k, _):
                to_sub = lax.rem(sub + k, subs)
                remote(sources(to_sub), targets, send_sem.at[n], recv_sem.at[n], (slab, to_sub)).start()
                return 0

            lax.fori_loop(1, subs, one, 0)

        if part == 1:
            all_to_all(lambda to: few.at[to], got_few.at[sub], 2)
        all_to_all(lambda to: send.at[to, rows], got.at[sub, rows], part)

    def exchanged(got, got_few, part, recv_sem):
        first, count = part_rows(part, got.shape[1] // TILES)
        landed(got.at[:, pl.ds(first, count)], recv_sem.at[part])
        if part == 1:
            landed(got_few, recv_sem.at[2])

    def iteration(it, _):
        density(
            slabs,
            subs,
            slab,
            r.mom.at[it],
            r.plane_t,
            r.plane_l,
            r.zhat,
            r.grid,
            lambda slot: landed(r.mom.at[it, slot], r.mom_recv.at[it, slot]),
        )
        got_a, got_b = r.got_a.at[it], r.got_b.at[it]
        few_a, few_b = r.got_few_a.at[it], r.got_few_b.at[it]
        first_frequency(
            slabs,
            subs,
            slab,
            r.grid,
            r.in_tx_t,
            r.in_tx_l,
            r.gather,
            r.send_a,
            r.few_a,
            r.edge,
            r.mid_rows,
            lambda part: exchange(r.send_a, r.few_a, got_a, few_a, part, r.a_send, r.a_recv.at[it]),
        )

        @pl.when(it == 0)
        def _():
            @pl.when(sub != middle)
            def _():
                landed(r.mids, r.mid_recv)

            for slot in range(2):
                for source in range(slabs):
                    landed(r.planes.at[slot, pl.ds(source * rows, rows)], r.plane_recv.at[slot, source])
            kernel_planes(slabs, subs, slab, sub, r.planes, r.mids, r.even, r.odd, r.mid_tile)

        cells, ghosts = r.cells.shape[0], r.ghosts.shape[2]
        for q in range(4):
            landed(r.landing.at[it, pl.ds(q * ghosts, ghosts)], r.ghost_recv.at[it, q])
        r.tables[cells:] = r.landing[it]
        cuts = [0, 3 * cells // 8, 5 * cells // 8, cells]

        def pairs(step):
            pair_field(cuts[step], cuts[step + 1], r.cells, r.counts, r.tables, r.near, r.pair)

        def sent_back(part):
            exchange(r.send_b, r.few_b, got_b, few_b, part, r.b_send, r.b_recv.at[it])
            pairs(1 + part)

        pairs(0)

        second(
            got_a,
            few_a,
            r.even,
            r.odd,
            r.mid_tile,
            r.in_ty_t,
            r.in_ty_l,
            r.in_by_t,
            r.in_by_l,
            r.send_b,
            r.few_b,
            lambda part: exchanged(got_a, few_a, part, r.a_recv.at[it]),
            sent_back,
        )
        for t in range(atoms // LANES):
            tile = r.pair[t * LANES : (t + 1) * LANES, :].T[:8]
            r.rest[:, t * LANES : (t + 1) * LANES] = tile
        r.rest[0:3] += r.perm[...]

        def share_copy(part, n):
            to_slab = lax.rem(slab + n, slabs)
            slot = part * slabs + slab
            return remote(
                r.share.at[part * slabs + to_slab],
                r.land.at[it, slot],
                r.share_send.at[part * (slabs - 1) + n - 1 + part],
                r.share_recv.at[it, slot],
                (to_slab, down if part else sub),
            )

        sample(
            slabs,
            subs,
            slab,
            got_b,
            few_b,
            r.plane_t,
            r.plane_l,
            r.zhat,
            r.in_bx_t,
            r.in_bx_l,
            r.bm_t.at[slab // 2],
            r.bm_l.at[slab // 2],
            r.expand,
            r.share,
            r.field,
            r.here,
            r.lhs,
            lambda part: exchanged(got_b, few_b, part, r.b_recv.at[it]),
            lambda part, n: share_copy(part, n).start(),
        )
        total = r.rest[0:3] + r.share[slab, 0:3]
        for slot in [*turns[1:], *(slabs + k for k in range(slabs))]:
            landed(r.land.at[it, slot], r.share_recv.at[it, slot])
            total = total + r.land[it, slot, 0:3]
        for copy in to_group(r.own, r.mom.at[it], r.mom_send, r.mom_recv.at[it]):
            copy.wait_send()
        for copy in ghost_copies(it):
            copy.wait_send()
        r.own[0:3] = r.pol[...] * total

        @pl.when(it + 1 < ITERS)
        def _():
            send_moments(it + 1)
            build_cells(it + 1)
            send_ghosts(it + 1)

        for n in range(1, slabs):
            share_copy(0, n).wait_send()
        for n in range(slabs):
            share_copy(1, n).wait_send()
        for part in range(2):
            rows_sent = pl.ds(*part_rows(part, r.send_a.shape[1] // TILES))
            landed(r.send_a.at[pl.ds(0, subs - 1), rows_sent], r.a_send.at[part])
            landed(r.send_b.at[pl.ds(0, subs - 1), rows_sent], r.b_send.at[part])
        landed(r.few_a.at[pl.ds(0, subs - 1)], r.a_send.at[2])
        landed(r.few_b.at[pl.ds(0, subs - 1)], r.b_send.at[2])
        return 0

    lax.fori_loop(0, ITERS, iteration, 0)
    r.out[...] = r.own[0:3]
    for copy in still_copies:
        copy.wait_send()

    @pl.when(sub == middle)
    def _():
        for n in range(1, slabs):
            hop(n).wait_send()
        for n in range(1, subs):
            mid(n).wait_send()

    for i in range(depth):
        far, slot, mine = plane(i)

        @pl.when(jnp.logical_not(mine))
        def _():
            far.wait_send()


def shards(
    positions,
    fraction,
    grid_base,
    polarizability,
    perm_field,
    influence,
    neighbour_cells,
    neighbour_count,
    send_cells,
):
    atoms = positions.shape[1]
    cells = neighbour_cells.shape[0]
    ghosts = send_cells.shape[2]
    slabs = lax.axis_size("slab")
    subs = lax.axis_size("sub")
    grid_x = G // slabs
    grid_y = G // subs
    depth = G // subs

    index = np.arange(G)
    angle = (index[:, None] * index[None, :] % G) * (2.0 * np.pi / G)
    kz_rows = np.arange(slabs)[:, None] + slabs * np.arange(subs)[None, :]
    turn = kz_rows[:, :, None] * index[None, None, :] % G * (2.0 * np.pi / G)
    ranks = 2 * subs + 8
    phase = np.zeros((slabs, ranks, G), np.float32)
    phase[:, :subs] = np.cos(turn)
    phase[:, subs : 2 * subs] = -np.sin(turn)
    phase[:, 2 * subs] = np.where(index % 2 == 0, 1.0, -1.0)
    cos_np, sin_np = np.cos(angle), np.sin(angle)
    halves = np.concatenate([index[:LANES], G + index[:LANES], index[LANES:], G + index[LANES:]])
    turn_x = parts_of(np.block([[cos_np, -sin_np], [sin_np, cos_np]])[:, halves])
    back_x = parts_of(np.block([[cos_np, sin_np], [-sin_np, cos_np]])[halves])
    turn_y = parts_of(np.concatenate([cos_np, sin_np], axis=1))
    back_y = parts_of(np.concatenate([cos_np, -sin_np], axis=1))
    wide = np.stack(
        [np.concatenate([cos_np[w : w + LANES], -sin_np[w : w + LANES]], axis=0) for w in range(0, G, LANES)]
    )
    phase, back_mid = parts_of(phase), parts_of(wide)
    select = np.zeros((4, LANES, LANES), np.float32)
    for q in range(4):
        for lane in range(LANES):
            select[q, lane, 2 + 2 * q + lane % 2] = 1.0
    gather = jnp.asarray(select.reshape(4 * LANES, LANES), jnp.bfloat16)
    expand = jnp.asarray(np.concatenate(list(select.transpose(0, 2, 1)), axis=1), jnp.bfloat16)

    operands = [
        neighbour_cells,
        neighbour_count,
        send_cells,
        polarizability[None, :],
        perm_field,
        positions,
        fraction,
        grid_base,
        *phase,
        *back_mid,
        gather,
        expand,
        influence,
        *turn_x,
        *back_x,
        *turn_y,
        *back_y,
    ]
    vmem = pl.BlockSpec(memory_space=pltpu.VMEM)
    smem = pl.BlockSpec(memory_space=pltpu.SMEM)
    far = len(TWIDDLES) + 1
    specs = [smem] * SMEM_INPUTS + [vmem] * (len(operands) - SMEM_INPUTS - far)
    specs += [pl.BlockSpec(memory_space=pl.ANY)] * far

    def held(*shape, dtype=jnp.float32):
        return pltpu.VMEM(shape, dtype)

    held16 = functools.partial(held, dtype=jnp.bfloat16)
    dma = pltpu.SemaphoreType.DMA
    chunk = (subs, TILES * grid_y, LANES)
    columns = 6 * subs + 16
    sends = 2 * slabs - 1
    planes = sum(plane_rows(slabs, subs))
    scratch = dict(
        mom=held(ITERS, 2 * slabs, 4, atoms),
        still=held(2 * slabs, 8, atoms),
        own=held(4, atoms),
        body=held(8, atoms),
        own_tiles=held(cells, 8, LANES),
        tables=held(cells + 4 * ghosts, 8, LANES),
        landing=held(ITERS, 4 * ghosts, 8, LANES),
        ghosts=held(ITERS, 4, ghosts, 8, LANES),
        near=held(atoms, LANES),
        pair=held(atoms, LANES),
        rest=held(8, atoms),
        plane_t=held16(slabs, planes, atoms),
        plane_l=held16(slabs, planes, atoms),
        zhat=held(2 * slabs, ranks, atoms),
        raw=held(G // LANES, grid_x, depth, LANES),
        moved=held(depth, grid_x, G),
        turned=held(G, LANES),
        hop=held(slabs, grid_x, LANES),
        planes=held(2, G, G),
        mids=held(slabs, 8, LANES),
        even=held(G, G),
        odd=held(G, G),
        mid_tile=held(G, LANES),
        grid=held(grid_y, G + 8, 256),
        mid_rows=held(4, grid_y, G),
        send_a=held(*chunk),
        got_a=held(ITERS, *chunk),
        few_a=held(subs, 1, LANES),
        got_few_a=held(ITERS, subs, 1, LANES),
        few_b=held(subs, 1, LANES),
        got_few_b=held(ITERS, subs, 1, LANES),
        edge=held(G, LANES),
        send_b=held(*chunk),
        got_b=held(ITERS, *chunk),
        field=held(6 * G * G // LANES, LANES),
        here=held(grid_y, columns, G),
        lhs=held16(slabs, 2 * columns, plane_rows(slabs, subs)[0]),
        share=held(2 * slabs, 4, atoms),
        land=held(ITERS, 2 * slabs, 4, atoms),
        **{
            "in_" + name: held16(*operand.shape)
            for name, operand in zip(TWIDDLES, operands[-len(TWIDDLES) :], strict=True)
        },
        load=dma((len(TWIDDLES),)),
        mom_send=dma((sends,)),
        mom_recv=dma((ITERS, 2 * slabs)),
        still_send=dma((sends,)),
        still_recv=dma((2 * slabs,)),
        ghost_send=dma((4,)),
        ghost_recv=dma((ITERS, 4)),
        move=dma((G // LANES,)),
        plane_send=dma((depth,)),
        plane_recv=dma((2, slabs)),
        hop_send=dma((slabs - 1,)),
        hop_recv=dma((slabs,)),
        mid_send=dma((subs - 1,)),
        mid_recv=dma,
        a_send=dma((3,)),
        a_recv=dma((ITERS, 3)),
        b_send=dma((3,)),
        b_recv=dma((ITERS, 3)),
        share_send=dma((sends,)),
        share_recv=dma((ITERS, 2 * slabs)),
    )
    names = [*INPUTS, "out", *scratch]
    return pl.pallas_call(
        functools.partial(whole_kernel, slabs, subs, names),
        out_shape=jax.ShapeDtypeStruct((3, atoms), jnp.float32),
        in_specs=specs,
        out_specs=vmem,
        scratch_shapes=list(scratch.values()),
        compiler_params=pltpu.CompilerParams(vmem_limit_bytes=60 << 20, collective_id=0, has_side_effects=True),
        name="dipoles",
    )(*operands)


def solution(mesh):
    in_specs = (
        P(None, ("slab", "sub")),
        P(None, ("slab", "sub")),
        P(None, ("slab", "sub")),
        P(("slab", "sub")),
        P(None, ("slab", "sub")),
        P("slab", "sub", None),
        P(("slab", "sub"), None),
        P(("slab", "sub")),
        P(("slab", "sub"), None, None),
    )
    out_specs = P(None, ("slab", "sub"))
    return jax.shard_map(shards, mesh=mesh, in_specs=in_specs, out_specs=out_specs, check_vma=False)
```

```python
import functools
import math

import jax
import jax.numpy as jnp
import numpy as np
from jax import lax
from jax.experimental import pallas as pl
from jax.experimental.pallas import tpu as pltpu
from jax.sharding import PartitionSpec as P

G = 256
ITERS = 2

damping = 1.0
recip_scale = 16.0
highest = lax.Precision.HIGHEST
LANES = 128
TILES = 4 * G // LANES
MESH = pl.DeviceIdType.MESH


def spline_weights(fraction):
    square = fraction * fraction
    cube = square * fraction
    rest = 1.0 - fraction
    return [
        rest * rest * rest / 6.0,
        (3.0 * cube - 6.0 * square + 4.0) / 6.0,
        (-3.0 * cube + 3.0 * square + 3.0 * fraction + 1.0) / 6.0,
        cube / 6.0,
    ]


def split(x):
    top = x.astype(jnp.bfloat16)
    return top, (x - top.astype(jnp.float32)).astype(jnp.bfloat16)


def dot3(a, b, turned=False):
    dims = (((1,), (1 if turned else 0,)), ((), ()))

    left = jnp.concatenate([a[1], a[0], a[0]], axis=1)
    right = jnp.concatenate([b[0], b[1], b[0]], axis=1 if turned else 0)
    return lax.dot_general(left, right, dims, preferred_element_type=jnp.float32)


def parts_of(table):
    table = np.asarray(table, np.float32)
    top = table.astype(jnp.bfloat16)
    low = (table - top.astype(np.float32)).astype(jnp.bfloat16)
    return jnp.asarray(top), jnp.asarray(low)


def lanes_of(shape):
    return lax.broadcasted_iota(jnp.int32, shape, len(shape) - 1)


def rows_of(shape):
    return lax.broadcasted_iota(jnp.int32, shape, len(shape) - 2)


def window_of(slabs):
    return G // slabs + 8


def plane_rows(slabs, subs):
    window = window_of(slabs)
    return tuple(-(-count * window // LANES) * LANES for count in (G // subs, 3))


def tables_of(slabs, subs, still_ref, block, before, phase, top_ref, low_ref, zh_ref):
    at = block + slabs if before else block
    still = still_ref[at]
    atoms = still.shape[1]

    def table(axis, length):
        offset = rows_of((length, atoms)) - still[3 + axis : 4 + axis].astype(jnp.int32)
        total = jnp.zeros(offset.shape, jnp.float32)
        for stencil, weight in enumerate(spline_weights(still[axis : 1 + axis])):
            total = jnp.where(offset == stencil, weight, total)
        return total

    along_x, along_y = table(0, window_of(slabs)), table(1, 16)
    grid_y = G // subs
    first, count = (grid_y, 3) if before else (0, grid_y)
    own, spilt = plane_rows(slabs, subs)
    start, rows = (own, spilt) if before else (0, own)
    blank = jnp.zeros((rows - count * along_x.shape[0], atoms), jnp.float32)
    plane = [along_x * along_y[first + y : first + y + 1] for y in range(count)]
    top, low = split(jnp.concatenate([*plane, blank], axis=0))
    top_ref[block, start : start + rows] = top
    low_ref[block, start : start + rows] = low
    z0 = still[5:6].astype(jnp.int32)
    chosen = (rows_of((G, atoms)) == z0).astype(jnp.float32).astype(jnp.bfloat16)
    start = jnp.dot(phase[0], chosen, preferred_element_type=jnp.float32) + jnp.dot(
        phase[1], chosen, preferred_element_type=jnp.float32
    )
    steps = phase[0][:, :LANES].astype(jnp.float32) + phase[1][:, :LANES].astype(jnp.float32)
    wide = [jnp.zeros((subs, atoms), jnp.float32)] * 2
    mid = jnp.zeros((1, atoms), jnp.float32)
    for t, weight in enumerate(spline_weights(still[2:3])):
        wide = [v + weight * steps[n * subs : (n + 1) * subs, t : t + 1] for n, v in enumerate(wide)]
        mid = mid + (weight if t % 2 == 0 else -weight)
    re, im = start[:subs], start[subs : 2 * subs]
    zh_ref[at, :subs] = re * wide[0] - im * wide[1]
    zh_ref[at, subs : 2 * subs] = re * wide[1] + im * wide[0]
    zh_ref[at, 2 * subs :] = start[2 * subs :] * mid


def frequency_rows(kind):
    k = lanes_of((1, G))
    signed = jnp.where(k < G // 2, k, k - G).astype(jnp.float32)
    if kind == "odd":
        return jnp.where(k == G // 2, 0.0, signed)
    if kind == "even":
        return jnp.where(k == G // 2, signed, 0.0)
    return signed


def frequency_columns(kind):
    k = lax.broadcasted_iota(jnp.int32, (G, 1), 0)
    signed = jnp.where(k < G // 2, k, k - G).astype(jnp.float32)
    if kind == "odd":
        return jnp.where(k == G // 2, 0.0, signed)
    if kind == "even":
        return jnp.where(k == G // 2, signed, 0.0)
    return signed


def density(slabs, subs, slab, mom_ref, top_ref, low_ref, zh_ref, grid_ref, wait_block):
    grid_y = G // subs
    grid_x = G // slabs
    window = window_of(slabs)
    own, _ = plane_rows(slabs, subs)
    grid_ref[...] = jnp.zeros_like(grid_ref)

    for part in range(2):

        def one(n, _):
            block = lax.rem(slab + n, slabs)
            at = block + part * slabs
            if part == 0:

                @pl.when(n > 0)
                def _():
                    wait_block(at)

            else:
                wait_block(at)
            mu = mom_ref[at]
            zh = zh_ref[at]
            row = rows_of((8, mu.shape[1]))
            last = jnp.where(row == 0, mu[0:1], jnp.where(row == 1, mu[1:2], mu[2:3]))
            values = jnp.concatenate(
                [zh[: 2 * subs] * mu[c : c + 1] for c in range(3)] + [last * zh[2 * subs : 2 * subs + 1]], axis=0
            )
            start, count = (0, grid_y) if part == 0 else (own, 3)
            rows = -(-count * window // 16) * 16
            plane = tuple(ref[block, start : start + rows] for ref in (top_ref, low_ref))
            got = dot3(plane, split(values), True)
            columns = values.shape[0]
            for y in range(count):
                where = pl.ds(pl.multiple_of(block * grid_x, grid_x), window)
                grid_ref[y, where, :columns] += got[y * window : (y + 1) * window]
            return 0

        lax.fori_loop(0, slabs, one, 0)
    for y in range(grid_y):
        grid_ref[y, :8] += grid_ref[y, G : G + 8]


def half_of(row, part):
    return row[:, part * LANES : (part + 1) * LANES]


def first_frequency(slabs, subs, slab, grid_ref, wt_ref, wl_ref, sel_ref, out_ref, few_ref, edge_ref, mid_ref, send_part):
    grid_y = G // subs
    half = G // 2
    flat_ref = out_ref.reshape(subs * TILES * grid_y, LANES)
    rows = []
    for y in range(grid_y):
        turned = grid_ref[y, :G].T
        for c in range(3):
            base = 2 * subs * c
            rows.append(
                jnp.concatenate([turned[base : base + subs], turned[base + subs : base + 2 * subs]], axis=1)
            )
        mids = turned[6 * subs : 6 * subs + 8]
        rows.append(jnp.concatenate([mids, jnp.zeros_like(mids)], axis=1))
    lhs = split(jnp.concatenate(rows, axis=0))
    odd, signed = frequency_rows("odd"), frequency_rows("signed")
    kz = (slabs * lax.broadcasted_iota(jnp.int32, (subs, 1), 0) + slab).astype(jnp.float32)
    lane = lanes_of((subs, LANES))
    per_y = 3 * subs + 8

    def transformed(part):
        columns = slice(part * 2 * LANES, (part + 1) * 2 * LANES)
        spec = dot3(lhs, (wt_ref[:, columns], wl_ref[:, columns]))
        for y in range(grid_y):
            at = spec[y * per_y : (y + 1) * per_y]
            sx, sy, sz = (at[c * subs : (c + 1) * subs] for c in range(3))
            tiles = [
                half_of(odd, part) * half_of(sx, n) + kz * half_of(sz, n) for n in range(2)
            ] + [half_of(sy, 0), half_of(sy, 1)]
            if part == 1:
                edge_ref[pl.ds(y, subs, stride=grid_y), :] = -float(half) * jnp.where(
                    lane == 0, sx[:, :1], jnp.where(lane == 1, sx[:, LANES : LANES + 1], 0.0)
                )
            for t, value in enumerate(tiles):
                flat_ref[pl.ds((part * 4 + t) * grid_y + y, subs, stride=TILES * grid_y), :] = value
            mid = at[3 * subs :]
            lanes = slice(part * LANES, (part + 1) * LANES)
            for n in range(2):
                mx, my, mz = (half_of(mid[c : c + 1], n) for c in range(3))
                mid_ref[n, y : y + 1, lanes] = half_of(signed, part) * mx - float(half) * mz
                mid_ref[2 + n, y : y + 1, lanes] = my

    transformed(0)
    send_part(0)
    transformed(1)
    window = pl.ds(pl.multiple_of(slab // 2 * LANES, LANES), LANES)
    pair = (lanes_of((grid_y, LANES)) - lax.rem(slab, 2) * (2 * subs)) >> 1
    columns = []
    for q in range(4):
        value = mid_ref[q, :, window]
        columns.append(jnp.concatenate([jnp.where(pair == j, value, 0.0) for j in range(subs)], axis=0))
    top, low = split(jnp.concatenate(columns, axis=1))
    sel = sel_ref[...]
    more = jnp.dot(top, sel, preferred_element_type=jnp.float32) + jnp.dot(
        low, sel, preferred_element_type=jnp.float32
    )
    pack_columns(edge_ref[...] + more, few_ref)
    send_part(1)


def part_rows(part, high):
    return part * 4 * high, 4 * high


def pack_columns(value, ref):
    spread = pltpu.roll(value, 0, 1, stride=LANES // 8, stride_axis=0)
    rows = jnp.sum(spread.reshape(ref.shape[0], 8, LANES), axis=1)
    for block in range(ref.shape[0]):
        ref[block] = rows[block : block + 1]


def unpack_columns(ref):
    rows = jnp.concatenate([jnp.broadcast_to(ref[block], (8, LANES)) for block in range(ref.shape[0])], axis=0)
    y = rows_of(rows.shape) & 7
    back = rows
    for n in range(1, 8):
        back = jnp.where(y == n, pltpu.roll(rows, LANES - n * (LANES // 8), 1), back)
    return jnp.where(lanes_of(back.shape) < LANES // 8, back, 0.0)


def from_tiles(ref, part):
    blocks, rows, lanes = ref.shape
    high = rows // TILES
    first, count = part_rows(part, high)
    return jnp.concatenate(
        [ref[:, r : r + high, :].reshape(blocks * high, lanes) for r in range(first, first + count, high)], axis=1
    )


def to_tiles(value, ref, part):
    blocks, rows, lanes = ref.shape
    high = rows // TILES
    first, count = part_rows(part, high)
    for t in range(count // high):
        ref[:, first + t * high : first + (t + 1) * high, :] = value[:, t * lanes : (t + 1) * lanes].reshape(
            blocks, high, lanes
        )


def with_swapped(x):
    def tile(v, t):
        return v[:, t * LANES : (t + 1) * LANES]

    both = [
        jnp.concatenate([v, jnp.concatenate([tile(v, 1), -tile(v, 0), tile(v, 3), -tile(v, 2)], axis=1)], axis=0)
        for v in split(x[:, : 4 * LANES])
    ]
    if x.shape[1] > 4 * LANES:
        last = x[:, 4 * LANES :]
        lane = lanes_of(last.shape)
        back, on = pltpu.roll(last, LANES - 1, 1), pltpu.roll(last, 1, 1)
        back2, on2 = pltpu.roll(last, LANES - 2, 1), pltpu.roll(last, 2, 1)
        upper = ((lane - 2) & 2) == 0
        turned = jnp.where(lane == 0, back, jnp.where(lane == 1, -on, jnp.where(upper, back2, -on2)))
        more = split(jnp.concatenate([last, turned], axis=0))
        both = [jnp.concatenate([a, b], axis=1) for a, b in zip(both, more)]
    return tuple(both)


def second(got_ref, few_ref, even_ref, odd_ref, mid_ref, ft_ref, fl_ref, bt_ref, bl_ref, out_ref, few_out_ref, wait_part, send_part):
    forward, backward = (ft_ref[...], fl_ref[...]), (bt_ref[...], bl_ref[...])
    odd_y, even_y, full_y = (frequency_columns(k) for k in ("odd", "even", "signed"))
    for part in range(2):
        wait_part(part)
        got = from_tiles(got_ref, part)
        if part == 1:
            got = jnp.concatenate([got, unpack_columns(few_ref)], axis=1)
        spec = dot3(forward, with_swapped(got))
        lanes = slice(part * LANES, (part + 1) * LANES)
        kernel_even, kernel_odd = even_ref[:, lanes], odd_ref[:, lanes]
        lane = lanes_of(kernel_even.shape)
        last = spec[:, 4 * LANES :]
        tiles, columns = [None] * 4, []
        for n in range(2):
            a = spec[:, n * LANES : (n + 1) * LANES]
            b = spec[:, (2 + n) * LANES : (3 + n) * LANES]
            level = a + odd_y * b
            edge = even_y * b
            if part == 1:
                edge = edge + jnp.where(lane == 0, last[:, n : n + 1], 0.0)
            phi = kernel_even * level + kernel_odd * edge
            phi_edge = kernel_odd * level + kernel_even * edge
            tiles[n] = phi
            tiles[2 + n] = odd_y * phi + even_y * phi_edge
            columns.append(phi_edge[:, :1])
        if part == 1:
            mid = mid_ref[...] * (last + full_y * pltpu.roll(last, LANES - 4, 1))
            mid = mid + full_y * pltpu.roll(mid, 4, 1)
            tiles.append(jnp.where(lane == 0, columns[0], jnp.where(lane == 1, columns[1], mid)))
        back = dot3(backward, with_swapped(jnp.concatenate(tiles, axis=1)))
        to_tiles(back, out_ref, part)
        if part == 1:
            pack_columns(back[:, 4 * LANES :], few_out_ref)
        send_part(part)


def sample(
    slabs,
    subs,
    slab,
    got_ref,
    few_ref,
    top_ref,
    low_ref,
    zh_ref,
    wt_ref,
    wl_ref,
    mt_ref,
    ml_ref,
    sel_ref,
    out_ref,
    field_ref,
    here_ref,
    lhs_ref,
    wait_part,
    send_share,
):
    grid_y = G // subs
    grid_x = G // slabs
    half = G // 2
    window = window_of(slabs)
    own, spilt = plane_rows(slabs, subs)
    odd, even = frequency_rows("odd"), frequency_rows("even")
    kz = (slabs * (lax.broadcasted_iota(jnp.int32, (G, 1), 0) // grid_y) + slab).astype(jnp.float32)
    for part in range(2):
        wait_part(part)
        got = from_tiles(got_ref, part)
        phi = got[:, : 2 * LANES]
        along_x = [half_of(odd, part) * half_of(phi, n) for n in range(2)]
        if part == 1:
            last = unpack_columns(few_ref)
            along_x = [v + half_of(even, part) * last[:, n : n + 1] for n, v in enumerate(along_x)]
        lhs = jnp.concatenate([jnp.concatenate(along_x, axis=1), got[:, 2 * LANES : 4 * LANES], kz * phi], axis=0)
        rows = slice(part * 2 * LANES, (part + 1) * 2 * LANES)
        field = dot3(split(lhs), (wt_ref[rows], wl_ref[rows]))
        for t in range(2 * G // LANES):
            where = pl.ds(3 * t * G, 3 * G)
            value = field[:, t * LANES : (t + 1) * LANES]
            field_ref[where, :] = value if part == 0 else field_ref[where, :] + value
    sel = sel_ref[...]
    top, low = split(last)
    expanded = jnp.dot(top, sel, preferred_element_type=jnp.float32) + jnp.dot(
        low, sel, preferred_element_type=jnp.float32
    )
    pair = ((lanes_of((grid_y, 4 * LANES)) & (LANES - 1)) - lax.rem(slab, 2) * (2 * subs)) >> 1
    mids = jnp.zeros((grid_y, 4 * LANES), jnp.float32)
    for j in range(subs):
        mids = mids + jnp.where(pair == j, expanded[j * grid_y : (j + 1) * grid_y], 0.0)
    k = slab // 2 * LANES + (lanes_of((1, 2 * LANES)) & (LANES - 1))
    signed = jnp.where(k < half, k, k - G).astype(jnp.float32)
    mid_phi = mids[:, : 2 * LANES]
    mid_lhs = jnp.concatenate([signed * mid_phi, mids[:, 2 * LANES :], -float(half) * mid_phi], axis=0)
    mid_field = dot3(split(mid_lhs), (mt_ref[...], ml_ref[...]))
    row = rows_of((8, G))
    for y in range(grid_y):
        rows = []
        for c in range(3):
            for part in range(2):
                tiles = [
                    field_ref[pl.ds((3 * (part * G // LANES + t) + c) * G + y, subs, stride=grid_y), :]
                    for t in range(G // LANES)
                ]
                rows.append(jnp.concatenate(tiles, axis=1))
        mid = jnp.zeros((8, G), jnp.float32)
        for c in range(3):
            mid = jnp.where(row == c, mid_field[c * grid_y + y : c * grid_y + y + 1], mid)
        here_ref[y] = jnp.concatenate(rows + [mid, jnp.zeros((8, G), jnp.float32)], axis=0)
    lane = lanes_of((here_ref.shape[1], LANES))
    for block in range(slabs):
        turned = [pltpu.roll(here_ref[y], (window * y - grid_x * block) % G, 1) for y in range(grid_y)]
        tiles = []
        for t in range(own // LANES):
            value = jnp.zeros(lane.shape, jnp.float32)
            for y in range(grid_y):
                low_lane = window * y - LANES * t
                if low_lane + window <= 0 or low_lane >= LANES:
                    continue
                side = t * LANES % G
                inside = jnp.logical_and(lane >= low_lane, lane < low_lane + window)
                value = jnp.where(inside, turned[y][:, side : side + LANES], value)
            tiles.append(value)
        height = tiles[0].shape[0]
        lhs_ref[block, :height], lhs_ref[block, height:] = split(jnp.concatenate(tiles, axis=1))

    for part in (1, 0):
        start, rows = (own, spilt) if part else (0, own)

        def one(n, _):
            block = lax.rem(slab + n, slabs)
            at = part * slabs + block
            zh = zh_ref[at]
            lhs = lhs_ref[block, :, :rows]
            top, low = (ref[block, start : start + rows] for ref in (top_ref, low_ref))
            mixed = jnp.dot(lhs, top, preferred_element_type=jnp.float32)
            mixed = (mixed[:height] + mixed[height:]) + jnp.dot(
                lhs[:height], low, preferred_element_type=jnp.float32
            )
            for c in range(3):
                base = 2 * subs * c
                value = jnp.sum(mixed[base : base + 2 * subs] * zh[: 2 * subs], axis=0, keepdims=True)
                row = 6 * subs + c
                out_ref[at, c : c + 1] = value + mixed[row : row + 1] * zh[2 * subs : 2 * subs + 1]
            if part:
                send_share(part, n)
            else:

                @pl.when(n < slabs)
                def _():
                    send_share(part, n)

            return 0

        lax.fori_loop(1 - part, slabs + 1 - part, one, 0)


def kernel_planes(slabs, subs, slab, sub, planes_ref, mids_ref, even_ref, odd_ref, mid_ref):
    half = G // 2
    width_sq = G / 4.0 * (G / 4.0)
    scale = -recip_scale / (float(G) ** 3)
    flip = ((rows_of((G, G)) + lanes_of((G, G))) & (G - 1)) == 0
    flip = flip.astype(jnp.float32).astype(jnp.bfloat16)

    def product(a, b):
        return jnp.dot(a, b, preferred_element_type=jnp.float32)

    top, low = split(planes_ref[1])
    top, low = split(product(flip, top) + product(flip, low))
    mirrored = product(top, flip) + product(low, flip)
    first = planes_ref[0]
    kx, ky = frequency_rows("signed"), frequency_columns("signed")
    kz_here = slabs * sub + slab
    kz = kz_here.astype(jnp.float32)
    freq_sq = kx * kx + ky * ky + kz * kz
    anchor = freq_sq == 0.0
    gauss = jnp.where(
        anchor, 0.0, scale * jnp.exp(freq_sq * (-0.5 / width_sq)) / jnp.where(anchor, 1.0, freq_sq)
    )
    flat = kz_here == 0
    even_ref[...] = gauss * jnp.where(flat, first, first + mirrored)
    odd_ref[...] = gauss * jnp.where(flat, first, first - mirrored)
    rows = G // slabs
    tall = [
        jnp.concatenate([mids_ref[s]] * (LANES // 8), axis=0).T[:rows] for s in range(slabs)
    ]
    tall = jnp.concatenate(tall, axis=0)
    lane = lanes_of(tall.shape)
    chosen = lax.rem(2 * sub, 8)
    columns = [jnp.sum(jnp.where(lane == chosen + t, tall, 0.0), axis=1, keepdims=True) for t in range(2)]
    kx = 2 * (subs * slab + sub) + (lane & 1)
    kx = jnp.where(kx < half, kx, kx - G).astype(jnp.float32)
    mid_sq = kx * kx + ky * ky + float(half * half)
    value = jnp.where((lane & 1) == 0, columns[0], columns[1])
    value = jnp.where(jnp.logical_and(lane >= 2, lane < 6), value, 0.0)
    mid_ref[...] = value * (scale * jnp.exp(mid_sq * (-0.5 / width_sq)) / mid_sq)


def near_columns(positions, near_ref):
    for t in range(positions.shape[1] // LANES):
        tile = positions[:, t * LANES : (t + 1) * LANES]
        near_ref[t * LANES : (t + 1) * LANES, :] = jnp.concatenate([tile] * (LANES // 8), axis=0).T


def own_cells(own_ref, table_ref):
    for t in range(own_ref.shape[1] // LANES):
        tile = own_ref[:, t * LANES : (t + 1) * LANES]
        other = pltpu.roll(tile, LANES // 2, 1)
        first = lanes_of(tile.shape) < LANES // 2
        table_ref[2 * t] = jnp.where(first, tile, other)
        table_ref[2 * t + 1] = jnp.where(first, other, tile)


def pair_field(first, last, list_ref, count_ref, table_ref, near_ref, pair_ref):
    entries = list_ref.shape[1]
    width = LANES // 2
    first_half = lanes_of((8, LANES)) < width
    is_moment = rows_of((8, LANES)) < 3
    itself = rows_of((width, LANES)) == lanes_of((width, LANES))

    def one_cell(cell, _):
        base = pl.multiple_of(cell * width, width)
        near = near_ref[pl.ds(base, width), :]
        near_x, near_y, near_z = (
            jnp.broadcast_to(near[:, 3 + a : 4 + a], (width, LANES)) for a in range(3)
        )
        count = count_ref[cell]

        def terms(pair, masked):
            one = table_ref[list_ref[cell, 2 * pair]]
            two = table_ref[list_ref[cell, 2 * pair + 1]]
            live_one = jnp.where(2 * pair < count, 1.0, 0.0)
            live_two = jnp.where(2 * pair + 1 < count, 1.0, 0.0)
            far = jnp.where(first_half, one, two)
            far = jnp.where(is_moment, far * jnp.where(first_half, live_one, live_two), far)
            mx, my, mz = far[0:1], far[1:2], far[2:3]
            dx = near_x - far[3:4]
            dy = near_y - far[4:5]
            dz = near_z - far[5:6]
            softened = dx * dx + dy * dy + dz * dz + damping
            inverse = lax.rsqrt(softened)
            square = inverse * inverse
            cube = square * inverse
            if masked:
                cube = jnp.where(itself, 0.0, cube)
            radial = (3.0 * (dx * mx + dy * my + dz * mz)) * (cube * square)
            return radial * dx - cube * mx, radial * dy - cube * my, radial * dz - cube * mz

        def step(pair, totals):
            return tuple(t + a for t, a in zip(totals, terms(pair, False)))

        totals = lax.fori_loop(1, entries // 2, step, terms(0, True))
        sums = [jnp.sum(t, axis=1, keepdims=True) for t in totals]
        lane = lanes_of((width, LANES))
        pair_ref[pl.ds(base, width), :] = jnp.where(
            lane == 0, sums[0], jnp.where(lane == 1, sums[1], jnp.where(lane == 2, sums[2], 0.0))
        )
        return 0

    lax.fori_loop(first, last, one_cell, 0)


def around(slabs, subs):
    slab, sub = lax.axis_index("slab"), lax.axis_index("sub")
    up, down = lax.rem(sub + 1, subs), lax.rem(sub + subs - 1, subs)
    turns = [lax.rem(slab + k, slabs) for k in range(slabs)]
    return slab, sub, up, down, turns


def remote(source, target, send_sem, recv_sem, device):
    return pltpu.make_async_remote_copy(
        src_ref=source,
        dst_ref=target,
        send_sem=send_sem,
        recv_sem=recv_sem,
        device_id=device,
        device_id_type=MESH,
    )


def landed(ref, sem):
    pltpu.make_async_copy(ref, ref, sem).wait()


INPUTS = (
    ["cells", "counts", "sends", "pol", "perm", "pos", "frac", "base"]
    + ["phase_t", "phase_l", "bm_t", "bm_l", "gather", "expand", "influence"]
    + ["tx_t", "tx_l", "bx_t", "bx_l", "ty_t", "ty_l", "by_t", "by_l"]
)
TWIDDLES = INPUTS[-8:]
SMEM_INPUTS = 3


class Refs:
    def __init__(self, names, refs):
        for name, ref in zip(names, refs, strict=True):
            setattr(self, name, ref)


def whole_kernel(slabs, subs, names, *refs):
    r = Refs(names, refs)
    slab, sub, up, down, turns = around(slabs, subs)
    depth, rows = r.moved.shape[0], r.moved.shape[1]
    half = slabs * subs
    middle = subs // 2
    group = 2 * subs

    barrier = pltpu.get_barrier_semaphore()

    def greet(to_slab, to_sub):
        pl.semaphore_signal(barrier, inc=1, device_id=(to_slab, to_sub), device_id_type=MESH)

    def folded_of(kz):
        upper = kz >= half
        folded = jnp.where(upper, lax.rem(2 * half - kz, half), kz)
        return folded, jnp.where(upper, 1, 0)

    for t in turns[1:]:
        greet(t, sub)
    for t in turns:
        greet(t, up)
        greet(t, down)

    def greet_sub(k, _):
        greet(slab, lax.rem(sub + k, subs))
        return 0

    lax.fori_loop(2, subs - 1, greet_sub, 0)
    here_kz = slabs * sub + slab
    expected = 3 * slabs - 1 + subs - 3
    for kz in (here_kz, jnp.where(here_kz == 0, half, 2 * half - here_kz)):
        from_sub = lax.div(kz, depth)
        for t in range(slabs):
            other = jnp.logical_or(from_sub != sub, slab != t)

            @pl.when(other)
            def _():
                greet(t, from_sub)

    for i in range(depth):
        folded, _ = folded_of(depth * sub + i)
        mine = jnp.logical_and(lax.rem(folded, slabs) == slab, lax.div(folded, slabs) == sub)
        expected = expected + jnp.where(mine, 0, 1)
    moves = [
        pltpu.make_async_copy(r.influence.at[:, :, pl.ds(h * LANES, LANES)], r.raw.at[h], r.move.at[h])
        for h in range(G // LANES)
    ]
    loads = [
        pltpu.make_async_copy(getattr(r, name), getattr(r, "in_" + name), r.load.at[n])
        for n, name in enumerate(TWIDDLES)
    ]
    for move in [*moves, *loads]:
        move.start()
    pl.semaphore_wait(barrier, expected)

    def to_group(source, target, send_sem, recv_sem):
        goals = [(t, sub, slab) for t in turns[1:]] + [(t, up, slabs + slab) for t in turns]
        return [
            remote(source, target.at[slot], send_sem.at[n], recv_sem.at[slot], (to_slab, to_sub))
            for n, (to_slab, to_sub, slot) in enumerate(goals)
        ]

    def ghost_copies(it):
        goals = [(slab, up), (slab, down), (turns[1], sub), (turns[-1], sub)]
        ghosts = r.ghosts.shape[2]
        return [
            remote(
                r.ghosts.at[it, q],
                r.landing.at[it, pl.ds(q * ghosts, ghosts)],
                r.ghost_send.at[q],
                r.ghost_recv.at[it, q],
                goal,
            )
            for q, goal in enumerate(goals)
        ]

    def send_cells(it):
        own_cells(r.body, r.own_tiles)
        r.tables[: r.cells.shape[0]] = r.own_tiles[...]
        ghosts = r.ghosts.shape[2]
        for q in range(4):
            for slot in range(ghosts):
                r.ghosts[it, q, slot] = r.own_tiles[r.sends[0, q, slot]]
        for copy in ghost_copies(it):
            copy.start()

    def send_moments(it):
        for copy in to_group(r.own, r.mom.at[it], r.mom_send, r.mom_recv.at[it]):
            copy.start()
        r.mom[it, slab] = r.own[...]
        r.body[0:3] = r.own[0:3]
        send_cells(it)

    atoms = r.own.shape[1]
    r.own[0:3] = r.pol[...] * r.perm[...]
    r.own[3:4] = jnp.zeros((1, atoms), jnp.float32)
    r.body[3:6] = r.pos[...]
    r.body[6:8] = jnp.zeros((2, atoms), jnp.float32)
    r.still[slab, 0:3] = r.frac[...]
    r.still[slab, 3:6] = r.base[...].astype(jnp.float32)
    r.still[slab, 6:8] = jnp.zeros((2, atoms), jnp.float32)
    still_copies = to_group(r.still.at[slab], r.still, r.still_send, r.still_recv)
    for copy in still_copies:
        copy.start()
    send_moments(0)

    def plane(i):
        folded, slot = folded_of(depth * sub + i)
        to_slab, to_sub = lax.rem(folded, slabs), lax.div(folded, slabs)
        target = r.planes.at[slot, pl.ds(slab * rows, rows)]
        far = remote(
            r.moved.at[i], target, r.plane_send.at[i], r.plane_recv.at[slot, slab], (to_slab, to_sub)
        )
        return far, slot, jnp.logical_and(to_slab == slab, to_sub == sub)

    def here(i, slot):
        return pltpu.make_async_copy(
            r.moved.at[i], r.planes.at[slot, pl.ds(slab * rows, rows)], r.plane_recv.at[slot, slab]
        )

    for move in moves:
        move.wait()
    raw = r.raw.reshape(G // LANES * rows * depth, LANES)
    for i in range(depth):
        for h in range(G // LANES):
            r.moved[i, :, h * LANES : (h + 1) * LANES] = raw[pl.ds(h * rows * depth + i, rows, stride=depth), :]
        far, slot, mine = plane(i)

        @pl.when(mine)
        def _():
            here(i, slot).start()

        @pl.when(jnp.logical_not(mine))
        def _():
            far.start()

    first = r.moved[0]
    r.turned[...] = jnp.concatenate([first] * (LANES // rows), axis=0).T

    def hop(n):
        return remote(
            r.turned.at[pl.ds(turns[n] * group, group)],
            r.hop.at[slab],
            r.hop_send.at[n - 1],
            r.hop_recv.at[slab],
            (turns[n], sub),
        )

    def mid(n):
        to_sub = lax.rem(middle + n, subs)
        return remote(
            r.hop.at[:, pl.ds(lax.div(to_sub, 4) * 8, 8)],
            r.mids,
            r.mid_send.at[n - 1],
            r.mid_recv,
            (slab, to_sub),
        )

    @pl.when(sub == middle)
    def _():
        for n in range(1, slabs):
            hop(n).start()
        r.hop[slab] = r.turned[pl.ds(pl.multiple_of(slab * group, group), group)]

    near_columns(r.body[...], r.near)
    phase = (r.phase_t[slab], r.phase_l[slab])

    def tables(before):
        def one(n, _):
            block = lax.rem(slab + n, slabs)
            at = block + slabs if before else block

            @pl.when(jnp.logical_or(before, n > 0))
            def _():
                landed(r.still.at[at], r.still_recv.at[at])

            tables_of(slabs, subs, r.still, block, before, phase, r.plane_t, r.plane_l, r.zhat)
            return 0

        lax.fori_loop(0, slabs, one, 0)

    tables(False)

    @pl.when(sub == middle)
    def _():
        for t in turns[1:]:
            landed(r.hop.at[t], r.hop_recv.at[t])
        for n in range(1, subs):
            mid(n).start()
        r.mids[...] = r.hop[:, (middle // 4) * 8 : (middle // 4) * 8 + 8]

    tables(True)
    for load in loads:
        load.wait()

    def exchange(send, few, got, got_few, part, send_sem, recv_sem):
        first, count = part_rows(part, send.shape[1] // TILES)
        rows = pl.ds(first, count)

        def all_to_all(sources, targets, n):
            pltpu.make_async_copy(sources(sub), targets, recv_sem.at[n]).start()

            def one(k, _):
                to_sub = lax.rem(sub + k, subs)
                remote(sources(to_sub), targets, send_sem.at[n], recv_sem.at[n], (slab, to_sub)).start()
                return 0

            lax.fori_loop(1, subs, one, 0)

        if part == 1:
            all_to_all(lambda to: few.at[to], got_few.at[sub], 2)
        all_to_all(lambda to: send.at[to, rows], got.at[sub, rows], part)

    def exchanged(got, got_few, part, recv_sem):
        first, count = part_rows(part, got.shape[1] // TILES)
        landed(got.at[:, pl.ds(first, count)], recv_sem.at[part])
        if part == 1:
            landed(got_few, recv_sem.at[2])

    def iteration(it, _):
        density(
            slabs,
            subs,
            slab,
            r.mom.at[it],
            r.plane_t,
            r.plane_l,
            r.zhat,
            r.grid,
            lambda slot: landed(r.mom.at[it, slot], r.mom_recv.at[it, slot]),
        )
        got_a, got_b = r.got_a.at[it], r.got_b.at[it]
        few_a, few_b = r.got_few_a.at[it], r.got_few_b.at[it]
        first_frequency(
            slabs,
            subs,
            slab,
            r.grid,
            r.in_tx_t,
            r.in_tx_l,
            r.gather,
            r.send_a,
            r.few_a,
            r.edge,
            r.mid_rows,
            lambda part: exchange(r.send_a, r.few_a, got_a, few_a, part, r.a_send, r.a_recv.at[it]),
        )

        @pl.when(it == 0)
        def _():
            @pl.when(sub != middle)
            def _():
                landed(r.mids, r.mid_recv)

            for slot in range(2):
                for source in range(slabs):
                    landed(r.planes.at[slot, pl.ds(source * rows, rows)], r.plane_recv.at[slot, source])
            kernel_planes(slabs, subs, slab, sub, r.planes, r.mids, r.even, r.odd, r.mid_tile)

        cells, ghosts = r.cells.shape[0], r.ghosts.shape[2]
        for q in range(4):
            landed(r.landing.at[it, pl.ds(q * ghosts, ghosts)], r.ghost_recv.at[it, q])
        r.tables[cells:] = r.landing[it]
        cuts = [0, 3 * cells // 8, 5 * cells // 8, cells]

        def pairs(step):
            pair_field(cuts[step], cuts[step + 1], r.cells, r.counts, r.tables, r.near, r.pair)

        def sent_back(part):
            exchange(r.send_b, r.few_b, got_b, few_b, part, r.b_send, r.b_recv.at[it])
            pairs(1 + part)

        pairs(0)

        second(
            got_a,
            few_a,
            r.even,
            r.odd,
            r.mid_tile,
            r.in_ty_t,
            r.in_ty_l,
            r.in_by_t,
            r.in_by_l,
            r.send_b,
            r.few_b,
            lambda part: exchanged(got_a, few_a, part, r.a_recv.at[it]),
            sent_back,
        )
        for t in range(atoms // LANES):
            tile = r.pair[t * LANES : (t + 1) * LANES, :].T[:8]
            r.rest[:, t * LANES : (t + 1) * LANES] = tile
        r.rest[0:3] += r.perm[...]

        def share_copy(part, n):
            to_slab = lax.rem(slab + n, slabs)
            slot = part * slabs + slab
            return remote(
                r.share.at[part * slabs + to_slab],
                r.land.at[it, slot],
                r.share_send.at[part * (slabs - 1) + n - 1 + part],
                r.share_recv.at[it, slot],
                (to_slab, down if part else sub),
            )

        sample(
            slabs,
            subs,
            slab,
            got_b,
            few_b,
            r.plane_t,
            r.plane_l,
            r.zhat,
            r.in_bx_t,
            r.in_bx_l,
            r.bm_t.at[slab // 2],
            r.bm_l.at[slab // 2],
            r.expand,
            r.share,
            r.field,
            r.here,
            r.lhs,
            lambda part: exchanged(got_b, few_b, part, r.b_recv.at[it]),
            lambda part, n: share_copy(part, n).start(),
        )
        total = r.rest[0:3] + r.share[slab, 0:3]
        for slot in [*turns[1:], *(slabs + k for k in range(slabs))]:
            landed(r.land.at[it, slot], r.share_recv.at[it, slot])
            total = total + r.land[it, slot, 0:3]
        for copy in to_group(r.own, r.mom.at[it], r.mom_send, r.mom_recv.at[it]):
            copy.wait_send()
        for copy in ghost_copies(it):
            copy.wait_send()
        r.own[0:3] = r.pol[...] * total

        @pl.when(it + 1 < ITERS)
        def _():
            send_moments(it + 1)

        for n in range(1, slabs):
            share_copy(0, n).wait_send()
        for n in range(slabs):
            share_copy(1, n).wait_send()
        for part in range(2):
            rows_sent = pl.ds(*part_rows(part, r.send_a.shape[1] // TILES))
            landed(r.send_a.at[pl.ds(0, subs - 1), rows_sent], r.a_send.at[part])
            landed(r.send_b.at[pl.ds(0, subs - 1), rows_sent], r.b_send.at[part])
        landed(r.few_a.at[pl.ds(0, subs - 1)], r.a_send.at[2])
        landed(r.few_b.at[pl.ds(0, subs - 1)], r.b_send.at[2])
        return 0

    lax.fori_loop(0, ITERS, iteration, 0)
    r.out[...] = r.own[0:3]
    for copy in still_copies:
        copy.wait_send()

    @pl.when(sub == middle)
    def _():
        for n in range(1, slabs):
            hop(n).wait_send()
        for n in range(1, subs):
            mid(n).wait_send()

    for i in range(depth):
        far, slot, mine = plane(i)

        @pl.when(jnp.logical_not(mine))
        def _():
            far.wait_send()


def shards(
    positions,
    fraction,
    grid_base,
    polarizability,
    perm_field,
    influence,
    neighbour_cells,
    neighbour_count,
    send_cells,
):
    atoms = positions.shape[1]
    cells = neighbour_cells.shape[0]
    ghosts = send_cells.shape[2]
    slabs = lax.axis_size("slab")
    subs = lax.axis_size("sub")
    grid_x = G // slabs
    grid_y = G // subs
    depth = G // subs

    index = np.arange(G)
    angle = (index[:, None] * index[None, :] % G) * (2.0 * np.pi / G)
    kz_rows = np.arange(slabs)[:, None] + slabs * np.arange(subs)[None, :]
    turn = kz_rows[:, :, None] * index[None, None, :] % G * (2.0 * np.pi / G)
    ranks = 2 * subs + 8
    phase = np.zeros((slabs, ranks, G), np.float32)
    phase[:, :subs] = np.cos(turn)
    phase[:, subs : 2 * subs] = -np.sin(turn)
    phase[:, 2 * subs] = np.where(index % 2 == 0, 1.0, -1.0)
    cos_np, sin_np = np.cos(angle), np.sin(angle)
    halves = np.concatenate([index[:LANES], G + index[:LANES], index[LANES:], G + index[LANES:]])
    turn_x = parts_of(np.block([[cos_np, -sin_np], [sin_np, cos_np]])[:, halves])
    back_x = parts_of(np.block([[cos_np, sin_np], [-sin_np, cos_np]])[halves])
    turn_y = parts_of(np.concatenate([cos_np, sin_np], axis=1))
    back_y = parts_of(np.concatenate([cos_np, -sin_np], axis=1))
    wide = np.stack(
        [np.concatenate([cos_np[w : w + LANES], -sin_np[w : w + LANES]], axis=0) for w in range(0, G, LANES)]
    )
    phase, back_mid = parts_of(phase), parts_of(wide)
    select = np.zeros((4, LANES, LANES), np.float32)
    for q in range(4):
        for lane in range(LANES):
            select[q, lane, 2 + 2 * q + lane % 2] = 1.0
    gather = jnp.asarray(select.reshape(4 * LANES, LANES), jnp.bfloat16)
    expand = jnp.asarray(np.concatenate(list(select.transpose(0, 2, 1)), axis=1), jnp.bfloat16)

    operands = [
        neighbour_cells,
        neighbour_count,
        send_cells,
        polarizability[None, :],
        perm_field,
        positions,
        fraction,
        grid_base,
        *phase,
        *back_mid,
        gather,
        expand,
        influence,
        *turn_x,
        *back_x,
        *turn_y,
        *back_y,
    ]
    vmem = pl.BlockSpec(memory_space=pltpu.VMEM)
    smem = pl.BlockSpec(memory_space=pltpu.SMEM)
    far = len(TWIDDLES) + 1
    specs = [smem] * SMEM_INPUTS + [vmem] * (len(operands) - SMEM_INPUTS - far)
    specs += [pl.BlockSpec(memory_space=pl.ANY)] * far

    def held(*shape, dtype=jnp.float32):
        return pltpu.VMEM(shape, dtype)

    held16 = functools.partial(held, dtype=jnp.bfloat16)
    dma = pltpu.SemaphoreType.DMA
    chunk = (subs, TILES * grid_y, LANES)
    columns = 6 * subs + 16
    sends = 2 * slabs - 1
    planes = sum(plane_rows(slabs, subs))
    scratch = dict(
        mom=held(ITERS, 2 * slabs, 4, atoms),
        still=held(2 * slabs, 8, atoms),
        own=held(4, atoms),
        body=held(8, atoms),
        own_tiles=held(cells, 8, LANES),
        tables=held(cells + 4 * ghosts, 8, LANES),
        landing=held(ITERS, 4 * ghosts, 8, LANES),
        ghosts=held(ITERS, 4, ghosts, 8, LANES),
        near=held(atoms, LANES),
        pair=held(atoms, LANES),
        rest=held(8, atoms),
        plane_t=held16(slabs, planes, atoms),
        plane_l=held16(slabs, planes, atoms),
        zhat=held(2 * slabs, ranks, atoms),
        raw=held(G // LANES, grid_x, depth, LANES),
        moved=held(depth, grid_x, G),
        turned=held(G, LANES),
        hop=held(slabs, grid_x, LANES),
        planes=held(2, G, G),
        mids=held(slabs, 8, LANES),
        even=held(G, G),
        odd=held(G, G),
        mid_tile=held(G, LANES),
        grid=held(grid_y, G + 8, 256),
        mid_rows=held(4, grid_y, G),
        send_a=held(*chunk),
        got_a=held(ITERS, *chunk),
        few_a=held(subs, 1, LANES),
        got_few_a=held(ITERS, subs, 1, LANES),
        few_b=held(subs, 1, LANES),
        got_few_b=held(ITERS, subs, 1, LANES),
        edge=held(G, LANES),
        send_b=held(*chunk),
        got_b=held(ITERS, *chunk),
        field=held(6 * G * G // LANES, LANES),
        here=held(grid_y, columns, G),
        lhs=held16(slabs, 2 * columns, plane_rows(slabs, subs)[0]),
        share=held(2 * slabs, 4, atoms),
        land=held(ITERS, 2 * slabs, 4, atoms),
        **{
            "in_" + name: held16(*operand.shape)
            for name, operand in zip(TWIDDLES, operands[-len(TWIDDLES) :], strict=True)
        },
        load=dma((len(TWIDDLES),)),
        mom_send=dma((sends,)),
        mom_recv=dma((ITERS, 2 * slabs)),
        still_send=dma((sends,)),
        still_recv=dma((2 * slabs,)),
        ghost_send=dma((4,)),
        ghost_recv=dma((ITERS, 4)),
        move=dma((G // LANES,)),
        plane_send=dma((depth,)),
        plane_recv=dma((2, slabs)),
        hop_send=dma((slabs - 1,)),
        hop_recv=dma((slabs,)),
        mid_send=dma((subs - 1,)),
        mid_recv=dma,
        a_send=dma((3,)),
        a_recv=dma((ITERS, 3)),
        b_send=dma((3,)),
        b_recv=dma((ITERS, 3)),
        share_send=dma((sends,)),
        share_recv=dma((ITERS, 2 * slabs)),
    )
    names = [*INPUTS, "out", *scratch]
    return pl.pallas_call(
        functools.partial(whole_kernel, slabs, subs, names),
        out_shape=jax.ShapeDtypeStruct((3, atoms), jnp.float32),
        in_specs=specs,
        out_specs=vmem,
        scratch_shapes=list(scratch.values()),
        compiler_params=pltpu.CompilerParams(vmem_limit_bytes=60 << 20, collective_id=0, has_side_effects=True),
        name="dipoles",
    )(*operands)


def solution(mesh):
    in_specs = (
        P(None, ("slab", "sub")),
        P(None, ("slab", "sub")),
        P(None, ("slab", "sub")),
        P(("slab", "sub")),
        P(None, ("slab", "sub")),
        P("slab", "sub", None),
        P(("slab", "sub"), None),
        P(("slab", "sub")),
        P(("slab", "sub"), None, None),
    )
    out_specs = P(None, ("slab", "sub"))
    return jax.shard_map(shards, mesh=mesh, in_specs=in_specs, out_specs=out_specs, check_vma=False)
```
